512 devices in a mesh: ctx: 64 (over z, y), lat: 8 (over x, core).
Axes of the slice: x: 4, y: 4, z: 16, core: 2. Of those that a mesh axis runs over, the one named last changes fastest.
Arguments:
- token_ids: int32 [32768], P('ctx'), may hold values from 0 to 255
- embed_table: bfloat16 [256, 1024], replicated, may hold values from -6 to 6
- input_gain: float32 [1024], replicated, may hold values from 0.25 to 1.75
- cross_qkv: bfloat16 [3, 1024, 1024], P(None, 'ctx', 'lat'), may hold values from -8 to 8
- cross_out: bfloat16 [1024, 1024], P('ctx'), may hold values from -0.1875 to 0.1875
- layer_gain: float32 [2, 1024], replicated, may hold values from 0.25 to 1.75
- layer_qkv: bfloat16 [2, 3, 1024, 1024], P(None, None, 'ctx', 'lat'), may hold values from -8 to 8
- layer_out: bfloat16 [2, 1024, 1024], P(None, 'ctx'), may hold values from -0.1875 to 0.1875
Outputs:
- latent_state: float32 [1024, 1024], P('lat')
The draws below stay inside these ranges and needn't reach their ends.
All inputs are finite; a program needn't handle non-finite values.
Results may differ from the reference program's by a relative error of at most 0.0055.
Values may be sent and summed in bfloat16 or wider, within the bound.
No kernel may reach another device: no remote copies, remote signals or barrier semaphores. Data moves between devices by JAX's collectives and lax.ppermute only.
A program may use at most 128 MiB of HBM per device.

```python
import jax
import jax.numpy as jnp
from jax import lax

D = 1024
H = 16
VOCAB = 256
LAYERS = 2
HD = 64
N = 32768
L = 1024


def projections(key, count):
    first, second, third = jax.random.split(key, 3)
    shape = (count, D, D)
    keys_part = jax.random.normal(first, shape, jnp.float32) * D ** (-0.5)
    values_part = jax.random.normal(second, shape, jnp.float32) * D ** (-0.5)
    query_part = jax.random.normal(third, shape, jnp.float32) * D ** (-0.5)
    stacked = jnp.stack([query_part, keys_part, values_part], axis=1)
    return jnp.clip(stacked, -8.0, 8.0)


def draw_cross_qkv(key, part):
    key = jax.random.fold_in(key, 11)
    return projections(key, 1)[0].astype(jnp.bfloat16)


def draw_layer_qkv(key, part):
    key = jax.random.fold_in(key, 23)
    return projections(key, LAYERS).astype(jnp.bfloat16)


def touch_ends(drawn, rng, least, top_value):
    longest = drawn.shape.index(max(drawn.shape))
    spots = []
    for shift in (0, 1):
        where = [jax.random.randint(jax.random.fold_in(rng, axis), (), 0, length) for axis, length in enumerate(drawn.shape)]
        where[longest] = (where[longest] + shift) % drawn.shape[longest]
        spots.append(tuple(where))
    return drawn.at[spots[0]].set(least).at[spots[1]].set(top_value)


def block_levels(rng, dims, pieces, smallest, top_value):
    level = 1.0
    for position, blocks in pieces:
        heights = jax.random.uniform(jax.random.fold_in(jax.random.fold_in(rng, 6), position), (blocks,), jnp.float32, smallest / len(pieces), top_value / len(pieces))
        level = level * jnp.repeat(jnp.exp(heights), dims[position] // blocks).reshape((-1,) + (1,) * (len(dims) - 1 - position))
    return level


def noise(rng, dims, scale, most, cuts=(), kind=jnp.bfloat16):
    loudness = block_levels(rng, dims, cuts, -0.22, 0.18) if cuts else 1.0
    result = jax.random.normal(rng, dims, jnp.float32) * scale * loudness
    return jnp.minimum(jnp.maximum(result, -most), most).astype(kind)


def setup_inputs(seed: int = 0) -> dict:
    key_list = jax.random.split(jax.random.key(seed), 9)
    return {
        "token_ids": touch_ends(jax.random.randint(key_list[0], (N,), 0, VOCAB), jax.random.fold_in(key_list[0], 1), 0, VOCAB - 1).astype(jnp.int32),
        "embed_table": noise(key_list[1], (VOCAB, D), 1.0, 6.0),
        "input_gain": jnp.clip(1.0 + 0.15 * jax.random.normal(key_list[2], (D,), jnp.float32), 0.25, 1.75),
        "cross_qkv": draw_cross_qkv(jax.random.fold_in(key_list[8], 71), 0),
        "cross_out": noise(key_list[4], (D, D), D ** -0.5, 0.1875, ((0, 64),)),
        "layer_gain": jnp.clip(1.0 + 0.15 * jax.random.normal(key_list[5], (LAYERS, D), jnp.float32), 0.25, 1.75),
        "layer_qkv": draw_layer_qkv(jax.random.fold_in(key_list[8], 71), 0),
        "layer_out": noise(key_list[7], (LAYERS, D, D), D ** -0.5, 0.1875, ((1, 64),)),
    }


def rms_norm(values, gain):
    return values * lax.rsqrt(lax.optimization_barrier(jnp.mean(values * values, axis=-1, keepdims=True)) + 1e-06) * gain

def rotate(values3, positions):
    half_size = values3.shape[-1] // 2
    inverse = 10000.0 ** (-2.0 * jnp.arange(half_size, dtype=jnp.float32) / (2 * half_size))
    angle = positions.astype(jnp.float32)[:, None] * inverse[None, :]
    cosine = jnp.cos(angle)[:, None, :]
    sine = jnp.sin(angle)[:, None, :]
    first = values3[..., :half_size]
    second = values3[..., half_size:]
    return jnp.concatenate([first * cosine - second * sine, second * cosine + first * sine], axis=-1)

def reference(token_ids, embed_table, input_gain, cross_qkv, cross_out, layer_gain, layer_qkv, layer_out):
    score_scale = HD ** (-0.5)
    embedded = embed_table[token_ids].astype(jnp.float32)
    normed = rms_norm(embedded, input_gain).astype(jnp.bfloat16)
    qpos = N - L + jnp.arange(L, dtype=jnp.int32)
    kpos = jnp.arange(N, dtype=jnp.int32)
    key_float = jnp.dot(normed, cross_qkv[1], preferred_element_type=jnp.float32)
    keys = rotate(key_float.reshape(N, H, HD), kpos).reshape(N, D).astype(jnp.bfloat16)
    values = jnp.dot(normed, cross_qkv[2], preferred_element_type=jnp.float32).astype(jnp.bfloat16)
    query_float = jnp.dot(normed[N - L:], cross_qkv[0], preferred_element_type=jnp.float32)
    queries = rotate(query_float.reshape(L, H, HD), qpos).reshape(L, D).astype(jnp.bfloat16)
    allowed = kpos[None, :] <= qpos[:, None]

    def cross_head(index):
        start = index * HD
        qh = lax.dynamic_slice_in_dim(queries, start, HD, 1).astype(jnp.float32)
        kh = lax.dynamic_slice_in_dim(keys, start, HD, 1).astype(jnp.float32)
        vh = lax.dynamic_slice_in_dim(values, start, HD, 1).astype(jnp.float32)
        attention_scores = jnp.dot(qh, kh.T) * score_scale
        attention_scores = jnp.where(allowed, attention_scores, -1e+30)
        weights = jax.nn.softmax(attention_scores, axis=-1)
        weights = jnp.where(allowed, weights, 0.0)
        return jnp.dot(weights, vh)
    heads = lax.map(cross_head, jnp.arange(H))
    cross_heads = jnp.transpose(heads, (1, 0, 2)).reshape(L, D).astype(jnp.bfloat16)
    state = embedded[N - L:] + jnp.dot(cross_heads, cross_out, preferred_element_type=jnp.float32)
    causal = jnp.arange(L)[None, :] <= jnp.arange(L)[:, None]
    latent_pos = jnp.arange(L, dtype=jnp.int32)
    for layer in range(LAYERS):
        latent_normed = rms_norm(state, layer_gain[layer]).astype(jnp.bfloat16)
        proj = layer_qkv[layer]
        lq_float = jnp.dot(latent_normed, proj[0], preferred_element_type=jnp.float32)
        lk_float = jnp.dot(latent_normed, proj[1], preferred_element_type=jnp.float32)
        lq = rotate(lq_float.reshape(L, H, HD), latent_pos).reshape(L, D).astype(jnp.bfloat16)
        lk = rotate(lk_float.reshape(L, H, HD), latent_pos).reshape(L, D).astype(jnp.bfloat16)
        lv = jnp.dot(latent_normed, proj[2], preferred_element_type=jnp.float32).astype(jnp.bfloat16)
        query_tensor3 = lq.reshape(L, H, HD).astype(jnp.float32)
        key_tensor3 = lk.reshape(L, H, HD).astype(jnp.float32)
        value_tensor3 = lv.reshape(L, H, HD).astype(jnp.float32)
        attention_scores = jnp.einsum('gey,sey->egs', query_tensor3, key_tensor3) * score_scale
        attention_scores = jnp.where(causal[None], attention_scores, -1e+30)
        attention_probabilities = jax.nn.softmax(attention_scores, axis=-1).astype(jnp.bfloat16)
        attended_values = jnp.einsum('jvq,qjy->vjy', attention_probabilities.astype(jnp.float32), value_tensor3)
        layer_heads = attended_values.reshape(L, D).astype(jnp.bfloat16)
        state = state + jnp.dot(layer_heads, layer_out[layer], preferred_element_type=jnp.float32)
    return state
```

```python
import functools

import jax
import jax.numpy as jnp
import numpy as np
from jax import lax
from jax.experimental import pallas as pl
from jax.experimental.pallas import tpu as pltpu
from jax.sharding import Mesh
from jax.sharding import PartitionSpec as P

D = 1024
HD = 64
HALF = 32
NZ, NY, NX, NC = 16, 4, 4, 2
NLAT = NX * NC
N = 32768
L = 1024
VOCAB = 256
WIDTH = 128
OWN = 16
PART = 32
BLOCK = 256
KEYS = 2048
STEPS = N // KEYS
LAT = ("x", "c")
CTX = ("z", "y")
BF = jnp.bfloat16
F32 = jnp.float32
MIB = 1 << 20


def inverse_frequencies():
    return 10000.0 ** (-2.0 * jnp.arange(HALF, dtype=F32) / (2 * HALF))


def gather(x, axis, count):
    return lax.all_to_all(
        jnp.broadcast_to(x[None], (count, *x.shape)), axis, split_axis=0, concat_axis=0, tiled=True
    )


def dot(a, b):
    return jnp.dot(a, b, preferred_element_type=F32)


def dot_nt(a, b):
    return lax.dot_general(a, b, (((1,), (1,)), ((), ())), preferred_element_type=F32)


def split_two(x):
    high = x.astype(BF)
    return high, (x - high.astype(F32)).astype(BF)


def rotate_lanes(x, cosine, sine):
    lane = lax.broadcasted_iota(jnp.int32, x.shape, 1)
    other = jnp.where(lane % HD < HALF, pltpu.roll(x, WIDTH - HALF, 1), pltpu.roll(x, HALF, 1))
    return x * cosine + other * sine


def cross_kernel(
    w_ref, normed_ref, pick_ref, qcos_ref, qsin_ref, cosb_ref, sinb_ref, cosa_ref, sina_ref, qpos_ref,
    out_ref, w_sc, table_sc, tv_sc, q_sc, hot_sc, m_sc, acc_sc,
):
    step = pl.program_id(0)

    @pl.when(step == 0)
    def _():
        for z in range(NZ):
            for y in range(NY):
                row = (z * NY + y) * 16
                for part in range(3):
                    w_sc[row : row + 16, part * WIDTH : (part + 1) * WIDTH] = w_ref[
                        y, z, part * 16 : (part + 1) * 16, :
                    ]
        normed = normed_ref[...]
        kv = dot(normed, w_sc[:, WIDTH:])
        high, low = split_two(kv[:, :WIDTH].T)
        table_sc[:WIDTH] = high
        table_sc[WIDTH:] = low
        tv_sc[...] = kv[:, WIDTH:].astype(BF)
        rows = dot(pick_ref[...], normed).astype(BF)
        query = rotate_lanes(dot(rows, w_sc[:, :WIDTH]), qcos_ref[...], qsin_ref[...])
        query = query.astype(BF).astype(F32) * (HD**-0.5)
        lane = lax.broadcasted_iota(jnp.int32, query.shape, 1)
        q_sc[:OWN] = jnp.where(lane < HD, query, 0.0).astype(BF)
        q_sc[OWN:] = jnp.where(lane < HD, 0.0, query).astype(BF)
        m_sc[...] = jnp.full(m_sc.shape, -1e30, F32)
        acc_sc[...] = jnp.zeros(acc_sc.shape, F32)

    token = lax.broadcasted_iota(jnp.int32, (VOCAB, 128), 0).astype(F32)
    for y in range(NY):
        ids = w_ref[y, step, 48:64, :].astype(F32)
        for r in range(4):
            start = y * 512 + r * 128
            hot_sc[:, start : start + 128] = jnp.where(
                token == ids[r : r + 1, :], 1.0, 0.0
            ).astype(BF)
    hot = hot_sc[...]
    both = dot(table_sc[...], hot)
    key = both[:WIDTH] + both[WIDTH:]
    ca = cosa_ref[0][:, :1]
    sa = sina_ref[0][:, :1]
    cosine = cosb_ref[...] * ca - sinb_ref[...] * sa
    sine = sinb_ref[...] * ca + cosb_ref[...] * sa
    pieces = []
    for head in range(2):
        first = key[head * HD : head * HD + HALF]
        second = key[head * HD + HALF : (head + 1) * HD]
        pieces.append(first * cosine - second * sine)
        pieces.append(second * cosine + first * sine)
    rotated = jnp.concatenate(pieces, axis=0).astype(BF)
    scores = dot(q_sc[...], rotated)
    kpos = step * KEYS + lax.broadcasted_iota(jnp.int32, scores.shape, 1)
    scores = jnp.where(kpos <= qpos_ref[:, :1], scores, -1e30)
    before = m_sc[...]
    now = jnp.maximum(before, jnp.max(scores, axis=1, keepdims=True))
    weight = jnp.exp(scores - now[:, :1])
    scale = jnp.exp(before - now)
    acc_sc[...] = acc_sc[...] * scale[:, :1] + dot_nt(weight.astype(BF), hot)
    m_sc[...] = now

    @pl.when(step == STEPS - 1)
    def _():
        acc = acc_sc[...]
        share = acc / jnp.sum(acc, axis=1, keepdims=True)
        high, low = split_two(share)
        value = dot(high, tv_sc[...]) + dot(low, tv_sc[...])
        lane = lax.broadcasted_iota(jnp.int32, (OWN, WIDTH), 1)
        out_ref[...] = jnp.where(lane < HD, value[:OWN], value[OWN:]).astype(BF)


def cross_attention(weights, normed, pick, qcos, qsin, cosb, sinb, cosa, sina, qpos):
    whole = lambda a: pl.BlockSpec(a.shape, lambda s, n=a.ndim: (0,) * n)
    angle = pl.BlockSpec((1, HALF, 128), lambda s: (s, 0, 0))
    return pl.pallas_call(
        cross_kernel,
        grid=(STEPS,),
        in_specs=[whole(a) for a in (weights, normed, pick, qcos, qsin, cosb, sinb)]
        + [angle, angle, whole(qpos)],
        out_specs=pl.BlockSpec((OWN, WIDTH), lambda s: (0, 0)),
        out_shape=jax.ShapeDtypeStruct((OWN, WIDTH), BF),
        scratch_shapes=[
            pltpu.VMEM((D, 3 * WIDTH), BF),
            pltpu.VMEM((2 * WIDTH, VOCAB), BF),
            pltpu.VMEM((VOCAB, WIDTH), BF),
            pltpu.VMEM((2 * OWN, WIDTH), BF),
            pltpu.VMEM((VOCAB, KEYS), BF),
            pltpu.VMEM((2 * OWN, 1), F32),
            pltpu.VMEM((2 * OWN, VOCAB), F32),
        ],
        compiler_params=pltpu.CompilerParams(vmem_limit_bytes=40 * MIB),
        cost_estimate=pl.CostEstimate(
            flops=2 * N * VOCAB * 320, bytes_accessed=4 * MIB, transcendentals=N * 32
        ),
        name="cross_attention",
    )(weights, normed, pick, qcos, qsin, cosb, sinb, cosa, sina, qpos)


def dense_kernel(first, heads_ref, out_w_ref, state_ref, table_ref, gain_ref, qkv_ref, cos_ref, sin_ref, state_out, q_out, kv_out):
    if first:
        state = dot(state_ref[...], table_ref[...])
    else:
        state = state_ref[...]
    heads = jnp.concatenate([heads_ref[i] for i in range(NLAT)], axis=1)
    out_w = jnp.concatenate([out_w_ref[i] for i in range(NLAT)], axis=1)
    state = state + dot(heads, out_w)
    state_out[...] = state
    scale = lax.rsqrt(jnp.mean(state * state, axis=1, keepdims=True) + 1e-06)
    normed = (state * scale * gain_ref[...]).astype(BF)
    cosine, sine = cos_ref[...], sin_ref[...]
    q_out[...] = rotate_lanes(dot(normed, qkv_ref[0]), cosine, sine).astype(BF)
    kv_out[:, :WIDTH] = rotate_lanes(dot(normed, qkv_ref[1]), cosine, sine).astype(BF)
    kv_out[:, WIDTH:] = dot(normed, qkv_ref[2]).astype(BF)


def dense(first, heads, out_w, state, table, gain, qkv, cosine, sine):
    return pl.pallas_call(
        functools.partial(dense_kernel, first),
        out_shape=(
            jax.ShapeDtypeStruct((BLOCK, D), F32),
            jax.ShapeDtypeStruct((BLOCK, WIDTH), BF),
            jax.ShapeDtypeStruct((BLOCK, 2 * WIDTH), BF),
        ),
        compiler_params=pltpu.CompilerParams(vmem_limit_bytes=40 * MIB),
        cost_estimate=pl.CostEstimate(
            flops=2 * BLOCK * D * (D + 3 * WIDTH), bytes_accessed=8 * MIB, transcendentals=BLOCK
        ),
        name="dense",
    )(heads, out_w, state, table, gain, qkv, cosine, sine)


def key_positions():
    column = lax.broadcasted_iota(jnp.int32, (1, L), 1)
    return (column % BLOCK) // PART * 128 + column // BLOCK * PART + column % PART


def attend(q, k, v, qpos, kpos):
    outs = []
    seen = kpos <= qpos
    for head in range(2):
        lanes = slice(head * HD, (head + 1) * HD)
        scores = dot_nt(q[:, lanes], k[:, lanes]) * (HD**-0.5)
        scores = jnp.where(seen, scores, -1e30)
        weight = jnp.exp(scores - jnp.max(scores, axis=1, keepdims=True))
        total = jnp.sum(weight, axis=1, keepdims=True)
        outs.append(dot(weight.astype(BF), v[:, lanes]) / total)
    return jnp.concatenate(outs, axis=1).astype(BF)


def attend_block_kernel(q_ref, kv_ref, qpos_ref, out_ref):
    kv = jnp.concatenate([kv_ref[i] for i in range(NY)], axis=0)
    out_ref[...] = attend(
        q_ref[...], kv[:, :WIDTH], kv[:, WIDTH:], qpos_ref[:, :1], key_positions()
    )


def attend_block(q, kv, qpos):
    return pl.pallas_call(
        attend_block_kernel,
        out_shape=jax.ShapeDtypeStruct((BLOCK, WIDTH), BF),
        compiler_params=pltpu.CompilerParams(vmem_limit_bytes=32 * MIB),
        cost_estimate=pl.CostEstimate(
            flops=8 * BLOCK * L * HD, bytes_accessed=2 * MIB, transcendentals=2 * BLOCK * L
        ),
        name="attend_block",
    )(q, kv, qpos)


def attend_all_kernel(q_ref, kv_ref, out_ref):
    kv = jnp.concatenate([kv_ref[i] for i in range(NY)], axis=0)
    kpos = key_positions()
    row = lax.broadcasted_iota(jnp.int32, (BLOCK, 1), 0)
    for y in range(NY):
        qpos = row // PART * 128 + y * PART + row % PART
        part = attend(q_ref[y], kv[:, :WIDTH], kv[:, WIDTH:], qpos, kpos)
        for i in range(NLAT):
            out_ref[i, y * PART : (y + 1) * PART, :] = part[i * PART : (i + 1) * PART]


def attend_all(q, kv):
    return pl.pallas_call(
        attend_all_kernel,
        out_shape=jax.ShapeDtypeStruct((NLAT, 128, WIDTH), BF),
        compiler_params=pltpu.CompilerParams(vmem_limit_bytes=32 * MIB),
        cost_estimate=pl.CostEstimate(
            flops=8 * L * L * HD, bytes_accessed=2 * MIB, transcendentals=2 * L * L
        ),
        name="attend_all",
    )(q, kv)


def last_kernel(heads_ref, out_w_ref, state_ref, out_ref):
    heads = jnp.concatenate([heads_ref[i] for i in range(NLAT)], axis=1)
    out_w = jnp.concatenate([out_w_ref[i] for i in range(NLAT)], axis=1)
    state = jnp.concatenate([state_ref[i] for i in range(NY)], axis=0)
    out_ref[...] = state + dot(heads, out_w)


def last(heads, out_w, state):
    return pl.pallas_call(
        last_kernel,
        out_shape=jax.ShapeDtypeStruct((128, D), F32),
        compiler_params=pltpu.CompilerParams(vmem_limit_bytes=32 * MIB),
        cost_estimate=pl.CostEstimate(
            flops=2 * 128 * D * D, bytes_accessed=4 * MIB, transcendentals=0
        ),
        name="last",
    )(heads, out_w, state)


def head_angles(positions):
    angle = positions.astype(F32)[:, None] * inverse_frequencies()[None, :]
    cosine, sine = jnp.cos(angle), jnp.sin(angle)
    return (
        jnp.concatenate([cosine] * 4, axis=1),
        jnp.concatenate([-sine, sine, -sine, sine], axis=1),
    )


def body(token_ids, embed_table, input_gain, cross_qkv, cross_out, layer_gain, layer_qkv, layer_out):
    z, y = lax.axis_index("z"), lax.axis_index("y")
    lat = lax.axis_index(LAT)

    latent = jnp.arange(OWN, dtype=jnp.int32) + (z // 2) * 128 + y * PART + (z % 2) * OWN
    qcos, qsin = head_angles(N - L + latent)
    row = jnp.arange(BLOCK, dtype=jnp.int32)
    lpos = row // PART * 128 + y * PART + row % PART
    lcos, lsin = head_angles(lpos)
    inverse = inverse_frequencies()
    fine = inverse[:, None] * jnp.arange(KEYS, dtype=F32)[None, :]
    coarse = jnp.arange(STEPS, dtype=F32)[:, None] * KEYS * inverse[None, :]
    coarse = jnp.broadcast_to(coarse[:, :, None], (STEPS, HALF, 128))
    wide = embed_table.astype(F32)
    normed = wide * lax.rsqrt(jnp.mean(wide * wide, axis=-1, keepdims=True) + 1e-06) * input_gain
    normed = normed.astype(BF)

    ids = token_ids.astype(BF).reshape(4, 128)
    pack = jnp.concatenate([cross_qkv.reshape(48, WIDTH), ids, jnp.zeros((12, 128), BF)], axis=0)
    by_z = gather(pack, "z", NZ)
    by_zy = gather(by_z, "y", NY)

    own_out = lax.dynamic_slice_in_dim(
        jnp.concatenate([cross_out[None], layer_out], axis=0), lat * WIDTH, WIDTH, 2
    )
    rest = jnp.concatenate([layer_qkv.reshape(6, 16, WIDTH), own_out], axis=0)
    rest, by_z = lax.optimization_barrier((rest, by_z))
    rest = gather(rest, "z", NZ)
    rest, by_zy = lax.optimization_barrier((rest, by_zy))
    rest = gather(rest, "y", NY)
    rest = jnp.transpose(rest, (2, 1, 0, 3, 4)).reshape(9, D, WIDTH)
    qkv = rest[:6].reshape(2, 3, D, WIDTH)
    outs = [lax.all_gather(rest[6 + i], LAT, axis=0) for i in range(3)]

    latent_ids = by_zy[2:, NZ - 1, 48:52, :].reshape(L).astype(jnp.int32)
    own_ids = lax.dynamic_slice_in_dim(latent_ids, latent[0], OWN, 0)
    pick = (own_ids[:, None] == jnp.arange(VOCAB, dtype=jnp.int32)[None, :]).astype(BF)
    block_ids = lax.dynamic_slice_in_dim(latent_ids.reshape(8, NY, PART), y, 1, 1).reshape(BLOCK)
    block_pick = (block_ids[:, None] == jnp.arange(VOCAB, dtype=jnp.int32)[None, :]).astype(BF)
    qpos = jnp.broadcast_to(
        (N - L + jnp.concatenate([latent, latent]))[:, None], (2 * OWN, 128)
    )
    heads = cross_attention(
        by_zy, normed, pick, qcos, qsin, jnp.cos(fine), jnp.sin(fine), jnp.cos(coarse),
        jnp.sin(coarse), qpos,
    )

    heads = gather(heads, "z", NZ).reshape(BLOCK, WIDTH)
    heads = gather(heads, LAT, NLAT)
    state, q, kv = dense(
        True, heads, outs[0], block_pick, embed_table, layer_gain[0:1], qkv[0], lcos, lsin
    )
    kv = gather(kv, "y", NY)
    heads = attend_block(q, kv, jnp.broadcast_to(lpos[:, None], (BLOCK, 128)))
    heads = gather(heads, LAT, NLAT)
    state, q, kv = dense(
        False, heads, outs[1], state, embed_table, layer_gain[1:2], qkv[1], lcos, lsin
    )
    own_state = lax.dynamic_slice_in_dim(state, lat * PART, PART, 0)
    qkv_all = gather(jnp.concatenate([q, kv], axis=1), "y", NY)
    own_state = gather(own_state, "y", NY)
    heads = attend_all(qkv_all[:, :, :WIDTH], qkv_all[:, :, WIDTH:])
    heads = lax.all_to_all(heads, LAT, split_axis=0, concat_axis=0, tiled=True)
    return last(heads, outs[2], own_state)


def solution(mesh):
    grid = Mesh(np.asarray(mesh.devices).reshape(NZ, NY, NX, NC), ("z", "y", "x", "c"))
    return jax.shard_map(
        body,
        mesh=grid,
        in_specs=(
            P(CTX),
            P(),
            P(),
            P(None, CTX, LAT),
            P(CTX, None),
            P(),
            P(None, None, CTX, LAT),
            P(None, CTX, None),
        ),
        out_specs=P(LAT, None),
        check_vma=False,
    )
```

```python
import functools

import jax
import jax.numpy as jnp
import numpy as np
from jax import lax
from jax.experimental import pallas as pl
from jax.experimental.pallas import tpu as pltpu
from jax.sharding import Mesh
from jax.sharding import PartitionSpec as P

D = 1024
HD = 64
HALF = 32
NZ, NY, NX, NC = 16, 4, 4, 2
NLAT = NX * NC
N = 32768
L = 1024
VOCAB = 256
WIDTH = 128
OWN = 16
LAYERS = 2
PART = 32
BLOCK = 256
KEYS = 2048
STEPS = N // KEYS
LAT = ("x", "c")
CTX = ("z", "y")
BF = jnp.bfloat16
F32 = jnp.float32
MIB = 1 << 20


def inverse_frequencies():
    return 10000.0 ** (-2.0 * jnp.arange(HALF, dtype=F32) / (2 * HALF))


def gather(x, axis, count):
    return lax.all_to_all(
        jnp.broadcast_to(x[None], (count, *x.shape)), axis, split_axis=0, concat_axis=0, tiled=True
    )


def dot(a, b):
    return jnp.dot(a, b, preferred_element_type=F32)


def dot_nt(a, b):
    return lax.dot_general(a, b, (((1,), (1,)), ((), ())), preferred_element_type=F32)


def split_two(x):
    high = x.astype(BF)
    return high, (x - high.astype(F32)).astype(BF)


def rotate_lanes(x, cosine, sine):
    lane = lax.broadcasted_iota(jnp.int32, x.shape, 1)
    other = jnp.where(lane % HD < HALF, pltpu.roll(x, WIDTH - HALF, 1), pltpu.roll(x, HALF, 1))
    return x * cosine + other * sine


def cross_kernel(
    w_ref, normed_ref, pick_ref, qcos_ref, qsin_ref, cosb_ref, sinb_ref, cosa_ref, sina_ref, qpos_ref,
    out_ref, w_sc, table_sc, q_sc, s_sc, v_sc,
):
    for z in range(NZ):
        for y in range(NY):
            row = (z * NY + y) * 16
            for part in range(3):
                w_sc[row : row + 16, part * WIDTH : (part + 1) * WIDTH] = w_ref[
                    y, z, part * 16 : (part + 1) * 16, :
                ]
    normed = normed_ref[...]
    table_sc[...] = dot(normed, w_sc[:, WIDTH:]).T.astype(BF)
    rows = dot(pick_ref[...], normed).astype(BF)
    query = rotate_lanes(dot(rows, w_sc[:, :WIDTH]), qcos_ref[...], qsin_ref[...])
    query = query.astype(BF).astype(F32) * (HD**-0.5)
    lane = lax.broadcasted_iota(jnp.int32, query.shape, 1)
    q_sc[:OWN] = jnp.where(lane < HD, query, 0.0).astype(BF)
    q_sc[OWN:] = jnp.where(lane < HD, 0.0, query).astype(BF)
    token = lax.broadcasted_iota(jnp.int32, (VOCAB, 128), 0).astype(F32)

    def scores_of(step, top):
        hot = []
        for y in range(NY):
            ids = w_ref[y, step, 64:80, :].astype(F32)
            for r in range(4):
                hot.append(jnp.where(token == ids[r : r + 1, :], 1.0, 0.0).astype(BF))
        both = dot(table_sc[...], jnp.concatenate(hot, axis=1))
        v_sc[step] = both[WIDTH:].astype(BF)
        ca = cosa_ref[step][:, :1]
        sa = sina_ref[step][:, :1]
        cosine = cosb_ref[...] * ca - sinb_ref[...] * sa
        sine = sinb_ref[...] * ca + cosb_ref[...] * sa
        pieces = []
        for head in range(2):
            first = both[head * HD : head * HD + HALF]
            second = both[head * HD + HALF : (head + 1) * HD]
            pieces.append(first * cosine - second * sine)
            pieces.append(second * cosine + first * sine)
        scores = dot(q_sc[...], jnp.concatenate(pieces, axis=0).astype(BF))
        kpos = step * KEYS + lax.broadcasted_iota(jnp.int32, scores.shape, 1)
        scores = jnp.where(kpos <= qpos_ref[:, :1], scores, -1e30)
        s_sc[step] = scores
        for i in range(KEYS // 128):
            top = jnp.maximum(top, scores[:, i * 128 : (i + 1) * 128])
        return top

    top = lax.fori_loop(0, STEPS, scores_of, jnp.full((2 * OWN, 128), -1e30, F32), unroll=4)
    most = jnp.max(top, axis=1, keepdims=True)

    def values_of(step, carry):
        total, acc = carry
        weight = jnp.exp(s_sc[step] - most)
        for i in range(KEYS // 128):
            total = total + weight[:, i * 128 : (i + 1) * 128]
        return total, acc + dot_nt(v_sc[step], weight.astype(BF))

    total, acc = lax.fori_loop(
        0, STEPS, values_of, (jnp.zeros((2 * OWN, 128), F32), jnp.zeros((WIDTH, 2 * OWN), F32)),
        unroll=4,
    )
    value = acc.T / jnp.sum(total, axis=1, keepdims=True)
    lane = lax.broadcasted_iota(jnp.int32, (OWN, WIDTH), 1)
    value = jnp.where(lane < HD, value[:OWN], value[OWN:]).astype(BF)
    for z in range(NZ):
        out_ref[z] = value


def cross_attention(*operands):
    return pl.pallas_call(
        cross_kernel,
        out_shape=jax.ShapeDtypeStruct((NZ, OWN, WIDTH), BF),
        scratch_shapes=[
            pltpu.VMEM((D, 3 * WIDTH), BF),
            pltpu.VMEM((2 * WIDTH, VOCAB), BF),
            pltpu.VMEM((2 * OWN, WIDTH), BF),
            pltpu.VMEM((STEPS, 2 * OWN, KEYS), F32),
            pltpu.VMEM((STEPS, WIDTH, KEYS), BF),
        ],
        compiler_params=pltpu.CompilerParams(vmem_limit_bytes=32 * MIB),
        cost_estimate=pl.CostEstimate(
            flops=2 * N * VOCAB * 320, bytes_accessed=4 * MIB, transcendentals=N * 32
        ),
        name="cross_attention",
    )(*operands)


def dense_kernel(first, *refs):
    lat_ref, heads_ref, out_w_ref, state_ref, table_ref, gain_ref, qkv_ref, cos_ref, sin_ref = refs[:9]
    w_sc, state_sc, w_sem, state_sem = refs[-4:]
    copies = [
        pltpu.make_async_copy(out_w_ref.at[i], w_sc.at[i], w_sem.at[i]) for i in range(NLAT)
    ]
    for copy in copies:
        copy.start()
    if first:
        state_sc[...] = dot(state_ref[...], table_ref[...])
    else:
        fetch = pltpu.make_async_copy(state_ref, state_sc, state_sem)
        fetch.start()
    heads = jnp.concatenate([heads_ref[i] for i in range(NLAT)], axis=1)
    added = []
    for i in range(0, NLAT, 2):
        copies[i].wait()
        copies[i + 1].wait()
        added.append(dot(heads, jnp.concatenate([w_sc[i], w_sc[i + 1]], axis=1)))
    if not first:
        fetch.wait()
    state = state_sc[...] + jnp.concatenate(added, axis=1)
    state_sc[...] = state
    if first:
        state_out, q_out, pack_out = refs[9:12]
        store = pltpu.make_async_copy(state_sc, state_out, state_sem)
        store.start()
    scale = lax.rsqrt(jnp.mean(state * state, axis=1, keepdims=True) + 1e-06)
    normed = (state * scale * gain_ref[...]).astype(BF)
    cosine, sine = cos_ref[...], sin_ref[...]
    q = rotate_lanes(dot(normed, qkv_ref[0]), cosine, sine).astype(BF)
    k = rotate_lanes(dot(normed, qkv_ref[1]), cosine, sine).astype(BF)
    v = dot(normed, qkv_ref[2]).astype(BF)
    if first:
        q_out[...] = q
        for y in range(NY):
            pack_out[y, :, :WIDTH] = k
            pack_out[y, :, WIDTH:] = v
        store.wait()
    else:
        pack_out = refs[9]
        own = state_sc[pl.ds(pl.multiple_of(lat_ref[0] * PART, PART), PART), :].astype(BF)
        for y in range(NY):
            for i, part in enumerate((q, k, v)):
                pack_out[y, :, i * WIDTH : (i + 1) * WIDTH] = part
            for i in range(NLAT):
                pack_out[y, i * PART : (i + 1) * PART, 3 * WIDTH :] = own[
                    :, i * WIDTH : (i + 1) * WIDTH
                ]


def dense(first, *operands):
    smem, vmem, hbm = (pl.BlockSpec(memory_space=m) for m in (pltpu.SMEM, pltpu.VMEM, pltpu.HBM))
    if first:
        out_shape = (
            jax.ShapeDtypeStruct((BLOCK, D), F32),
            jax.ShapeDtypeStruct((BLOCK, WIDTH), BF),
            jax.ShapeDtypeStruct((NY, BLOCK, 2 * WIDTH), BF),
        )
    else:
        out_shape = jax.ShapeDtypeStruct((NY, BLOCK, 4 * WIDTH), BF)
    return pl.pallas_call(
        functools.partial(dense_kernel, first),
        out_shape=out_shape,
        in_specs=[smem, vmem, hbm, vmem if first else hbm, vmem, vmem, vmem, vmem, vmem],
        out_specs=(hbm, vmem, vmem) if first else vmem,
        scratch_shapes=[
            pltpu.VMEM((NLAT, D, WIDTH), BF),
            pltpu.VMEM((BLOCK, D), F32),
            pltpu.SemaphoreType.DMA((NLAT,)),
            pltpu.SemaphoreType.DMA,
        ],
        compiler_params=pltpu.CompilerParams(vmem_limit_bytes=24 * MIB),
        cost_estimate=pl.CostEstimate(
            flops=2 * BLOCK * D * (D + 3 * WIDTH), bytes_accessed=8 * MIB, transcendentals=BLOCK
        ),
        name="dense",
    )(*operands)


def key_positions():
    column = lax.broadcasted_iota(jnp.int32, (1, L), 1)
    return (column % BLOCK) // PART * 128 + column // BLOCK * PART + column % PART


def attend(q, k, v, qpos, kpos):
    outs = []
    seen = kpos <= qpos
    for head in range(2):
        lanes = slice(head * HD, (head + 1) * HD)
        scores = dot_nt(q[:, lanes], k[:, lanes]) * (HD**-0.5)
        scores = jnp.where(seen, scores, -1e30)
        weight = jnp.exp(scores - jnp.max(scores, axis=1, keepdims=True))
        total = jnp.sum(weight, axis=1, keepdims=True)
        outs.append(dot(weight.astype(BF), v[:, lanes]) / total)
    return jnp.concatenate(outs, axis=1).astype(BF)


def attend_block_kernel(q_ref, kv_ref, qpos_ref, out_ref):
    kv = jnp.concatenate([kv_ref[i] for i in range(NY)], axis=0)
    out = attend(q_ref[...], kv[:, :WIDTH], kv[:, WIDTH:], qpos_ref[:, :1], key_positions())
    for i in range(NLAT):
        out_ref[i] = out


def attend_block(q, kv, qpos):
    return pl.pallas_call(
        attend_block_kernel,
        out_shape=jax.ShapeDtypeStruct((NLAT, BLOCK, WIDTH), BF),
        compiler_params=pltpu.CompilerParams(vmem_limit_bytes=16 * MIB),
        cost_estimate=pl.CostEstimate(
            flops=8 * BLOCK * L * HD, bytes_accessed=2 * MIB, transcendentals=2 * BLOCK * L
        ),
        name="attend_block",
    )(q, kv, qpos)


def attend_all_kernel(pack_ref, out_ref, state_ref):
    k = jnp.concatenate([pack_ref[i, :, WIDTH : 2 * WIDTH] for i in range(NY)], axis=0)
    v = jnp.concatenate([pack_ref[i, :, 2 * WIDTH : 3 * WIDTH] for i in range(NY)], axis=0)
    kpos = key_positions()
    row = lax.broadcasted_iota(jnp.int32, (BLOCK, 1), 0)
    for y in range(NY):
        qpos = row // PART * 128 + y * PART + row % PART
        part = attend(pack_ref[y, :, :WIDTH], k, v, qpos, kpos)
        for i in range(NLAT):
            out_ref[i, y * PART : (y + 1) * PART, :] = part[i * PART : (i + 1) * PART]
            state_ref[y * PART : (y + 1) * PART, i * WIDTH : (i + 1) * WIDTH] = pack_ref[
                y, i * PART : (i + 1) * PART, 3 * WIDTH :
            ]


def attend_all(pack):
    return pl.pallas_call(
        attend_all_kernel,
        out_shape=(
            jax.ShapeDtypeStruct((NLAT, 128, WIDTH), BF),
            jax.ShapeDtypeStruct((128, D), BF),
        ),
        compiler_params=pltpu.CompilerParams(vmem_limit_bytes=24 * MIB),
        cost_estimate=pl.CostEstimate(
            flops=8 * L * L * HD, bytes_accessed=2 * MIB, transcendentals=2 * L * L
        ),
        name="attend_all",
    )(pack)


def last_kernel(heads_ref, out_w_ref, state_ref, out_ref):
    heads = jnp.concatenate([heads_ref[i] for i in range(NLAT)], axis=1)
    out_w = jnp.concatenate([out_w_ref[i] for i in range(NLAT)], axis=1)
    out_ref[...] = state_ref[...].astype(F32) + dot(heads, out_w)


def last(heads, out_w, state):
    return pl.pallas_call(
        last_kernel,
        out_shape=jax.ShapeDtypeStruct((128, D), F32),
        compiler_params=pltpu.CompilerParams(vmem_limit_bytes=16 * MIB),
        cost_estimate=pl.CostEstimate(
            flops=2 * 128 * D * D, bytes_accessed=4 * MIB, transcendentals=0
        ),
        name="last",
    )(heads, out_w, state)


def head_angles(positions):
    angle = positions.astype(F32)[:, None] * inverse_frequencies()[None, :]
    cosine, sine = jnp.cos(angle), jnp.sin(angle)
    return (
        jnp.concatenate([cosine] * 4, axis=1),
        jnp.concatenate([-sine, sine, -sine, sine], axis=1),
    )


def body(token_ids, embed_table, input_gain, cross_qkv, cross_out, layer_gain, layer_qkv, layer_out):
    z, y = lax.axis_index("z"), lax.axis_index("y")
    lat = lax.axis_index(LAT)

    latent = jnp.arange(OWN, dtype=jnp.int32) + (z // 2) * 128 + y * PART + (z % 2) * OWN
    qcos, qsin = head_angles(N - L + latent)
    row = jnp.arange(BLOCK, dtype=jnp.int32)
    lpos = row // PART * 128 + y * PART + row % PART
    lcos, lsin = head_angles(lpos)
    inverse = inverse_frequencies()
    fine = inverse[:, None] * jnp.arange(KEYS, dtype=F32)[None, :]
    coarse = jnp.arange(STEPS, dtype=F32)[:, None] * KEYS * inverse[None, :]
    coarse = jnp.broadcast_to(coarse[:, :, None], (STEPS, HALF, 128))
    wide = embed_table.astype(F32)
    normed = wide * lax.rsqrt(jnp.mean(wide * wide, axis=-1, keepdims=True) + 1e-06) * input_gain
    normed = normed.astype(BF)

    tables = (qcos, qsin, jnp.cos(fine), jnp.sin(fine), jnp.cos(coarse), jnp.sin(coarse))

    own_out = lax.dynamic_slice_in_dim(
        jnp.concatenate([cross_out[None], layer_out], axis=0), lat * WIDTH, WIDTH, 2
    )
    ids = token_ids.astype(BF).reshape(4, 128)
    pack = jnp.concatenate(
        [cross_qkv.reshape(48, WIDTH), own_out[0], ids, jnp.zeros((12, 128), BF)], axis=0
    )
    by_z = gather(pack, "z", NZ)
    rest = jnp.concatenate([layer_qkv, own_out[1:, None]], axis=1).reshape(128, WIDTH)
    rest_y = jnp.zeros((NY, 128, WIDTH), BF)
    for k in range(NY):
        piece = rest
        if k:
            piece = lax.ppermute(rest, "y", [(i, (i + k) % NY) for i in range(NY)])
        rest_y = lax.dynamic_update_slice_in_dim(rest_y, piece[None], (y - k) % NY, 0)
    by_z, rest_y = lax.optimization_barrier((by_z, rest_y))
    rest_zy = lax.all_gather(rest_y.reshape(NY * 128, WIDTH), "z", axis=0)
    by_z, normed, lcos, lsin, tables = lax.optimization_barrier((by_z, normed, lcos, lsin, tables))
    by_zy = gather(by_z, "y", NY)

    cross_w = jnp.transpose(by_zy[:, :, 48:64, :], (1, 0, 2, 3)).reshape(D, WIDTH)
    cross_w = lax.all_gather(cross_w, LAT, axis=0)
    latent_ids = by_zy[2:, NZ - 1, 64:68, :].reshape(L).astype(jnp.int32)
    own_ids = lax.dynamic_slice_in_dim(latent_ids, latent[0], OWN, 0)
    pick = (own_ids[:, None] == jnp.arange(VOCAB, dtype=jnp.int32)[None, :]).astype(BF)
    block_ids = lax.dynamic_slice_in_dim(latent_ids.reshape(8, NY, PART), y, 1, 1).reshape(BLOCK)
    block_pick = (block_ids[:, None] == jnp.arange(VOCAB, dtype=jnp.int32)[None, :]).astype(BF)
    qpos = jnp.broadcast_to(
        (N - L + jnp.concatenate([latent, latent]))[:, None], (2 * OWN, 128)
    )
    heads = cross_attention(by_zy, normed, pick, *tables, qpos)

    heads = lax.all_to_all(heads, "z", split_axis=0, concat_axis=0, tiled=True)
    heads, rest_zy = lax.optimization_barrier((heads, rest_zy))
    heads = gather(heads.reshape(BLOCK, WIDTH), LAT, NLAT)
    rest_zy = rest_zy.reshape(NZ, NY, 8, 16, WIDTH)
    late = jnp.transpose(rest_zy, (2, 0, 1, 3, 4)).reshape(LAYERS, 4, D, WIDTH)
    layer_w = lax.all_gather(late[:, 3], LAT, axis=1)

    lat_index = jnp.full((1,), lat, jnp.int32)
    state, q, kv = dense(
        True, lat_index, heads, cross_w, block_pick, embed_table, layer_gain[0:1], late[0, :3], lcos, lsin
    )
    kv = lax.all_to_all(kv, "y", split_axis=0, concat_axis=0, tiled=True)
    heads = attend_block(q, kv, jnp.broadcast_to(lpos[:, None], (BLOCK, 128)))
    heads = lax.all_to_all(heads, LAT, split_axis=0, concat_axis=0, tiled=True)
    pack = dense(
        False, lat_index, heads, layer_w[0], state, embed_table, layer_gain[1:2], late[1, :3], lcos, lsin
    )
    pack = lax.all_to_all(pack, "y", split_axis=0, concat_axis=0, tiled=True)
    pack, last_w = lax.optimization_barrier((pack, layer_w[1]))
    heads, state = attend_all(pack)
    heads = lax.all_to_all(heads, LAT, split_axis=0, concat_axis=0, tiled=True)
    return last(heads, last_w, state)


def solution(mesh):
    grid = Mesh(np.asarray(mesh.devices).reshape(NZ, NY, NX, NC), ("z", "y", "x", "c"))
    return jax.shard_map(
        body,
        mesh=grid,
        in_specs=(
            P(CTX),
            P(),
            P(),
            P(None, CTX, LAT),
            P(CTX, None),
            P(),
            P(None, None, CTX, LAT),
            P(None, CTX, None),
        ),
        out_specs=P(LAT, None),
        check_vma=False,
    )
```

```python
import functools

import jax
import jax.numpy as jnp
import numpy as np
from jax import lax
from jax.experimental import pallas as pl
from jax.experimental.pallas import tpu as pltpu
from jax.sharding import Mesh
from jax.sharding import PartitionSpec as P

D = 1024
HD = 64
HALF = 32
NZ, NY, NX, NC = 16, 4, 4, 2
NLAT = NX * NC
N = 32768
L = 1024
VOCAB = 256
WIDTH = 128
OWN = 16
LAYERS = 2
PART = 32
BLOCK = 256
KEYS = 2048
STEPS = N // KEYS
LAT = ("x", "c")
CTX = ("z", "y")
BF = jnp.bfloat16
F32 = jnp.float32
MIB = 1 << 20


def inverse_frequencies():
    return 10000.0 ** (-2.0 * jnp.arange(HALF, dtype=F32) / (2 * HALF))


def gather(x, axis, count):
    return lax.all_to_all(
        jnp.broadcast_to(x[None], (count, *x.shape)), axis, split_axis=0, concat_axis=0, tiled=True
    )


def dot(a, b):
    return jnp.dot(a, b, preferred_element_type=F32)


def dot_nt(a, b):
    return lax.dot_general(a, b, (((1,), (1,)), ((), ())), preferred_element_type=F32)


def split_two(x):
    high = x.astype(BF)
    return high, (x - high.astype(F32)).astype(BF)


def rotate_lanes(x, cosine, sine):
    lane = lax.broadcasted_iota(jnp.int32, x.shape, 1)
    other = jnp.where(lane % HD < HALF, pltpu.roll(x, WIDTH - HALF, 1), pltpu.roll(x, HALF, 1))
    return x * cosine + other * sine


def cross_kernel(
    w_ref, normed_ref, pick_ref, qcos_ref, qsin_ref, cosb_ref, sinb_ref, cosa_ref, sina_ref, qpos_ref,
    out_ref, w_sc, table_sc, q_sc, s_sc, v_sc,
):
    for z in range(NZ):
        for y in range(NY):
            row = (z * NY + y) * 16
            for part in range(3):
                w_sc[row : row + 16, part * WIDTH : (part + 1) * WIDTH] = w_ref[
                    y, z, part * 16 : (part + 1) * 16, :
                ]
    normed = normed_ref[...]
    table_sc[...] = dot(normed, w_sc[:, WIDTH:]).T.astype(BF)
    rows = dot(pick_ref[...], normed).astype(BF)
    query = rotate_lanes(dot(rows, w_sc[:, :WIDTH]), qcos_ref[...], qsin_ref[...])
    query = query.astype(BF).astype(F32) * (HD**-0.5)
    lane = lax.broadcasted_iota(jnp.int32, query.shape, 1)
    q_sc[:OWN] = jnp.where(lane < HD, query, 0.0).astype(BF)
    q_sc[OWN:] = jnp.where(lane < HD, 0.0, query).astype(BF)
    token = lax.broadcasted_iota(jnp.int32, (VOCAB, 128), 0).astype(F32)

    def scores_of(step, top):
        hot = []
        for y in range(NY):
            ids = w_ref[y, step, 48:64, :].astype(F32)
            for r in range(4):
                hot.append(jnp.where(token == ids[r : r + 1, :], 1.0, 0.0).astype(BF))
        both = dot(table_sc[...], jnp.concatenate(hot, axis=1))
        v_sc[step] = both[WIDTH:].astype(BF)
        ca = cosa_ref[step][:, :1]
        sa = sina_ref[step][:, :1]
        cosine = cosb_ref[...] * ca - sinb_ref[...] * sa
        sine = sinb_ref[...] * ca + cosb_ref[...] * sa
        pieces = []
        for head in range(2):
            first = both[head * HD : head * HD + HALF]
            second = both[head * HD + HALF : (head + 1) * HD]
            pieces.append(first * cosine - second * sine)
            pieces.append(second * cosine + first * sine)
        scores = dot(q_sc[...], jnp.concatenate(pieces, axis=0).astype(BF))
        kpos = step * KEYS + lax.broadcasted_iota(jnp.int32, scores.shape, 1)
        scores = jnp.where(kpos <= qpos_ref[:, :1], scores, -1e30)
        s_sc[step] = scores
        for i in range(KEYS // 128):
            top = jnp.maximum(top, scores[:, i * 128 : (i + 1) * 128])
        return top

    top = lax.fori_loop(0, STEPS, scores_of, jnp.full((2 * OWN, 128), -1e30, F32), unroll=4)
    most = jnp.max(top, axis=1, keepdims=True)

    def values_of(step, carry):
        total, acc = carry
        weight = jnp.exp(s_sc[step] - most)
        for i in range(KEYS // 128):
            total = total + weight[:, i * 128 : (i + 1) * 128]
        return total, acc + dot_nt(v_sc[step], weight.astype(BF))

    total, acc = lax.fori_loop(
        0, STEPS, values_of, (jnp.zeros((2 * OWN, 128), F32), jnp.zeros((WIDTH, 2 * OWN), F32)),
        unroll=4,
    )
    value = acc.T / jnp.sum(total, axis=1, keepdims=True)
    lane = lax.broadcasted_iota(jnp.int32, (OWN, WIDTH), 1)
    value = jnp.where(lane < HD, value[:OWN], value[OWN:]).astype(BF)
    for z in range(NZ):
        out_ref[z] = value


def cross_attention(*operands):
    return pl.pallas_call(
        cross_kernel,
        out_shape=jax.ShapeDtypeStruct((NZ, OWN, WIDTH), BF),
        scratch_shapes=[
            pltpu.VMEM((D, 3 * WIDTH), BF),
            pltpu.VMEM((2 * WIDTH, VOCAB), BF),
            pltpu.VMEM((2 * OWN, WIDTH), BF),
            pltpu.VMEM((STEPS, 2 * OWN, KEYS), F32),
            pltpu.VMEM((STEPS, WIDTH, KEYS), BF),
        ],
        compiler_params=pltpu.CompilerParams(vmem_limit_bytes=32 * MIB),
        cost_estimate=pl.CostEstimate(
            flops=2 * N * VOCAB * 320, bytes_accessed=4 * MIB, transcendentals=N * 32
        ),
        name="cross_attention",
    )(*operands)


def out_weights(ref):
    columns = []
    for i in range(NLAT):
        rows = [ref[i // 2, y, z, i % 2] for z in range(NZ) for y in range(NY)]
        columns.append(jnp.concatenate(rows, axis=0))
    return jnp.concatenate(columns, axis=1)


def dense_kernel(first, *refs):
    lat_ref, heads_ref, out_w_ref, state_ref, table_ref, gain_ref, qkv_ref, cos_ref, sin_ref = refs[:9]
    if first:
        state = dot(state_ref[...], table_ref[...])
    else:
        state = state_ref[...]
    heads = jnp.concatenate([heads_ref[i] for i in range(NLAT)], axis=1)
    state = state + dot(heads, out_weights(out_w_ref))
    scale = lax.rsqrt(jnp.mean(state * state, axis=1, keepdims=True) + 1e-06)
    normed = (state * scale * gain_ref[...]).astype(BF)
    cosine, sine = cos_ref[...], sin_ref[...]
    weights = [
        jnp.concatenate([qkv_ref[y, z, i] for z in range(NZ) for y in range(NY)], axis=0)
        for i in range(3)
    ]
    product = dot(normed, jnp.concatenate(weights, axis=1))
    q = rotate_lanes(product[:, :WIDTH], cosine, sine).astype(BF)
    k = rotate_lanes(product[:, WIDTH : 2 * WIDTH], cosine, sine).astype(BF)
    v = product[:, 2 * WIDTH :].astype(BF)
    if first:
        state_out, q_out, pack_out = refs[9:12]
        state_out[...] = state
        q_out[...] = q
        for y in range(NY):
            pack_out[y, :, :WIDTH] = k
            pack_out[y, :, WIDTH:] = v
    else:
        pack_out, state_sc = refs[9:11]
        state_sc[...] = state
        own = state_sc[pl.ds(pl.multiple_of(lat_ref[0] * PART, PART), PART), :].astype(BF)
        for y in range(NY):
            for i, part in enumerate((q, k, v)):
                pack_out[y, :, i * WIDTH : (i + 1) * WIDTH] = part
            for i in range(NLAT):
                pack_out[y, i * PART : (i + 1) * PART, 3 * WIDTH :] = own[
                    :, i * WIDTH : (i + 1) * WIDTH
                ]


def dense(first, *operands):
    smem, vmem = (pl.BlockSpec(memory_space=m) for m in (pltpu.SMEM, pltpu.VMEM))
    if first:
        out_shape = (
            jax.ShapeDtypeStruct((BLOCK, D), F32),
            jax.ShapeDtypeStruct((BLOCK, WIDTH), BF),
            jax.ShapeDtypeStruct((NY, BLOCK, 2 * WIDTH), BF),
        )
    else:
        out_shape = jax.ShapeDtypeStruct((NY, BLOCK, 4 * WIDTH), BF)
    return pl.pallas_call(
        functools.partial(dense_kernel, first),
        out_shape=out_shape,
        in_specs=[smem] + [vmem] * 8,
        scratch_shapes=[] if first else [pltpu.VMEM((BLOCK, D), F32)],
        compiler_params=pltpu.CompilerParams(vmem_limit_bytes=24 * MIB),
        cost_estimate=pl.CostEstimate(
            flops=2 * BLOCK * D * (D + 3 * WIDTH), bytes_accessed=8 * MIB, transcendentals=BLOCK
        ),
        name="dense",
    )(*operands)


def key_positions():
    column = lax.broadcasted_iota(jnp.int32, (1, L), 1)
    return (column % BLOCK) // PART * 128 + column // BLOCK * PART + column % PART


def attend(q, k, v, qpos, kpos):
    outs = []
    seen = kpos <= qpos
    for head in range(2):
        lanes = slice(head * HD, (head + 1) * HD)
        scores = dot_nt(q[:, lanes], k[:, lanes]) * (HD**-0.5)
        scores = jnp.where(seen, scores, -1e30)
        weight = jnp.exp(scores - jnp.max(scores, axis=1, keepdims=True))
        total = jnp.sum(weight, axis=1, keepdims=True)
        outs.append(dot(weight.astype(BF), v[:, lanes]) / total)
    return jnp.concatenate(outs, axis=1).astype(BF)


def attend_block_kernel(q_ref, kv_ref, qpos_ref, out_ref):
    kv = jnp.concatenate([kv_ref[i] for i in range(NY)], axis=0)
    out = attend(q_ref[...], kv[:, :WIDTH], kv[:, WIDTH:], qpos_ref[:, :1], key_positions())
    for i in range(NLAT):
        out_ref[i] = out


def attend_block(q, kv, qpos):
    return pl.pallas_call(
        attend_block_kernel,
        out_shape=jax.ShapeDtypeStruct((NLAT, BLOCK, WIDTH), BF),
        compiler_params=pltpu.CompilerParams(vmem_limit_bytes=16 * MIB),
        cost_estimate=pl.CostEstimate(
            flops=8 * BLOCK * L * HD, bytes_accessed=2 * MIB, transcendentals=2 * BLOCK * L
        ),
        name="attend_block",
    )(q, kv, qpos)


def attend_all_kernel(pack_ref, out_ref, state_ref):
    k = jnp.concatenate([pack_ref[i, :, WIDTH : 2 * WIDTH] for i in range(NY)], axis=0)
    v = jnp.concatenate([pack_ref[i, :, 2 * WIDTH : 3 * WIDTH] for i in range(NY)], axis=0)
    kpos = key_positions()
    row = lax.broadcasted_iota(jnp.int32, (BLOCK, 1), 0)
    for y in range(NY):
        qpos = row // PART * 128 + y * PART + row % PART
        part = attend(pack_ref[y, :, :WIDTH], k, v, qpos, kpos)
        for i in range(NLAT):
            out_ref[i, y * PART : (y + 1) * PART, :] = part[i * PART : (i + 1) * PART]
            state_ref[y * PART : (y + 1) * PART, i * WIDTH : (i + 1) * WIDTH] = pack_ref[
                y, i * PART : (i + 1) * PART, 3 * WIDTH :
            ]


def attend_all(pack):
    return pl.pallas_call(
        attend_all_kernel,
        out_shape=(
            jax.ShapeDtypeStruct((NLAT, 128, WIDTH), BF),
            jax.ShapeDtypeStruct((128, D), BF),
        ),
        compiler_params=pltpu.CompilerParams(vmem_limit_bytes=24 * MIB),
        cost_estimate=pl.CostEstimate(
            flops=8 * L * L * HD, bytes_accessed=2 * MIB, transcendentals=2 * L * L
        ),
        name="attend_all",
    )(pack)


def last_kernel(heads_ref, out_w_ref, state_ref, out_ref):
    heads = jnp.concatenate([heads_ref[i] for i in range(NLAT)], axis=1)
    out_ref[...] = state_ref[...].astype(F32) + dot(heads, out_weights(out_w_ref))


def last(heads, out_w, state):
    return pl.pallas_call(
        last_kernel,
        out_shape=jax.ShapeDtypeStruct((128, D), F32),
        compiler_params=pltpu.CompilerParams(vmem_limit_bytes=16 * MIB),
        cost_estimate=pl.CostEstimate(
            flops=2 * 128 * D * D, bytes_accessed=4 * MIB, transcendentals=0
        ),
        name="last",
    )(heads, out_w, state)


def head_angles(positions):
    angle = positions.astype(F32)[:, None] * inverse_frequencies()[None, :]
    cosine, sine = jnp.cos(angle), jnp.sin(angle)
    return (
        jnp.concatenate([cosine] * 4, axis=1),
        jnp.concatenate([-sine, sine, -sine, sine], axis=1),
    )


def body(token_ids, embed_table, input_gain, cross_qkv, cross_out, layer_gain, layer_qkv, layer_out):
    z, y = lax.axis_index("z"), lax.axis_index("y")
    lat = lax.axis_index(LAT)

    latent = jnp.arange(OWN, dtype=jnp.int32) + (z // 2) * 128 + y * PART + (z % 2) * OWN
    qcos, qsin = head_angles(N - L + latent)
    row = jnp.arange(BLOCK, dtype=jnp.int32)
    lpos = row // PART * 128 + y * PART + row % PART
    lcos, lsin = head_angles(lpos)
    inverse = inverse_frequencies()
    fine = inverse[:, None] * jnp.arange(KEYS, dtype=F32)[None, :]
    coarse = jnp.arange(STEPS, dtype=F32)[:, None] * KEYS * inverse[None, :]
    coarse = jnp.broadcast_to(coarse[:, :, None], (STEPS, HALF, 128))
    wide = embed_table.astype(F32)
    normed = wide * lax.rsqrt(jnp.mean(wide * wide, axis=-1, keepdims=True) + 1e-06) * input_gain
    normed = normed.astype(BF)

    tables = (qcos, qsin, jnp.cos(fine), jnp.sin(fine), jnp.cos(coarse), jnp.sin(coarse))

    slices = lax.dynamic_slice_in_dim(
        jnp.concatenate([cross_out[None], layer_out], axis=0), lax.axis_index("x") * 256, 256, 2
    )
    slices = jnp.transpose(slices.reshape(3, 16, 2, WIDTH), (0, 2, 1, 3)).reshape(96, WIDTH)
    rest = jnp.concatenate(
        [slices, layer_qkv.reshape(96, WIDTH), jnp.zeros((64, WIDTH), BF)], axis=0
    )
    rest_z = lax.all_gather(rest, "z", axis=0)

    ids = token_ids.astype(BF).reshape(4, 128)
    pack = jnp.concatenate(
        [cross_qkv.reshape(48, WIDTH), ids, jnp.zeros((12, 128), BF)], axis=0
    )
    by_z = gather(pack, "z", NZ)
    by_z, normed, lcos, lsin, tables = lax.optimization_barrier((by_z, normed, lcos, lsin, tables))
    by_zy = gather(by_z, "y", NY)
    by_zy, rest_z = lax.optimization_barrier((by_zy, rest_z))
    rest_zy = lax.all_gather(rest_z[:, :192], "y", axis=0).reshape(NY, NZ, 12, 16, WIDTH)

    latent_ids = by_zy[2:, NZ - 1, 48:52, :].reshape(L).astype(jnp.int32)
    own_ids = lax.dynamic_slice_in_dim(latent_ids, latent[0], OWN, 0)
    pick = (own_ids[:, None] == jnp.arange(VOCAB, dtype=jnp.int32)[None, :]).astype(BF)
    block_ids = lax.dynamic_slice_in_dim(latent_ids.reshape(8, NY, PART), y, 1, 1).reshape(BLOCK)
    block_pick = (block_ids[:, None] == jnp.arange(VOCAB, dtype=jnp.int32)[None, :]).astype(BF)
    qpos = jnp.broadcast_to(
        (N - L + jnp.concatenate([latent, latent]))[:, None], (2 * OWN, 128)
    )
    heads = cross_attention(by_zy, normed, pick, *tables, qpos)

    heads = lax.all_to_all(heads, "z", split_axis=0, concat_axis=0, tiled=True)
    heads, rest_zy = lax.optimization_barrier((heads, rest_zy))
    out_w = [lax.all_gather(rest_zy[:, :, 2 * i : 2 * i + 2], "x", axis=0) for i in range(3)]
    qkv = [rest_zy[:, :, 6 + 3 * i : 9 + 3 * i] for i in range(LAYERS)]
    heads = gather(heads.reshape(BLOCK, WIDTH), LAT, NLAT)

    lat_index = jnp.full((1,), lat, jnp.int32)
    state, q, kv = dense(
        True, lat_index, heads, out_w[0], block_pick, embed_table, layer_gain[0:1], qkv[0], lcos, lsin
    )
    kv = lax.all_to_all(kv, "y", split_axis=0, concat_axis=0, tiled=True)
    heads = attend_block(q, kv, jnp.broadcast_to(lpos[:, None], (BLOCK, 128)))
    heads = lax.all_to_all(heads, LAT, split_axis=0, concat_axis=0, tiled=True)
    pack = dense(
        False, lat_index, heads, out_w[1], state, embed_table, layer_gain[1:2], qkv[1], lcos, lsin
    )
    pack = lax.all_to_all(pack, "y", split_axis=0, concat_axis=0, tiled=True)
    pack, last_w = lax.optimization_barrier((pack, out_w[2]))
    heads, state = attend_all(pack)
    heads = lax.all_to_all(heads, LAT, split_axis=0, concat_axis=0, tiled=True)
    return last(heads, last_w, state)


def solution(mesh):
    grid = Mesh(np.asarray(mesh.devices).reshape(NZ, NY, NX, NC), ("z", "y", "x", "c"))
    return jax.shard_map(
        body,
        mesh=grid,
        in_specs=(
            P(CTX),
            P(),
            P(),
            P(None, CTX, LAT),
            P(CTX, None),
            P(),
            P(None, None, CTX, LAT),
            P(None, CTX, None),
        ),
        out_specs=P(LAT, None),
        check_vma=False,
    )
```

```python
import functools

import jax
import jax.numpy as jnp
import numpy as np
from jax import lax
from jax.experimental import pallas as pl
from jax.experimental.pallas import tpu as pltpu
from jax.sharding import Mesh
from jax.sharding import PartitionSpec as P

D = 1024
HD = 64
HALF = 32
NZ, NY, NX, NC = 16, 4, 4, 2
NLAT = NX * NC
N = 32768
L = 1024
VOCAB = 256
WIDTH = 128
OWN = 16
LAYERS = 2
PART = 32
BLOCK = 256
KEYS = 2048
STEPS = N // KEYS
LAT = ("x", "c")
CTX = ("z", "y")
BF = jnp.bfloat16
F32 = jnp.float32
MIB = 1 << 20


def inverse_frequencies():
    return 10000.0 ** (-2.0 * jnp.arange(HALF, dtype=F32) / (2 * HALF))


def gather(x, axis, count):
    return lax.all_to_all(
        jnp.broadcast_to(x[None], (count, *x.shape)), axis, split_axis=0, concat_axis=0, tiled=True
    )


def shifted_y(x):
    return [x] + [lax.ppermute(x, "y", [(i, (i + k) % NY) for i in range(NY)]) for k in range(1, NY)]


def stack_y(pieces, y):
    stacked = jnp.zeros((NY, *pieces[0].shape), pieces[0].dtype)
    for k, piece in enumerate(pieces):
        stacked = lax.dynamic_update_slice_in_dim(stacked, piece[None], (y - k) % NY, 0)
    return stacked


def dot(a, b):
    return jnp.dot(a, b, preferred_element_type=F32)


def dot_nt(a, b):
    return lax.dot_general(a, b, (((1,), (1,)), ((), ())), preferred_element_type=F32)


def split_two(x):
    high = x.astype(BF)
    return high, (x - high.astype(F32)).astype(BF)


def rotate_lanes(x, cosine, sine):
    lane = lax.broadcasted_iota(jnp.int32, x.shape, 1)
    other = jnp.where(lane % HD < HALF, pltpu.roll(x, WIDTH - HALF, 1), pltpu.roll(x, HALF, 1))
    return x * cosine + other * sine


def cross_kernel(
    w_ref, normed_ref, pick_ref, qcos_ref, qsin_ref, cosb_ref, sinb_ref, cosa_ref, sina_ref, qpos_ref,
    out_ref, w_sc, table_sc, q_sc, s_sc, v_sc,
):
    for z in range(NZ):
        for y in range(NY):
            row = (z * NY + y) * 16
            for part in range(3):
                w_sc[row : row + 16, part * WIDTH : (part + 1) * WIDTH] = w_ref[
                    y, z, part * 16 : (part + 1) * 16, :
                ]
    normed = normed_ref[...]
    table_sc[...] = dot(normed, w_sc[:, WIDTH:]).T.astype(BF)
    rows = dot(pick_ref[...], normed).astype(BF)
    query = rotate_lanes(dot(rows, w_sc[:, :WIDTH]), qcos_ref[...], qsin_ref[...])
    query = query.astype(BF).astype(F32) * (HD**-0.5)
    lane = lax.broadcasted_iota(jnp.int32, query.shape, 1)
    q_sc[:OWN] = jnp.where(lane < HD, query, 0.0).astype(BF)
    q_sc[OWN:] = jnp.where(lane < HD, 0.0, query).astype(BF)
    token = lax.broadcasted_iota(jnp.int32, (VOCAB, 128), 0).astype(F32)

    def scores_of(step, top):
        hot = []
        for y in range(NY):
            ids = w_ref[y, step, 64:80, :].astype(F32)
            for r in range(4):
                hot.append(jnp.where(token == ids[r : r + 1, :], 1.0, 0.0).astype(BF))
        both = dot(table_sc[...], jnp.concatenate(hot, axis=1))
        v_sc[step] = both[WIDTH:].astype(BF)
        ca = cosa_ref[step][:, :1]
        sa = sina_ref[step][:, :1]
        cosine = cosb_ref[...] * ca - sinb_ref[...] * sa
        sine = sinb_ref[...] * ca + cosb_ref[...] * sa
        pieces = []
        for head in range(2):
            first = both[head * HD : head * HD + HALF]
            second = both[head * HD + HALF : (head + 1) * HD]
            pieces.append(first * cosine - second * sine)
            pieces.append(second * cosine + first * sine)
        scores = dot(q_sc[...], jnp.concatenate(pieces, axis=0).astype(BF))
        kpos = step * KEYS + lax.broadcasted_iota(jnp.int32, scores.shape, 1)
        scores = jnp.where(kpos <= qpos_ref[:, :1], scores, -1e30)
        s_sc[step] = scores
        for i in range(KEYS // 128):
            top = jnp.maximum(top, scores[:, i * 128 : (i + 1) * 128])
        return top

    top = lax.fori_loop(0, STEPS, scores_of, jnp.full((2 * OWN, 128), -1e30, F32), unroll=4)
    most = jnp.max(top, axis=1, keepdims=True)

    def values_of(step, carry):
        total, acc = carry
        weight = jnp.exp(s_sc[step] - most)
        for i in range(KEYS // 128):
            total = total + weight[:, i * 128 : (i + 1) * 128]
        return total, acc + dot_nt(v_sc[step], weight.astype(BF))

    total, acc = lax.fori_loop(
        0, STEPS, values_of, (jnp.zeros((2 * OWN, 128), F32), jnp.zeros((WIDTH, 2 * OWN), F32)),
        unroll=4,
    )
    value = acc.T / jnp.sum(total, axis=1, keepdims=True)
    lane = lax.broadcasted_iota(jnp.int32, (OWN, WIDTH), 1)
    value = jnp.where(lane < HD, value[:OWN], value[OWN:]).astype(BF)
    for z in range(NZ):
        out_ref[z] = value


def cross_attention(*operands):
    return pl.pallas_call(
        cross_kernel,
        out_shape=jax.ShapeDtypeStruct((NZ, OWN, WIDTH), BF),
        scratch_shapes=[
            pltpu.VMEM((D, 3 * WIDTH), BF),
            pltpu.VMEM((2 * WIDTH, VOCAB), BF),
            pltpu.VMEM((2 * OWN, WIDTH), BF),
            pltpu.VMEM((STEPS, 2 * OWN, KEYS), F32),
            pltpu.VMEM((STEPS, WIDTH, KEYS), BF),
        ],
        compiler_params=pltpu.CompilerParams(vmem_limit_bytes=32 * MIB),
        cost_estimate=pl.CostEstimate(
            flops=MIB, bytes_accessed=MIB, transcendentals=0
        ),
        name="cross_attention",
    )(*operands)


def out_weights(ref):
    columns = []
    for i in range(NLAT):
        rows = [ref[i, y, z] for z in range(NZ) for y in range(NY)]
        columns.append(jnp.concatenate(rows, axis=0))
    return jnp.concatenate(columns, axis=1)


def dense_kernel(first, *refs):
    lat_ref, heads_ref, out_w_ref, state_ref, table_ref, gain_ref, qkv_ref, cos_ref, sin_ref = refs[:9]
    if first:
        state = dot(state_ref[...], table_ref[...])
    else:
        state = state_ref[...]
    heads = jnp.concatenate([heads_ref[i] for i in range(NLAT)], axis=1)
    state = state + dot(heads, out_weights(out_w_ref))
    scale = lax.rsqrt(jnp.mean(state * state, axis=1, keepdims=True) + 1e-06)
    normed = (state * scale * gain_ref[...]).astype(BF)
    cosine, sine = cos_ref[...], sin_ref[...]
    weights = [
        jnp.concatenate([qkv_ref[y, z, i] for z in range(NZ) for y in range(NY)], axis=0)
        for i in range(3)
    ]
    product = dot(normed, jnp.concatenate(weights, axis=1))
    q = rotate_lanes(product[:, :WIDTH], cosine, sine).astype(BF)
    k = rotate_lanes(product[:, WIDTH : 2 * WIDTH], cosine, sine).astype(BF)
    v = product[:, 2 * WIDTH :].astype(BF)
    if first:
        state_out, q_out, pack_out = refs[9:12]
        state_out[...] = state
        q_out[...] = q
        for y in range(NY):
            pack_out[y, :, :WIDTH] = k
            pack_out[y, :, WIDTH:] = v
    else:
        pack_out, state_sc = refs[9:11]
        state_sc[...] = state
        own = state_sc[pl.ds(pl.multiple_of(lat_ref[0] * PART, PART), PART), :].astype(BF)
        for y in range(NY):
            for i, part in enumerate((q, k, v)):
                pack_out[y, :, i * WIDTH : (i + 1) * WIDTH] = part
            for i in range(NLAT):
                pack_out[y, i * PART : (i + 1) * PART, 3 * WIDTH :] = own[
                    :, i * WIDTH : (i + 1) * WIDTH
                ]


def dense(first, *operands):
    smem, vmem = (pl.BlockSpec(memory_space=m) for m in (pltpu.SMEM, pltpu.VMEM))
    if first:
        out_shape = (
            jax.ShapeDtypeStruct((BLOCK, D), F32),
            jax.ShapeDtypeStruct((BLOCK, WIDTH), BF),
            jax.ShapeDtypeStruct((NY, BLOCK, 2 * WIDTH), BF),
        )
    else:
        out_shape = jax.ShapeDtypeStruct((NY, BLOCK, 4 * WIDTH), BF)
    return pl.pallas_call(
        functools.partial(dense_kernel, first),
        out_shape=out_shape,
        in_specs=[smem] + [vmem] * 8,
        scratch_shapes=[] if first else [pltpu.VMEM((BLOCK, D), F32)],
        compiler_params=pltpu.CompilerParams(vmem_limit_bytes=24 * MIB),
        cost_estimate=pl.CostEstimate(
            flops=2 * BLOCK * D * (D + 3 * WIDTH), bytes_accessed=8 * MIB, transcendentals=BLOCK
        ),
        name="dense",
    )(*operands)


def key_positions():
    column = lax.broadcasted_iota(jnp.int32, (1, L), 1)
    return (column % BLOCK) // PART * 128 + column // BLOCK * PART + column % PART


def attend(q, k, v, qpos, kpos):
    outs = []
    seen = kpos <= qpos
    for head in range(2):
        lanes = slice(head * HD, (head + 1) * HD)
        scores = dot_nt(q[:, lanes], k[:, lanes]) * (HD**-0.5)
        scores = jnp.where(seen, scores, -1e30)
        weight = jnp.exp(scores - jnp.max(scores, axis=1, keepdims=True))
        total = jnp.sum(weight, axis=1, keepdims=True)
        outs.append(dot(weight.astype(BF), v[:, lanes]) / total)
    return jnp.concatenate(outs, axis=1).astype(BF)


def attend_block_kernel(q_ref, kv_ref, qpos_ref, out_ref):
    kv = jnp.concatenate([kv_ref[i] for i in range(NY)], axis=0)
    out = attend(q_ref[...], kv[:, :WIDTH], kv[:, WIDTH:], qpos_ref[:, :1], key_positions())
    for i in range(NLAT):
        out_ref[i] = out


def attend_block(q, kv, qpos):
    return pl.pallas_call(
        attend_block_kernel,
        out_shape=jax.ShapeDtypeStruct((NLAT, BLOCK, WIDTH), BF),
        compiler_params=pltpu.CompilerParams(vmem_limit_bytes=16 * MIB),
        cost_estimate=pl.CostEstimate(
            flops=8 * BLOCK * L * HD, bytes_accessed=2 * MIB, transcendentals=2 * BLOCK * L
        ),
        name="attend_block",
    )(q, kv, qpos)


def attend_all_kernel(pack_ref, out_ref, state_ref):
    k = jnp.concatenate([pack_ref[i, :, WIDTH : 2 * WIDTH] for i in range(NY)], axis=0)
    v = jnp.concatenate([pack_ref[i, :, 2 * WIDTH : 3 * WIDTH] for i in range(NY)], axis=0)
    kpos = key_positions()
    row = lax.broadcasted_iota(jnp.int32, (BLOCK, 1), 0)
    for y in range(NY):
        qpos = row // PART * 128 + y * PART + row % PART
        part = attend(pack_ref[y, :, :WIDTH], k, v, qpos, kpos)
        for i in range(NLAT):
            out_ref[i, y * PART : (y + 1) * PART, :] = part[i * PART : (i + 1) * PART]
            state_ref[y * PART : (y + 1) * PART, i * WIDTH : (i + 1) * WIDTH] = pack_ref[
                y, i * PART : (i + 1) * PART, 3 * WIDTH :
            ]


def attend_all(pack):
    return pl.pallas_call(
        attend_all_kernel,
        out_shape=(
            jax.ShapeDtypeStruct((NLAT, 128, WIDTH), BF),
            jax.ShapeDtypeStruct((128, D), BF),
        ),
        compiler_params=pltpu.CompilerParams(vmem_limit_bytes=24 * MIB),
        cost_estimate=pl.CostEstimate(
            flops=8 * L * L * HD, bytes_accessed=2 * MIB, transcendentals=2 * L * L
        ),
        name="attend_all",
    )(pack)


def last_kernel(heads_ref, out_w_ref, state_ref, out_ref):
    heads = jnp.concatenate([heads_ref[i] for i in range(NLAT)], axis=1)
    out_ref[...] = state_ref[...].astype(F32) + dot(heads, out_weights(out_w_ref))


def last(heads, out_w, state):
    return pl.pallas_call(
        last_kernel,
        out_shape=jax.ShapeDtypeStruct((128, D), F32),
        compiler_params=pltpu.CompilerParams(vmem_limit_bytes=16 * MIB),
        cost_estimate=pl.CostEstimate(
            flops=2 * 128 * D * D, bytes_accessed=4 * MIB, transcendentals=0
        ),
        name="last",
    )(heads, out_w, state)


def head_angles(positions):
    angle = positions.astype(F32)[:, None] * inverse_frequencies()[None, :]
    cosine, sine = jnp.cos(angle), jnp.sin(angle)
    return (
        jnp.concatenate([cosine] * 4, axis=1),
        jnp.concatenate([-sine, sine, -sine, sine], axis=1),
    )


def body(token_ids, embed_table, input_gain, cross_qkv, cross_out, layer_gain, layer_qkv, layer_out):
    z, y = lax.axis_index("z"), lax.axis_index("y")
    lat = lax.axis_index(LAT)

    latent = jnp.arange(OWN, dtype=jnp.int32) + (z // 2) * 128 + y * PART + (z % 2) * OWN
    qcos, qsin = head_angles(N - L + latent)
    row = jnp.arange(BLOCK, dtype=jnp.int32)
    lpos = row // PART * 128 + y * PART + row % PART
    lcos, lsin = head_angles(lpos)
    inverse = inverse_frequencies()
    fine = inverse[:, None] * jnp.arange(KEYS, dtype=F32)[None, :]
    coarse = jnp.arange(STEPS, dtype=F32)[:, None] * KEYS * inverse[None, :]
    coarse = jnp.broadcast_to(coarse[:, :, None], (STEPS, HALF, 128))
    wide = embed_table.astype(F32)
    normed = wide * lax.rsqrt(jnp.mean(wide * wide, axis=-1, keepdims=True) + 1e-06) * input_gain
    normed = normed.astype(BF)

    tables = (qcos, qsin, jnp.cos(fine), jnp.sin(fine), jnp.cos(coarse), jnp.sin(coarse))

    own_out = lax.dynamic_slice_in_dim(
        jnp.concatenate([cross_out[None], layer_out], axis=0), lat * WIDTH, WIDTH, 2
    )
    rest = jnp.concatenate([layer_qkv, own_out[1:, None]], axis=1).reshape(128, WIDTH)
    ids = token_ids.astype(BF).reshape(4, 128)
    pack = jnp.concatenate(
        [cross_qkv.reshape(48, WIDTH), own_out[0], ids, jnp.zeros((12, 128), BF), rest], axis=0
    )
    by_z = gather(pack, "z", NZ)
    by_z, normed, lcos, lsin, tables = lax.optimization_barrier((by_z, normed, lcos, lsin, tables))
    by_z, rest_z = by_z[:, :80], by_z[:, 80:]
    by_zy = gather(by_z, "y", NY)
    cross_w = lax.all_gather(by_zy[:, :, 48:64, :], LAT, axis=0)

    latent_ids = by_zy[2:, NZ - 1, 64:68, :].reshape(L).astype(jnp.int32)
    own_ids = lax.dynamic_slice_in_dim(latent_ids, latent[0], OWN, 0)
    pick = (own_ids[:, None] == jnp.arange(VOCAB, dtype=jnp.int32)[None, :]).astype(BF)
    block_ids = lax.dynamic_slice_in_dim(latent_ids.reshape(8, NY, PART), y, 1, 1).reshape(BLOCK)
    block_pick = (block_ids[:, None] == jnp.arange(VOCAB, dtype=jnp.int32)[None, :]).astype(BF)
    qpos = jnp.broadcast_to(
        (N - L + jnp.concatenate([latent, latent]))[:, None], (2 * OWN, 128)
    )
    heads = cross_attention(by_zy, normed, pick, *tables, qpos)

    heads = lax.all_to_all(heads, "z", split_axis=0, concat_axis=0, tiled=True)
    heads, rest_y = lax.optimization_barrier((heads, shifted_y(rest_z)))
    rest_zy = stack_y(rest_y, y).reshape(NY, NZ, 8, 16, WIDTH)
    out_w = [lax.all_gather(rest_zy[:, :, 3 + 4 * i], LAT, axis=0) for i in range(LAYERS)]
    qkv = [rest_zy[:, :, 4 * i : 4 * i + 3] for i in range(LAYERS)]
    heads = gather(heads.reshape(BLOCK, WIDTH), LAT, NLAT)

    lat_index = jnp.full((1,), lat, jnp.int32)
    state, q, kv = dense(
        True, lat_index, heads, cross_w, block_pick, embed_table, layer_gain[0:1], qkv[0], lcos, lsin
    )
    kv = lax.all_to_all(kv, "y", split_axis=0, concat_axis=0, tiled=True)
    heads = attend_block(q, kv, jnp.broadcast_to(lpos[:, None], (BLOCK, 128)))
    heads = lax.all_to_all(heads, LAT, split_axis=0, concat_axis=0, tiled=True)
    pack = dense(
        False, lat_index, heads, out_w[0], state, embed_table, layer_gain[1:2], qkv[1], lcos, lsin
    )
    pack = lax.all_to_all(pack, "y", split_axis=0, concat_axis=0, tiled=True)
    pack, last_w = lax.optimization_barrier((pack, out_w[1]))
    heads, state = attend_all(pack)
    heads = lax.all_to_all(heads, LAT, split_axis=0, concat_axis=0, tiled=True)
    return last(heads, last_w, state)


def solution(mesh):
    grid = Mesh(np.asarray(mesh.devices).reshape(NZ, NY, NX, NC), ("z", "y", "x", "c"))
    return jax.shard_map(
        body,
        mesh=grid,
        in_specs=(
            P(CTX),
            P(),
            P(),
            P(None, CTX, LAT),
            P(CTX, None),
            P(),
            P(None, None, CTX, LAT),
            P(None, CTX, None),
        ),
        out_specs=P(LAT, None),
        check_vma=False,
    )
```

```python
import functools

import jax
import jax.numpy as jnp
import numpy as np
from jax import lax
from jax.experimental import pallas as pl
from jax.experimental.pallas import tpu as pltpu
from jax.sharding import Mesh
from jax.sharding import PartitionSpec as P

D = 1024
HD = 64
HALF = 32
NZ, NY, NX, NC = 16, 4, 4, 2
NLAT = NX * NC
N = 32768
L = 1024
VOCAB = 256
WIDTH = 128
OWN = 16
LAYERS = 2
PART = 32
BLOCK = 256
KEYS = 2048
STEPS = N // KEYS
LAT = ("x", "c")
CTX = ("z", "y")
BF = jnp.bfloat16
F32 = jnp.float32
MIB = 1 << 20


def inverse_frequencies():
    return 10000.0 ** (-2.0 * jnp.arange(HALF, dtype=F32) / (2 * HALF))


def gather(x, axis, count):
    return lax.all_to_all(
        jnp.broadcast_to(x[None], (count, *x.shape)), axis, split_axis=0, concat_axis=0, tiled=True
    )


def gather_lat(copies):
    by_x = lax.all_to_all(copies, "x", split_axis=0, concat_axis=0, tiled=True)
    return lax.all_gather(by_x, "c", axis=0)


def pack_kernel(lat_ref, ids_ref, cross_ref, layer_ref, cross_out_ref, layer_out_ref, out_ref):
    own = pl.ds(pl.multiple_of(lat_ref[0] * WIDTH, WIDTH), WIDTH)
    out_ref[0:48] = cross_ref[...]
    out_ref[48:64] = cross_out_ref[:, own]
    ids = ids_ref[...].astype(F32)
    out_ref[64:80] = jnp.concatenate([ids, jnp.zeros((12, WIDTH), F32)], axis=0).astype(BF)
    for layer in range(LAYERS):
        start = 80 + layer * 64
        out_ref[start : start + 48] = layer_ref[layer * 48 : (layer + 1) * 48]
        out_ref[start + 48 : start + 64] = layer_out_ref[layer * 16 : (layer + 1) * 16, own]


def pack_shards(*operands):
    smem, vmem = (pl.BlockSpec(memory_space=m) for m in (pltpu.SMEM, pltpu.VMEM))
    return pl.pallas_call(
        pack_kernel,
        out_shape=jax.ShapeDtypeStruct((208, WIDTH), BF),
        in_specs=[smem] + [vmem] * 5,
        compiler_params=pltpu.CompilerParams(vmem_limit_bytes=8 * MIB),
        name="pack_shards",
    )(*operands)


def dot(a, b):
    return jnp.dot(a, b, preferred_element_type=F32)


def dot_nt(a, b):
    return lax.dot_general(a, b, (((1,), (1,)), ((), ())), preferred_element_type=F32)


def split_two(x):
    high = x.astype(BF)
    return high, (x - high.astype(F32)).astype(BF)


def rotate_lanes(x, cosine, sine):
    lane = lax.broadcasted_iota(jnp.int32, x.shape, 1)
    other = jnp.where(lane % HD < HALF, pltpu.roll(x, WIDTH - HALF, 1), pltpu.roll(x, HALF, 1))
    return x * cosine + other * sine


def cross_kernel(
    w_ref, normed_ref, pick_ref, qcos_ref, qsin_ref, cosb_ref, sinb_ref, cosa_ref, sina_ref, qpos_ref,
    out_ref, w_sc, table_sc, q_sc, s_sc, v_sc,
):
    for z in range(NZ):
        for y in range(NY):
            row = (z * NY + y) * 16
            for part in range(3):
                w_sc[row : row + 16, part * WIDTH : (part + 1) * WIDTH] = w_ref[
                    y, z, part * 16 : (part + 1) * 16, :
                ]
    normed = normed_ref[...]
    table_sc[...] = dot(normed, w_sc[:, WIDTH:]).T.astype(BF)
    rows = dot(pick_ref[...], normed).astype(BF)
    query = rotate_lanes(dot(rows, w_sc[:, :WIDTH]), qcos_ref[...], qsin_ref[...])
    query = query.astype(BF).astype(F32) * (HD**-0.5)
    lane = lax.broadcasted_iota(jnp.int32, query.shape, 1)
    q_sc[:OWN] = jnp.where(lane < HD, query, 0.0).astype(BF)
    q_sc[OWN:] = jnp.where(lane < HD, 0.0, query).astype(BF)
    token = lax.broadcasted_iota(jnp.int32, (VOCAB, 128), 0).astype(F32)

    def scores_of(step, top):
        hot = []
        for y in range(NY):
            ids = w_ref[y, step, 64:80, :].astype(F32)
            for r in range(4):
                hot.append(jnp.where(token == ids[r : r + 1, :], 1.0, 0.0).astype(BF))
        both = dot(table_sc[...], jnp.concatenate(hot, axis=1))
        v_sc[step] = both[WIDTH:].astype(BF)
        ca = cosa_ref[step][:, :1]
        sa = sina_ref[step][:, :1]
        cosine = cosb_ref[...] * ca - sinb_ref[...] * sa
        sine = sinb_ref[...] * ca + cosb_ref[...] * sa
        pieces = []
        for head in range(2):
            first = both[head * HD : head * HD + HALF]
            second = both[head * HD + HALF : (head + 1) * HD]
            pieces.append(first * cosine - second * sine)
            pieces.append(second * cosine + first * sine)
        scores = dot(q_sc[...], jnp.concatenate(pieces, axis=0).astype(BF))
        kpos = step * KEYS + lax.broadcasted_iota(jnp.int32, scores.shape, 1)
        scores = jnp.where(kpos <= qpos_ref[:, :1], scores, -1e30)
        s_sc[step] = scores
        for i in range(KEYS // 128):
            top = jnp.maximum(top, scores[:, i * 128 : (i + 1) * 128])
        return top

    top = lax.fori_loop(0, STEPS, scores_of, jnp.full((2 * OWN, 128), -1e30, F32), unroll=4)
    most = jnp.max(top, axis=1, keepdims=True)

    def values_of(step, carry):
        total, acc = carry
        weight = jnp.exp(s_sc[step] - most)
        for i in range(KEYS // 128):
            total = total + weight[:, i * 128 : (i + 1) * 128]
        return total, acc + dot_nt(v_sc[step], weight.astype(BF))

    total, acc = lax.fori_loop(
        0, STEPS, values_of, (jnp.zeros((2 * OWN, 128), F32), jnp.zeros((WIDTH, 2 * OWN), F32)),
        unroll=4,
    )
    value = acc.T / jnp.sum(total, axis=1, keepdims=True)
    lane = lax.broadcasted_iota(jnp.int32, (OWN, WIDTH), 1)
    value = jnp.where(lane < HD, value[:OWN], value[OWN:]).astype(BF)
    for z in range(NZ):
        out_ref[z] = value


def cross_attention(*operands):
    return pl.pallas_call(
        cross_kernel,
        out_shape=jax.ShapeDtypeStruct((NZ, OWN, WIDTH), BF),
        scratch_shapes=[
            pltpu.VMEM((D, 3 * WIDTH), BF),
            pltpu.VMEM((2 * WIDTH, VOCAB), BF),
            pltpu.VMEM((2 * OWN, WIDTH), BF),
            pltpu.VMEM((STEPS, 2 * OWN, KEYS), F32),
            pltpu.VMEM((STEPS, WIDTH, KEYS), BF),
        ],
        compiler_params=pltpu.CompilerParams(vmem_limit_bytes=32 * MIB),
        cost_estimate=pl.CostEstimate(
            flops=MIB, bytes_accessed=MIB, transcendentals=0
        ),
        name="cross_attention",
    )(*operands)


def out_weights(ref):
    columns = []
    for i in range(NLAT):
        rows = [ref[i, y, z] for z in range(NZ) for y in range(NY)]
        columns.append(jnp.concatenate(rows, axis=0))
    return jnp.concatenate(columns, axis=1)


def dense_kernel(first, *refs):
    lat_ref, heads_ref, out_w_ref, state_ref, table_ref, gain_ref, qkv_ref, cos_ref, sin_ref = refs[:9]
    state_out, q_out, kv_out = refs[9:12]
    if first:
        state = dot(state_ref[...], table_ref[...])
    else:
        state = state_ref[...]
    heads = jnp.concatenate([heads_ref[i % NC, i // NC] for i in range(NLAT)], axis=1)
    state = state + dot(heads, out_weights(out_w_ref))
    if first:
        state_out[...] = state
    else:
        state_sc = refs[12]
        state_sc[...] = state
        own = pl.ds(pl.multiple_of(lat_ref[0] * WIDTH, WIDTH), WIDTH)
        state_out[...] = state_sc[:, own].astype(BF)
    scale = lax.rsqrt(jnp.mean(state * state, axis=1, keepdims=True) + 1e-06)
    normed = (state * scale * gain_ref[...]).astype(BF)
    cosine, sine = cos_ref[...], sin_ref[...]
    weights = [
        jnp.concatenate(
            [qkv_ref[y, z, i * 16 : (i + 1) * 16] for z in range(NZ) for y in range(NY)], axis=0
        )
        for i in range(3)
    ]
    product = dot(normed, jnp.concatenate(weights, axis=1))
    q_out[...] = rotate_lanes(product[:, :WIDTH], cosine, sine).astype(BF)
    k = rotate_lanes(product[:, WIDTH : 2 * WIDTH], cosine, sine).astype(BF)
    v = product[:, 2 * WIDTH :].astype(BF)
    for y in range(NY):
        kv_out[y, :, :WIDTH] = k
        kv_out[y, :, WIDTH:] = v


def dense(first, *operands):
    smem, vmem = (pl.BlockSpec(memory_space=m) for m in (pltpu.SMEM, pltpu.VMEM))
    return pl.pallas_call(
        functools.partial(dense_kernel, first),
        out_shape=(
            jax.ShapeDtypeStruct((BLOCK, D), F32)
            if first
            else jax.ShapeDtypeStruct((BLOCK, WIDTH), BF),
            jax.ShapeDtypeStruct((BLOCK, WIDTH), BF),
            jax.ShapeDtypeStruct((NY, BLOCK, 2 * WIDTH), BF),
        ),
        in_specs=[smem] + [vmem] * 8,
        scratch_shapes=[] if first else [pltpu.VMEM((BLOCK, D), F32)],
        compiler_params=pltpu.CompilerParams(vmem_limit_bytes=24 * MIB),
        cost_estimate=pl.CostEstimate(
            flops=2 * BLOCK * D * (D + 3 * WIDTH), bytes_accessed=8 * MIB, transcendentals=BLOCK
        ),
        name="dense",
    )(*operands)


def key_positions():
    column = lax.broadcasted_iota(jnp.int32, (1, L), 1)
    return (column % BLOCK) // PART * 128 + column // BLOCK * PART + column % PART


def attend(q, k, v, qpos, kpos):
    outs = []
    seen = kpos <= qpos
    for head in range(2):
        lanes = slice(head * HD, (head + 1) * HD)
        scores = dot_nt(q[:, lanes], k[:, lanes]) * (HD**-0.5)
        scores = jnp.where(seen, scores, -1e30)
        weight = jnp.exp(scores - jnp.max(scores, axis=1, keepdims=True))
        total = jnp.sum(weight, axis=1, keepdims=True)
        outs.append(dot(weight.astype(BF), v[:, lanes]) / total)
    return jnp.concatenate(outs, axis=1).astype(BF)


def attend_kernel(final, q_ref, kv_ref, qpos_ref, *refs):
    out_ref = refs[-1]
    kv = jnp.concatenate([kv_ref[i] for i in range(NY)], axis=0)
    out = attend(q_ref[...], kv[:, :WIDTH], kv[:, WIDTH:], qpos_ref[:, :1], key_positions())
    if final:
        state = refs[0][...]
        for y in range(NY):
            for i in range(NLAT):
                out_ref[y * NLAT + i, :PART] = out[i * PART : (i + 1) * PART]
                out_ref[y * NLAT + i, PART:] = state[i * PART : (i + 1) * PART]
    else:
        for i in range(NX):
            out_ref[i] = out


def attend_latents(final, *operands):
    shape = (NY * NLAT, 2 * PART, WIDTH) if final else (NX, BLOCK, WIDTH)
    return pl.pallas_call(
        functools.partial(attend_kernel, final),
        out_shape=jax.ShapeDtypeStruct(shape, BF),
        compiler_params=pltpu.CompilerParams(vmem_limit_bytes=16 * MIB),
        cost_estimate=pl.CostEstimate(
            flops=8 * BLOCK * L * HD, bytes_accessed=2 * MIB, transcendentals=2 * BLOCK * L
        ),
        name="attend_latents",
    )(*operands)


def last_kernel(both_ref, out_w_ref, out_ref):
    heads, state = (
        jnp.concatenate(
            [
                jnp.concatenate(
                    [both_ref[y * NLAT + i, half * PART : (half + 1) * PART] for i in range(NLAT)],
                    axis=1,
                )
                for y in range(NY)
            ],
            axis=0,
        )
        for half in range(2)
    )
    out_ref[...] = state.astype(F32) + dot(heads, out_weights(out_w_ref))


def last(both, out_w):
    return pl.pallas_call(
        last_kernel,
        out_shape=jax.ShapeDtypeStruct((128, D), F32),
        compiler_params=pltpu.CompilerParams(vmem_limit_bytes=16 * MIB),
        cost_estimate=pl.CostEstimate(
            flops=2 * 128 * D * D, bytes_accessed=4 * MIB, transcendentals=0
        ),
        name="last",
    )(both, out_w)


def head_angles(positions, inverse):
    angle = positions.astype(F32)[:, None] * inverse[None, :]
    cosine, sine = jnp.cos(angle), jnp.sin(angle)
    return (
        jnp.concatenate([cosine] * 4, axis=1),
        jnp.concatenate([-sine, sine, -sine, sine], axis=1),
    )


def body(token_ids, embed_table, input_gain, cross_qkv, cross_out, layer_gain, layer_qkv, layer_out):
    z, y = lax.axis_index("z"), lax.axis_index("y")
    lat = lax.axis_index(LAT)

    lat_index = jnp.full((1,), lat, jnp.int32)
    pack = pack_shards(
        lat_index, token_ids.reshape(4, 128), cross_qkv.reshape(48, WIDTH),
        layer_qkv.reshape(96, WIDTH), cross_out, layer_out.reshape(32, D),
    )
    by_z = lax.all_gather(pack, "z", axis=0)
    rest_zy = lax.all_gather(by_z[:, 80:], "y", axis=0)
    by_z, inverse, embed_table, input_gain = lax.optimization_barrier(
        (by_z, inverse_frequencies(), embed_table, input_gain)
    )
    by_zy = gather(by_z[:, :80], "y", NY)

    latent = jnp.arange(OWN, dtype=jnp.int32) + (z // 2) * 128 + y * PART + (z % 2) * OWN
    qcos, qsin = head_angles(N - L + latent, inverse)
    row = jnp.arange(BLOCK, dtype=jnp.int32)
    lpos = row // PART * 128 + y * PART + row % PART
    lcos, lsin = head_angles(lpos, inverse)
    fine = inverse[:, None] * jnp.arange(KEYS, dtype=F32)[None, :]
    coarse = jnp.arange(STEPS, dtype=F32)[:, None] * KEYS * inverse[None, :]
    coarse = jnp.broadcast_to(coarse[:, :, None], (STEPS, HALF, 128))
    tables = (qcos, qsin, jnp.cos(fine), jnp.sin(fine), jnp.cos(coarse), jnp.sin(coarse))
    wide = embed_table.astype(F32)
    normed = wide * lax.rsqrt(jnp.mean(wide * wide, axis=-1, keepdims=True) + 1e-06) * input_gain
    normed = normed.astype(BF)
    by_zy, normed, tables, lcos, lsin = lax.optimization_barrier((by_zy, normed, tables, lcos, lsin))
    cross_w = lax.all_gather(by_zy[:, :, 48:64, :], LAT, axis=0)

    latent_ids = by_zy[2:, NZ - 1, 64:68, :].reshape(L).astype(jnp.int32)
    own_ids = lax.dynamic_slice_in_dim(latent_ids, latent[0], OWN, 0)
    pick = (own_ids[:, None] == jnp.arange(VOCAB, dtype=jnp.int32)[None, :]).astype(BF)
    block_ids = lax.dynamic_slice_in_dim(latent_ids.reshape(8, NY, PART), y, 1, 1).reshape(BLOCK)
    block_pick = (block_ids[:, None] == jnp.arange(VOCAB, dtype=jnp.int32)[None, :]).astype(BF)
    qpos = jnp.broadcast_to(
        (N - L + jnp.concatenate([latent, latent]))[:, None], (2 * OWN, 128)
    )
    heads = cross_attention(by_zy, normed, pick, *tables, qpos)

    heads = lax.all_to_all(heads, "z", split_axis=0, concat_axis=0, tiled=True)
    heads, rest_zy = lax.optimization_barrier((heads, rest_zy))
    out_w = [
        lax.all_gather(rest_zy[:, :, 64 * i + 48 : 64 * i + 64], LAT, axis=0) for i in range(LAYERS)
    ]
    qkv = [rest_zy[:, :, 64 * i : 64 * i + 48] for i in range(LAYERS)]
    heads = heads.reshape(BLOCK, WIDTH)
    heads = gather_lat(jnp.broadcast_to(heads[None], (NX, BLOCK, WIDTH)))

    state, q, kv = dense(
        True, lat_index, heads, cross_w, block_pick, embed_table, layer_gain[0:1], qkv[0], lcos, lsin
    )
    kv = lax.all_to_all(kv, "y", split_axis=0, concat_axis=0, tiled=True)
    lpos = jnp.broadcast_to(lpos[:, None], (BLOCK, 128))
    heads = gather_lat(attend_latents(False, q, kv, lpos))
    state, q, kv = dense(
        False, lat_index, heads, out_w[0], state, embed_table, layer_gain[1:2], qkv[1], lcos, lsin
    )
    kv = lax.all_to_all(kv, "y", split_axis=0, concat_axis=0, tiled=True)
    both = attend_latents(True, q, kv, lpos, state)
    both = lax.all_to_all(both, ("y", "x", "c"), split_axis=0, concat_axis=0, tiled=True)
    return last(both, out_w[1])


def solution(mesh):
    grid = Mesh(np.asarray(mesh.devices).reshape(NZ, NY, NX, NC), ("z", "y", "x", "c"))
    return jax.shard_map(
        body,
        mesh=grid,
        in_specs=(
            P(CTX),
            P(),
            P(),
            P(None, CTX, LAT),
            P(CTX, None),
            P(),
            P(None, None, CTX, LAT),
            P(None, CTX, None),
        ),
        out_specs=P(LAT, None),
        check_vma=False,
    )
```

```python
import functools

import jax
import jax.numpy as jnp
import numpy as np
from jax import lax
from jax.experimental import pallas as pl
from jax.experimental.pallas import tpu as pltpu
from jax.sharding import Mesh
from jax.sharding import PartitionSpec as P

D = 1024
HD = 64
HALF = 32
NZ, NY, NX, NC = 16, 4, 4, 2
NLAT = NX * NC
N = 32768
L = 1024
VOCAB = 256
WIDTH = 128
OWN = 16
LAYERS = 2
PART = 32
BLOCK = 256
KEYS = 2048
STEPS = N // KEYS
LAT = ("x", "c")
CTX = ("z", "y")
BF = jnp.bfloat16
F32 = jnp.float32
MIB = 1 << 20


def inverse_frequencies():
    return 10000.0 ** (-2.0 * jnp.arange(HALF, dtype=F32) / (2 * HALF))


def gather(x, axis, count):
    return lax.all_to_all(
        jnp.broadcast_to(x[None], (count, *x.shape)), axis, split_axis=0, concat_axis=0, tiled=True
    )


def gather_lat(copies):
    by_x = lax.all_to_all(copies, "x", split_axis=0, concat_axis=0, tiled=True)
    return lax.all_gather(by_x, "c", axis=0)


def pack_kernel(lat_ref, *refs):
    ids_ref, cross_ref, layer_ref, cross_out_ref, layer_out_ref = refs[5:10]
    out_ref, sem = refs[10:]
    copies = [pltpu.make_async_copy(refs[i], refs[i + 5], sem.at[i]) for i in range(5)]
    for copy in copies:
        copy.start()
    for copy in copies:
        copy.wait()
    own = pl.ds(pl.multiple_of(lat_ref[0] * WIDTH, WIDTH), WIDTH)
    out_ref[0:48] = cross_ref[...]
    out_ref[48:64] = cross_out_ref[:, own]
    ids = ids_ref[...].astype(F32)
    out_ref[64:80] = jnp.concatenate([ids, jnp.zeros((12, WIDTH), F32)], axis=0).astype(BF)
    for layer in range(LAYERS):
        start = 80 + layer * 64
        out_ref[start : start + 48] = layer_ref[layer * 48 : (layer + 1) * 48]
        out_ref[start + 48 : start + 64] = layer_out_ref[layer * 16 : (layer + 1) * 16, own]


def pack_shards(lat_index, *operands):
    def kernel(lat_ref, *refs):
        pack_kernel(lat_ref, *refs[:5], *refs[6:11], refs[5], refs[11])

    return pl.pallas_call(
        kernel,
        out_shape=jax.ShapeDtypeStruct((208, WIDTH), BF),
        in_specs=[pl.BlockSpec(memory_space=pltpu.SMEM)] + [pl.BlockSpec(memory_space=pl.ANY)] * 5,
        out_specs=pl.BlockSpec(memory_space=pltpu.VMEM),
        scratch_shapes=[pltpu.VMEM(a.shape, a.dtype) for a in operands]
        + [pltpu.SemaphoreType.DMA((5,))],
        compiler_params=pltpu.CompilerParams(vmem_limit_bytes=58 * MIB),
        name="pack_shards",
    )(lat_index, *operands)


def project_kernel(heads_ref, w_ref, out_ref):
    heads = jnp.concatenate([heads_ref[i] for i in range(NLAT)], axis=1)
    rows = [w_ref[y, z, 48:64, :] for z in range(NZ) for y in range(NY)]
    out = dot(heads, jnp.concatenate(rows, axis=0)).astype(BF)
    for z in range(NZ):
        out_ref[z] = out


def project_columns(heads, weights):
    return pl.pallas_call(
        project_kernel,
        out_shape=jax.ShapeDtypeStruct((NZ, OWN, WIDTH), BF),
        compiler_params=pltpu.CompilerParams(vmem_limit_bytes=8 * MIB),
        cost_estimate=pl.CostEstimate(
            flops=2 * OWN * D * WIDTH, bytes_accessed=MIB, transcendentals=0
        ),
        name="project_columns",
    )(heads, weights)


def dot(a, b):
    return jnp.dot(a, b, preferred_element_type=F32)


def dot_nt(a, b):
    return lax.dot_general(a, b, (((1,), (1,)), ((), ())), preferred_element_type=F32)


def split_two(x):
    high = x.astype(BF)
    return high, (x - high.astype(F32)).astype(BF)


def rotate_lanes(x, cosine, sine):
    lane = lax.broadcasted_iota(jnp.int32, x.shape, 1)
    other = jnp.where(lane % HD < HALF, pltpu.roll(x, WIDTH - HALF, 1), pltpu.roll(x, HALF, 1))
    return x * cosine + other * sine


def cross_kernel(
    w_ref, normed_ref, pick_ref, qcos_ref, qsin_ref, cosb_ref, sinb_ref, cosa_ref, sina_ref, qpos_ref,
    out_ref, w_sc, table_sc, q_sc, s_sc, v_sc, cos_sc, sin_sc,
):
    for z in range(NZ):
        for y in range(NY):
            row = (z * NY + y) * 16
            for part in range(3):
                w_sc[row : row + 16, part * WIDTH : (part + 1) * WIDTH] = w_ref[
                    y, z, part * 16 : (part + 1) * 16, :
                ]
    normed = normed_ref[...]
    table_sc[...] = dot(normed, w_sc[:, WIDTH:]).T.astype(BF)
    rows = dot(pick_ref[...], normed).astype(BF)
    query = rotate_lanes(dot(rows, w_sc[:, :WIDTH]), qcos_ref[...], qsin_ref[...])
    query = query.astype(BF).astype(F32) * (HD**-0.5)
    lane = lax.broadcasted_iota(jnp.int32, query.shape, 1)
    q_sc[:OWN] = jnp.where(lane < HD, query, 0.0).astype(BF)
    q_sc[OWN:] = jnp.where(lane < HD, 0.0, query).astype(BF)
    token = lax.broadcasted_iota(jnp.int32, (VOCAB, 128), 0).astype(F32)
    ca, sa = cosa_ref[:, :1], sina_ref[:, :1]
    cos_sc[...], sin_sc[...] = cosb_ref[...], sinb_ref[...]

    def scores_of(step, top):
        hot = []
        for y in range(NY):
            ids = w_ref[y, step, 64:80, :].astype(F32)
            for r in range(4):
                hot.append(jnp.where(token == ids[r : r + 1, :], 1.0, 0.0).astype(BF))
        both = dot(table_sc[...], jnp.concatenate(hot, axis=1))
        v_sc[step] = both[WIDTH:].astype(BF)
        cosine, sine = cos_sc[...], sin_sc[...]
        cos_sc[...] = cosine * ca - sine * sa
        sin_sc[...] = sine * ca + cosine * sa
        pieces = []
        for head in range(2):
            first = both[head * HD : head * HD + HALF]
            second = both[head * HD + HALF : (head + 1) * HD]
            pieces.append(first * cosine - second * sine)
            pieces.append(second * cosine + first * sine)
        scores = dot(q_sc[...], jnp.concatenate(pieces, axis=0).astype(BF))
        kpos = step * KEYS + lax.broadcasted_iota(jnp.int32, scores.shape, 1)
        scores = jnp.where(kpos <= qpos_ref[:, :1], scores, -1e30)
        s_sc[step] = scores
        for i in range(KEYS // 128):
            top = jnp.maximum(top, scores[:, i * 128 : (i + 1) * 128])
        return top

    top = lax.fori_loop(0, STEPS, scores_of, jnp.full((2 * OWN, 128), -1e30, F32), unroll=4)
    most = jnp.max(top, axis=1, keepdims=True)

    def values_of(step, carry):
        total, acc = carry
        weight = jnp.exp(s_sc[step] - most)
        for i in range(KEYS // 128):
            total = total + weight[:, i * 128 : (i + 1) * 128]
        return total, acc + dot_nt(v_sc[step], weight.astype(BF))

    total, acc = lax.fori_loop(
        0, STEPS, values_of, (jnp.zeros((2 * OWN, 128), F32), jnp.zeros((WIDTH, 2 * OWN), F32)),
        unroll=4,
    )
    value = acc.T / jnp.sum(total, axis=1, keepdims=True)
    lane = lax.broadcasted_iota(jnp.int32, (OWN, WIDTH), 1)
    value = jnp.where(lane < HD, value[:OWN], value[OWN:]).astype(BF)
    for i in range(NLAT):
        out_ref[i] = value


def cross_attention(*operands):
    return pl.pallas_call(
        cross_kernel,
        out_shape=jax.ShapeDtypeStruct((NLAT, OWN, WIDTH), BF),
        scratch_shapes=[
            pltpu.VMEM((D, 3 * WIDTH), BF),
            pltpu.VMEM((2 * WIDTH, VOCAB), BF),
            pltpu.VMEM((2 * OWN, WIDTH), BF),
            pltpu.VMEM((STEPS, 2 * OWN, KEYS), F32),
            pltpu.VMEM((STEPS, WIDTH, KEYS), BF),
            pltpu.VMEM((HALF, KEYS), F32),
            pltpu.VMEM((HALF, KEYS), F32),
        ],
        compiler_params=pltpu.CompilerParams(vmem_limit_bytes=32 * MIB),
        cost_estimate=pl.CostEstimate(
            flops=MIB, bytes_accessed=MIB, transcendentals=0
        ),
        name="cross_attention",
    )(*operands)


def out_weights(ref):
    columns = []
    for i in range(NLAT):
        rows = [ref[i, y, z] for z in range(NZ) for y in range(NY)]
        columns.append(jnp.concatenate(rows, axis=0))
    return jnp.concatenate(columns, axis=1)


def dense_kernel(first, *refs):
    lat_ref, parts_ref, state_ref, matrix_ref, gain_ref, qkv_ref, cos_ref, sin_ref = refs[:8]
    state_out, q_out, kv_out = refs[8:11]
    parts = jnp.concatenate([parts_ref[i % NC, i // NC] for i in range(NLAT)], axis=1)
    if first:
        state = dot(state_ref[...], matrix_ref[...]) + parts.astype(F32)
        state_out[...] = state
    else:
        state = state_ref[...] + dot(parts, out_weights(matrix_ref))
        state_sc = refs[11]
        state_sc[...] = state
        own = pl.ds(pl.multiple_of(lat_ref[0] * WIDTH, WIDTH), WIDTH)
        state_out[...] = state_sc[:, own].astype(BF)
    scale = lax.rsqrt(jnp.mean(state * state, axis=1, keepdims=True) + 1e-06)
    normed = (state * scale * gain_ref[...]).astype(BF)
    cosine, sine = cos_ref[...], sin_ref[...]
    weights = [
        jnp.concatenate(
            [qkv_ref[y, z, i * 16 : (i + 1) * 16] for z in range(NZ) for y in range(NY)], axis=0
        )
        for i in range(3)
    ]
    product = dot(normed, jnp.concatenate(weights, axis=1))
    q_out[...] = rotate_lanes(product[:, :WIDTH], cosine, sine).astype(BF)
    k = rotate_lanes(product[:, WIDTH : 2 * WIDTH], cosine, sine).astype(BF)
    v = product[:, 2 * WIDTH :].astype(BF)
    for y in range(NY):
        kv_out[y, :, :WIDTH] = k
        kv_out[y, :, WIDTH:] = v


def dense(first, *operands):
    smem, vmem = (pl.BlockSpec(memory_space=m) for m in (pltpu.SMEM, pltpu.VMEM))
    return pl.pallas_call(
        functools.partial(dense_kernel, first),
        out_shape=(
            jax.ShapeDtypeStruct((BLOCK, D), F32)
            if first
            else jax.ShapeDtypeStruct((BLOCK, WIDTH), BF),
            jax.ShapeDtypeStruct((BLOCK, WIDTH), BF),
            jax.ShapeDtypeStruct((NY, BLOCK, 2 * WIDTH), BF),
        ),
        in_specs=[smem] + [vmem] * 7,
        scratch_shapes=[] if first else [pltpu.VMEM((BLOCK, D), F32)],
        compiler_params=pltpu.CompilerParams(vmem_limit_bytes=24 * MIB),
        cost_estimate=pl.CostEstimate(
            flops=2 * BLOCK * D * (D + 3 * WIDTH), bytes_accessed=8 * MIB, transcendentals=BLOCK
        ),
        name="dense",
    )(*operands)


def key_positions():
    column = lax.broadcasted_iota(jnp.int32, (1, L), 1)
    return (column % BLOCK) // PART * 128 + column // BLOCK * PART + column % PART


def attend(q, k, v, qpos, kpos):
    outs = []
    seen = kpos <= qpos
    for head in range(2):
        lanes = slice(head * HD, (head + 1) * HD)
        scores = dot_nt(q[:, lanes], k[:, lanes]) * (HD**-0.5)
        scores = jnp.where(seen, scores, -1e30)
        weight = jnp.exp(scores - jnp.max(scores, axis=1, keepdims=True))
        total = jnp.sum(weight, axis=1, keepdims=True)
        outs.append(dot(weight.astype(BF), v[:, lanes]) / total)
    return jnp.concatenate(outs, axis=1).astype(BF)


def attend_kernel(final, q_ref, kv_ref, qpos_ref, *refs):
    out_ref = refs[-1]
    kv = jnp.concatenate([kv_ref[i] for i in range(NY)], axis=0)
    out = attend(q_ref[...], kv[:, :WIDTH], kv[:, WIDTH:], qpos_ref[:, :1], key_positions())
    if final:
        state = refs[0][...]
        for y in range(NY):
            for i in range(NLAT):
                out_ref[y * NLAT + i, :PART] = out[i * PART : (i + 1) * PART]
                out_ref[y * NLAT + i, PART:] = state[i * PART : (i + 1) * PART]
    else:
        for i in range(NX):
            out_ref[i] = out


def attend_latents(final, *operands):
    shape = (NY * NLAT, 2 * PART, WIDTH) if final else (NX, BLOCK, WIDTH)
    return pl.pallas_call(
        functools.partial(attend_kernel, final),
        out_shape=jax.ShapeDtypeStruct(shape, BF),
        compiler_params=pltpu.CompilerParams(vmem_limit_bytes=16 * MIB),
        cost_estimate=pl.CostEstimate(
            flops=8 * BLOCK * L * HD, bytes_accessed=2 * MIB, transcendentals=2 * BLOCK * L
        ),
        name="attend_latents",
    )(*operands)


def last_kernel(both_ref, out_w_ref, out_ref):
    heads, state = (
        jnp.concatenate(
            [
                jnp.concatenate(
                    [both_ref[y * NLAT + i, half * PART : (half + 1) * PART] for i in range(NLAT)],
                    axis=1,
                )
                for y in range(NY)
            ],
            axis=0,
        )
        for half in range(2)
    )
    out_ref[...] = state.astype(F32) + dot(heads, out_weights(out_w_ref))


def last(both, out_w):
    return pl.pallas_call(
        last_kernel,
        out_shape=jax.ShapeDtypeStruct((128, D), F32),
        compiler_params=pltpu.CompilerParams(vmem_limit_bytes=16 * MIB),
        cost_estimate=pl.CostEstimate(
            flops=2 * 128 * D * D, bytes_accessed=4 * MIB, transcendentals=0
        ),
        name="last",
    )(both, out_w)


def head_angles(positions, inverse):
    angle = positions.astype(F32)[:, None] * inverse[None, :]
    cosine, sine = jnp.cos(angle), jnp.sin(angle)
    return (
        jnp.concatenate([cosine] * 4, axis=1),
        jnp.concatenate([-sine, sine, -sine, sine], axis=1),
    )


def body(token_ids, embed_table, input_gain, cross_qkv, cross_out, layer_gain, layer_qkv, layer_out):
    z, y = lax.axis_index("z"), lax.axis_index("y")
    lat = lax.axis_index(LAT)

    lat_index = jnp.full((1,), lat, jnp.int32)
    pack = pack_shards(
        lat_index, token_ids.reshape(4, 128), cross_qkv.reshape(48, WIDTH),
        layer_qkv.reshape(96, WIDTH), cross_out, layer_out.reshape(32, D),
    )
    by_z = lax.all_gather(pack, "z", axis=0)
    rest_zy = lax.all_gather(by_z[:, 80:], "y", axis=0)
    by_z, inverse, embed_table, input_gain = lax.optimization_barrier(
        (by_z, inverse_frequencies(), embed_table, input_gain)
    )
    by_zy = gather(by_z[:, :80], "y", NY)

    latent = jnp.arange(OWN, dtype=jnp.int32) + (z // 2) * 128 + y * PART + (z % 2) * OWN
    qcos, qsin = head_angles(N - L + latent, inverse)
    row = jnp.arange(BLOCK, dtype=jnp.int32)
    lpos = row // PART * 128 + y * PART + row % PART
    lcos, lsin = head_angles(lpos, inverse)
    fine = inverse[:, None] * jnp.arange(KEYS, dtype=F32)[None, :]
    coarse = jnp.broadcast_to(inverse[:, None] * KEYS, (HALF, 128))
    tables = (qcos, qsin, jnp.cos(fine), jnp.sin(fine), jnp.cos(coarse), jnp.sin(coarse))
    wide = embed_table.astype(F32)
    normed = wide * lax.rsqrt(jnp.mean(wide * wide, axis=-1, keepdims=True) + 1e-06) * input_gain
    normed = normed.astype(BF)
    by_zy, normed, tables, lcos, lsin = lax.optimization_barrier((by_zy, normed, tables, lcos, lsin))
    latent_ids = by_zy[2:, NZ - 1, 64:68, :].reshape(L).astype(jnp.int32)
    own_ids = lax.dynamic_slice_in_dim(latent_ids, latent[0], OWN, 0)
    pick = (own_ids[:, None] == jnp.arange(VOCAB, dtype=jnp.int32)[None, :]).astype(BF)
    block_ids = lax.dynamic_slice_in_dim(latent_ids.reshape(8, NY, PART), y, 1, 1).reshape(BLOCK)
    block_pick = (block_ids[:, None] == jnp.arange(VOCAB, dtype=jnp.int32)[None, :]).astype(BF)
    qpos = jnp.broadcast_to(
        (N - L + jnp.concatenate([latent, latent]))[:, None], (2 * OWN, 128)
    )
    heads = cross_attention(by_zy, normed, pick, *tables, qpos)

    heads = lax.all_to_all(heads, LAT, split_axis=0, concat_axis=0, tiled=True)
    added = project_columns(heads, by_zy)

    added = lax.all_to_all(added, "z", split_axis=0, concat_axis=0, tiled=True)
    added, rest_zy = lax.optimization_barrier((added, rest_zy))
    out_w = [
        lax.all_gather(rest_zy[:, :, 64 * i + 48 : 64 * i + 64], LAT, axis=0) for i in range(LAYERS)
    ]
    qkv = [rest_zy[:, :, 64 * i : 64 * i + 48] for i in range(LAYERS)]
    added = added.reshape(BLOCK, WIDTH)
    added = gather_lat(jnp.broadcast_to(added[None], (NX, BLOCK, WIDTH)))

    state, q, kv = dense(
        True, lat_index, added, block_pick, embed_table, layer_gain[0:1], qkv[0], lcos, lsin
    )
    kv = lax.all_to_all(kv, "y", split_axis=0, concat_axis=0, tiled=True)
    kv, *out_w = lax.optimization_barrier((kv, *out_w[:1])) + (out_w[1],)
    lpos = jnp.broadcast_to(lpos[:, None], (BLOCK, 128))
    heads = gather_lat(attend_latents(False, q, kv, lpos))
    state, q, kv = dense(
        False, lat_index, heads, state, out_w[0], layer_gain[1:2], qkv[1], lcos, lsin
    )
    kv = lax.all_to_all(kv, "y", split_axis=0, concat_axis=0, tiled=True)
    kv, last_w = lax.optimization_barrier((kv, out_w[1]))
    both = attend_latents(True, q, kv, lpos, state)
    both = lax.all_to_all(both, ("y", "x", "c"), split_axis=0, concat_axis=0, tiled=True)
    return last(both, last_w)


def solution(mesh):
    grid = Mesh(np.asarray(mesh.devices).reshape(NZ, NY, NX, NC), ("z", "y", "x", "c"))
    return jax.shard_map(
        body,
        mesh=grid,
        in_specs=(
            P(CTX),
            P(),
            P(),
            P(None, CTX, LAT),
            P(CTX, None),
            P(),
            P(None, None, CTX, LAT),
            P(None, CTX, None),
        ),
        out_specs=P(LAT, None),
        check_vma=False,
    )
```

```python
import functools

import jax
import jax.numpy as jnp
import numpy as np
from jax import lax
from jax.experimental import pallas as pl
from jax.experimental.pallas import tpu as pltpu
from jax.sharding import Mesh
from jax.sharding import PartitionSpec as P

D = 1024
HD = 64
HALF = 32
NZ, NY, NX, NC = 16, 4, 4, 2
NLAT = NX * NC
N = 32768
L = 1024
VOCAB = 256
WIDTH = 128
OWN = 16
LAYERS = 2
PART = 32
BLOCK = 256
KEYS = 2048
STEPS = N // KEYS
LAT = ("x", "c")
CTX = ("z", "y")
BF = jnp.bfloat16
F32 = jnp.float32
MIB = 1 << 20


def inverse_frequencies():
    return 10000.0 ** (-2.0 * jnp.arange(HALF, dtype=F32) / (2 * HALF))


def gather(x, axis, count):
    return lax.all_to_all(
        jnp.broadcast_to(x[None], (count, *x.shape)), axis, split_axis=0, concat_axis=0, tiled=True
    )


def gather_lat(copies):
    by_x = lax.all_to_all(copies, "x", split_axis=0, concat_axis=0, tiled=True)
    return lax.all_gather(by_x, "c", axis=0)


def pack_kernel(lat_ref, *refs):
    ids_ref, cross_ref, layer_ref, cross_out_ref, layer_out_ref = refs[5:10]
    out_ref, sem = refs[10:]
    copies = [pltpu.make_async_copy(refs[i], refs[i + 5], sem.at[i]) for i in range(5)]
    for copy in copies:
        copy.start()
    for copy in copies:
        copy.wait()
    own = pl.ds(pl.multiple_of(lat_ref[0] * WIDTH, WIDTH), WIDTH)
    out_ref[0:48] = cross_ref[...]
    out_ref[48:64] = cross_out_ref[:, own]
    ids = ids_ref[...].astype(F32)
    out_ref[192:200] = jnp.concatenate([ids, jnp.zeros((4, WIDTH), F32)], axis=0).astype(BF)
    for layer in range(LAYERS):
        start = 64 + layer * 64
        out_ref[start : start + 48] = layer_ref[layer * 48 : (layer + 1) * 48]
        out_ref[start + 48 : start + 64] = layer_out_ref[layer * 16 : (layer + 1) * 16, own]


def pack_shards(lat_index, *operands):
    def kernel(lat_ref, *refs):
        pack_kernel(lat_ref, *refs[:5], *refs[6:11], refs[5], refs[11])

    return pl.pallas_call(
        kernel,
        out_shape=jax.ShapeDtypeStruct((200, WIDTH), BF),
        in_specs=[pl.BlockSpec(memory_space=pltpu.SMEM)] + [pl.BlockSpec(memory_space=pl.ANY)] * 5,
        out_specs=pl.BlockSpec(memory_space=pltpu.VMEM),
        scratch_shapes=[pltpu.VMEM(a.shape, a.dtype) for a in operands]
        + [pltpu.SemaphoreType.DMA((5,))],
        compiler_params=pltpu.CompilerParams(vmem_limit_bytes=58 * MIB),
        name="pack_shards",
    )(lat_index, *operands)


def project_kernel(heads_ref, w_ref, out_ref):
    heads = jnp.concatenate([heads_ref[i] for i in range(NLAT)], axis=1)
    rows = [w_ref[y, z * 64 + 48 : z * 64 + 64] for z in range(NZ) for y in range(NY)]
    out = dot(heads, jnp.concatenate(rows, axis=0)).astype(BF)
    for z in range(NZ):
        out_ref[z] = out


def project_columns(heads, weights):
    return pl.pallas_call(
        project_kernel,
        out_shape=jax.ShapeDtypeStruct((NZ, OWN, WIDTH), BF),
        compiler_params=pltpu.CompilerParams(vmem_limit_bytes=8 * MIB),
        cost_estimate=pl.CostEstimate(
            flops=2 * OWN * D * WIDTH, bytes_accessed=MIB, transcendentals=0
        ),
        name="project_columns",
    )(heads, weights)


def dot(a, b):
    return jnp.dot(a, b, preferred_element_type=F32)


def dot_nt(a, b):
    return lax.dot_general(a, b, (((1,), (1,)), ((), ())), preferred_element_type=F32)


def split_two(x):
    high = x.astype(BF)
    return high, (x - high.astype(F32)).astype(BF)


def rotate_lanes(x, cosine, sine):
    lane = lax.broadcasted_iota(jnp.int32, x.shape, 1)
    other = jnp.where(lane % HD < HALF, pltpu.roll(x, WIDTH - HALF, 1), pltpu.roll(x, HALF, 1))
    return x * cosine + other * sine


def cross_kernel(
    w_ref, normed_ref, pick_ref, qcos_ref, qsin_ref, cosb_ref, sinb_ref, cosa_ref, sina_ref, qpos_ref,
    out_ref, w_sc, table_sc, q_sc, s_sc, v_sc, cos_sc, sin_sc, ids_sc,
):
    for z in range(NZ):
        for y in range(NY):
            row = (z * NY + y) * 16
            for part in range(3):
                start = z * 64 + part * 16
                w_sc[row : row + 16, part * WIDTH : (part + 1) * WIDTH] = w_ref[
                    y, start : start + 16, :
                ]
    for y in range(NY):
        ids = w_ref[y, NZ * 64 :, :].astype(F32)
        for z in range(NZ):
            ids_sc[z, y * 4 : (y + 1) * 4] = ids[z * 4 : (z + 1) * 4]
    normed = normed_ref[...]
    table_sc[...] = dot(normed, w_sc[:, WIDTH:]).T.astype(BF)
    rows = dot(pick_ref[...], normed).astype(BF)
    query = rotate_lanes(dot(rows, w_sc[:, :WIDTH]), qcos_ref[...], qsin_ref[...])
    query = query.astype(BF).astype(F32) * (HD**-0.5)
    lane = lax.broadcasted_iota(jnp.int32, query.shape, 1)
    q_sc[:OWN] = jnp.where(lane < HD, query, 0.0).astype(BF)
    q_sc[OWN:] = jnp.where(lane < HD, 0.0, query).astype(BF)
    token = lax.broadcasted_iota(jnp.int32, (VOCAB, 128), 0).astype(F32)
    ca, sa = cosa_ref[:, :1], sina_ref[:, :1]
    cos_sc[...], sin_sc[...] = cosb_ref[...], sinb_ref[...]

    def scores_of(step, top):
        hot = []
        ids = ids_sc[step]
        for r in range(16):
            hot.append(jnp.where(token == ids[r : r + 1, :], 1.0, 0.0).astype(BF))
        both = dot(table_sc[...], jnp.concatenate(hot, axis=1))
        v_sc[step] = both[WIDTH:].astype(BF)
        cosine, sine = cos_sc[...], sin_sc[...]
        cos_sc[...] = cosine * ca - sine * sa
        sin_sc[...] = sine * ca + cosine * sa
        pieces = []
        for head in range(2):
            first = both[head * HD : head * HD + HALF]
            second = both[head * HD + HALF : (head + 1) * HD]
            pieces.append(first * cosine - second * sine)
            pieces.append(second * cosine + first * sine)
        scores = dot(q_sc[...], jnp.concatenate(pieces, axis=0).astype(BF))
        kpos = step * KEYS + lax.broadcasted_iota(jnp.int32, scores.shape, 1)
        scores = jnp.where(kpos <= qpos_ref[:, :1], scores, -1e30)
        s_sc[step] = scores
        for i in range(KEYS // 128):
            top = jnp.maximum(top, scores[:, i * 128 : (i + 1) * 128])
        return top

    top = lax.fori_loop(0, STEPS, scores_of, jnp.full((2 * OWN, 128), -1e30, F32), unroll=4)
    most = jnp.max(top, axis=1, keepdims=True)

    def values_of(step, carry):
        total, acc = carry
        weight = jnp.exp(s_sc[step] - most)
        for i in range(KEYS // 128):
            total = total + weight[:, i * 128 : (i + 1) * 128]
        return total, acc + dot_nt(v_sc[step], weight.astype(BF))

    total, acc = lax.fori_loop(
        0, STEPS, values_of, (jnp.zeros((2 * OWN, 128), F32), jnp.zeros((WIDTH, 2 * OWN), F32)),
        unroll=4,
    )
    value = acc.T / jnp.sum(total, axis=1, keepdims=True)
    lane = lax.broadcasted_iota(jnp.int32, (OWN, WIDTH), 1)
    value = jnp.where(lane < HD, value[:OWN], value[OWN:]).astype(BF)
    for i in range(NLAT):
        out_ref[i] = value


def cross_attention(*operands):
    return pl.pallas_call(
        cross_kernel,
        out_shape=jax.ShapeDtypeStruct((NLAT, OWN, WIDTH), BF),
        scratch_shapes=[
            pltpu.VMEM((D, 3 * WIDTH), BF),
            pltpu.VMEM((2 * WIDTH, VOCAB), BF),
            pltpu.VMEM((2 * OWN, WIDTH), BF),
            pltpu.VMEM((STEPS, 2 * OWN, KEYS), F32),
            pltpu.VMEM((STEPS, WIDTH, KEYS), BF),
            pltpu.VMEM((HALF, KEYS), F32),
            pltpu.VMEM((HALF, KEYS), F32),
            pltpu.VMEM((NZ, 16, 128), F32),
        ],
        compiler_params=pltpu.CompilerParams(vmem_limit_bytes=32 * MIB),
        cost_estimate=pl.CostEstimate(
            flops=MIB, bytes_accessed=MIB, transcendentals=0
        ),
        name="cross_attention",
    )(*operands)


def out_weights(ref):
    columns = []
    for i in range(NLAT):
        rows = [ref[i, y, z] for z in range(NZ) for y in range(NY)]
        columns.append(jnp.concatenate(rows, axis=0))
    return jnp.concatenate(columns, axis=1)


def dense_kernel(first, *refs):
    lat_ref, parts_ref, state_ref, matrix_ref, gain_ref, qkv_ref, cos_ref, sin_ref = refs[:8]
    state_out, q_out, kv_out = refs[8:11]
    parts = jnp.concatenate([parts_ref[i % NC, i // NC] for i in range(NLAT)], axis=1)
    if first:
        state = dot(state_ref[...], matrix_ref[...]) + parts.astype(F32)
        state_out[...] = state
    else:
        state = state_ref[...] + dot(parts, out_weights(matrix_ref))
        state_sc = refs[11]
        state_sc[...] = state
        own = pl.ds(pl.multiple_of(lat_ref[0] * WIDTH, WIDTH), WIDTH)
        state_out[...] = state_sc[:, own].astype(BF)
    scale = lax.rsqrt(jnp.mean(state * state, axis=1, keepdims=True) + 1e-06)
    normed = (state * scale * gain_ref[0 if first else 1, :][None]).astype(BF)
    cosine, sine = cos_ref[...], sin_ref[...]
    weights = [
        jnp.concatenate(
            [qkv_ref[y, z, i * 16 : (i + 1) * 16] for z in range(NZ) for y in range(NY)], axis=0
        )
        for i in range(3)
    ]
    product = dot(normed, jnp.concatenate(weights, axis=1))
    q_out[...] = rotate_lanes(product[:, :WIDTH], cosine, sine).astype(BF)
    k = rotate_lanes(product[:, WIDTH : 2 * WIDTH], cosine, sine).astype(BF)
    v = product[:, 2 * WIDTH :].astype(BF)
    for y in range(NY):
        kv_out[y, :, :WIDTH] = k
        kv_out[y, :, WIDTH:] = v


def dense(first, *operands):
    smem, vmem = (pl.BlockSpec(memory_space=m) for m in (pltpu.SMEM, pltpu.VMEM))
    return pl.pallas_call(
        functools.partial(dense_kernel, first),
        out_shape=(
            jax.ShapeDtypeStruct((BLOCK, D), F32)
            if first
            else jax.ShapeDtypeStruct((BLOCK, WIDTH), BF),
            jax.ShapeDtypeStruct((BLOCK, WIDTH), BF),
            jax.ShapeDtypeStruct((NY, BLOCK, 2 * WIDTH), BF),
        ),
        in_specs=[smem] + [vmem] * 7,
        scratch_shapes=[] if first else [pltpu.VMEM((BLOCK, D), F32)],
        compiler_params=pltpu.CompilerParams(vmem_limit_bytes=24 * MIB),
        cost_estimate=pl.CostEstimate(
            flops=2 * BLOCK * D * (D + 3 * WIDTH), bytes_accessed=8 * MIB, transcendentals=BLOCK
        ),
        name="dense",
    )(*operands)


def key_positions():
    column = lax.broadcasted_iota(jnp.int32, (1, L), 1)
    return (column % BLOCK) // PART * 128 + column // BLOCK * PART + column % PART


def attend(q, k, v, qpos, kpos):
    outs = []
    seen = kpos <= qpos
    for head in range(2):
        lanes = slice(head * HD, (head + 1) * HD)
        scores = dot_nt(q[:, lanes], k[:, lanes]) * (HD**-0.5)
        scores = jnp.where(seen, scores, -1e30)
        weight = jnp.exp(scores - jnp.max(scores, axis=1, keepdims=True))
        total = jnp.sum(weight, axis=1, keepdims=True)
        outs.append(dot(weight.astype(BF), v[:, lanes]) / total)
    return jnp.concatenate(outs, axis=1).astype(BF)


def attend_kernel(final, y_ref, q_ref, kv_ref, *refs):
    out_ref = refs[-1]
    row = lax.broadcasted_iota(jnp.int32, (BLOCK, 1), 0)
    qpos = row // PART * 128 + y_ref[0] * PART + row % PART
    kv = jnp.concatenate([kv_ref[i] for i in range(NY)], axis=0)
    out = attend(q_ref[...], kv[:, :WIDTH], kv[:, WIDTH:], qpos, key_positions())
    if final:
        state = refs[0][...]
        for y in range(NY):
            for i in range(NLAT):
                out_ref[y * NLAT + i, :PART] = out[i * PART : (i + 1) * PART]
                out_ref[y * NLAT + i, PART:] = state[i * PART : (i + 1) * PART]
    else:
        for i in range(NX):
            out_ref[i] = out


def attend_latents(final, *operands):
    shape = (NY * NLAT, 2 * PART, WIDTH) if final else (NX, BLOCK, WIDTH)
    smem, vmem = (pl.BlockSpec(memory_space=m) for m in (pltpu.SMEM, pltpu.VMEM))
    return pl.pallas_call(
        functools.partial(attend_kernel, final),
        out_shape=jax.ShapeDtypeStruct(shape, BF),
        in_specs=[smem] + [vmem] * (len(operands) - 1),
        compiler_params=pltpu.CompilerParams(vmem_limit_bytes=16 * MIB),
        cost_estimate=pl.CostEstimate(
            flops=8 * BLOCK * L * HD, bytes_accessed=2 * MIB, transcendentals=2 * BLOCK * L
        ),
        name="attend_latents",
    )(*operands)


def last_kernel(both_ref, out_w_ref, out_ref):
    heads, state = (
        jnp.concatenate(
            [
                jnp.concatenate(
                    [both_ref[y * NLAT + i, half * PART : (half + 1) * PART] for i in range(NLAT)],
                    axis=1,
                )
                for y in range(NY)
            ],
            axis=0,
        )
        for half in range(2)
    )
    out_ref[...] = state.astype(F32) + dot(heads, out_weights(out_w_ref))


def last(both, out_w):
    return pl.pallas_call(
        last_kernel,
        out_shape=jax.ShapeDtypeStruct((128, D), F32),
        compiler_params=pltpu.CompilerParams(vmem_limit_bytes=16 * MIB),
        cost_estimate=pl.CostEstimate(
            flops=2 * 128 * D * D, bytes_accessed=4 * MIB, transcendentals=0
        ),
        name="last",
    )(both, out_w)


def head_angles(positions, inverse):
    angle = positions.astype(F32)[:, None] * inverse[None, :]
    cosine, sine = jnp.cos(angle), jnp.sin(angle)
    return (
        jnp.concatenate([cosine] * 4, axis=1),
        jnp.concatenate([-sine, sine, -sine, sine], axis=1),
    )


def body(token_ids, embed_table, input_gain, cross_qkv, cross_out, layer_gain, layer_qkv, layer_out):
    z, y = lax.axis_index("z"), lax.axis_index("y")
    lat = lax.axis_index(LAT)

    lat_index = jnp.full((1,), lat, jnp.int32)
    pack = pack_shards(
        lat_index, token_ids.reshape(4, 128), cross_qkv.reshape(48, WIDTH),
        layer_qkv.reshape(96, WIDTH), cross_out, layer_out.reshape(32, D),
    )
    by_z = lax.all_gather(pack, "z", axis=0)
    by_z, inverse, embed_table, input_gain = lax.optimization_barrier(
        (by_z, inverse_frequencies(), embed_table, input_gain)
    )
    now = jnp.concatenate(
        [by_z[:, :64].reshape(NZ * 64, WIDTH), by_z[:, 192:196].reshape(NZ * 4, WIDTH)], axis=0
    )
    by_zy = gather(now, "y", NY)

    latent = jnp.arange(OWN, dtype=jnp.int32) + (z // 2) * 128 + y * PART + (z % 2) * OWN
    qcos, qsin = head_angles(N - L + latent, inverse)
    row = jnp.arange(BLOCK, dtype=jnp.int32)
    lpos = row // PART * 128 + y * PART + row % PART
    lcos, lsin = head_angles(lpos, inverse)
    fine = inverse[:, None] * jnp.arange(KEYS, dtype=F32)[None, :]
    coarse = jnp.broadcast_to(inverse[:, None] * KEYS, (HALF, 128))
    tables = (qcos, qsin, jnp.cos(fine), jnp.sin(fine), jnp.cos(coarse), jnp.sin(coarse))
    wide = embed_table.astype(F32)
    normed = wide * lax.rsqrt(jnp.mean(wide * wide, axis=-1, keepdims=True) + 1e-06) * input_gain
    normed = normed.astype(BF)
    by_zy, rest_z, normed, tables, lcos, lsin = lax.optimization_barrier(
        (by_zy, by_z[:, 64:192], normed, tables, lcos, lsin)
    )
    rest_zy = lax.all_gather(rest_z, "y", axis=0)
    outs = [rest_zy[:, :, 64 * i + 48 : 64 * i + 64] for i in range(LAYERS)]
    qkv = [rest_zy[:, :, 64 * i : 64 * i + 48] for i in range(LAYERS)]
    latent_ids = by_zy[2:, NZ * 68 - 4 :].reshape(L).astype(jnp.int32)
    own_ids = lax.dynamic_slice_in_dim(latent_ids, latent[0], OWN, 0)
    pick = (own_ids[:, None] == jnp.arange(VOCAB, dtype=jnp.int32)[None, :]).astype(BF)
    block_ids = lax.dynamic_slice_in_dim(latent_ids.reshape(8, NY, PART), y, 1, 1).reshape(BLOCK)
    block_pick = (block_ids[:, None] == jnp.arange(VOCAB, dtype=jnp.int32)[None, :]).astype(BF)
    qpos = jnp.broadcast_to(
        (N - L + jnp.concatenate([latent, latent]))[:, None], (2 * OWN, 128)
    )
    heads = cross_attention(by_zy, normed, pick, *tables, qpos)

    heads = lax.all_to_all(heads, LAT, split_axis=0, concat_axis=0, tiled=True)
    added = project_columns(heads, by_zy)

    added = lax.all_to_all(added, "z", split_axis=0, concat_axis=0, tiled=True)
    added, outs, qkv, block_pick = lax.optimization_barrier((added, outs, qkv, block_pick))
    out_w = [lax.all_gather(w, LAT, axis=0) for w in outs]
    added = added.reshape(BLOCK, WIDTH)
    added = gather_lat(jnp.broadcast_to(added[None], (NX, BLOCK, WIDTH)))

    state, q, kv = dense(
        True, lat_index, added, block_pick, embed_table, layer_gain, qkv[0], lcos, lsin
    )
    kv = lax.all_to_all(kv, "y", split_axis=0, concat_axis=0, tiled=True)
    y_index = jnp.full((1,), y, jnp.int32)
    heads = attend_latents(False, y_index, q, kv)
    heads, layer_w = lax.optimization_barrier((heads, out_w[0]))
    heads = gather_lat(heads)
    state, q, kv = dense(
        False, lat_index, heads, state, layer_w, layer_gain, qkv[1], lcos, lsin
    )
    kv = lax.all_to_all(kv, "y", split_axis=0, concat_axis=0, tiled=True)
    both = attend_latents(True, y_index, q, kv, state)
    both = lax.all_to_all(both, ("y", "x", "c"), split_axis=0, concat_axis=0, tiled=True)
    return last(both, out_w[1])


def solution(mesh):
    grid = Mesh(np.asarray(mesh.devices).reshape(NZ, NY, NX, NC), ("z", "y", "x", "c"))
    return jax.shard_map(
        body,
        mesh=grid,
        in_specs=(
            P(CTX),
            P(),
            P(),
            P(None, CTX, LAT),
            P(CTX, None),
            P(),
            P(None, None, CTX, LAT),
            P(None, CTX, None),
        ),
        out_specs=P(LAT, None),
        check_vma=False,
    )
```

```python
import functools

import jax
import jax.numpy as jnp
import numpy as np
from jax import lax
from jax.experimental import pallas as pl
from jax.experimental.pallas import tpu as pltpu
from jax.sharding import Mesh
from jax.sharding import PartitionSpec as P

D = 1024
HD = 64
HALF = 32
NZ, NY, NX, NC = 16, 4, 4, 2
NLAT = NX * NC
N = 32768
L = 1024
VOCAB = 256
WIDTH = 128
OWN = 16
LAYERS = 2
PART = 32
BLOCK = 256
KEYS = 2048
STEPS = N // KEYS
LAT = ("x", "c")
CTX = ("z", "y")
BF = jnp.bfloat16
F32 = jnp.float32
MIB = 1 << 20


def inverse_frequencies():
    return 10000.0 ** (-2.0 * jnp.arange(HALF, dtype=F32) / (2 * HALF))


def gather(x, axis, count):
    return lax.all_to_all(
        jnp.broadcast_to(x[None], (count, *x.shape)), axis, split_axis=0, concat_axis=0, tiled=True
    )


def gather_lat(copies):
    by_x = lax.all_to_all(copies, "x", split_axis=0, concat_axis=0, tiled=True)
    return lax.all_gather(by_x, "c", axis=0)


def pack_kernel(lat_ref, *refs):
    ids_ref, cross_ref, layer_ref, cross_out_ref, layer_out_ref = refs[5:10]
    out_ref, sem = refs[10:]
    copies = [pltpu.make_async_copy(refs[i], refs[i + 5], sem.at[i]) for i in range(5)]
    for copy in copies:
        copy.start()
    for copy in copies:
        copy.wait()
    own = pl.ds(pl.multiple_of(lat_ref[0] * WIDTH, WIDTH), WIDTH)
    out_ref[0:48] = cross_ref[...]
    out_ref[48:64] = cross_out_ref[:, own]
    ids = ids_ref[...].astype(F32)
    out_ref[192:200] = jnp.concatenate([ids, jnp.zeros((4, WIDTH), F32)], axis=0).astype(BF)
    for layer in range(LAYERS):
        start = 64 + layer * 64
        out_ref[start : start + 48] = layer_ref[layer * 48 : (layer + 1) * 48]
        out_ref[start + 48 : start + 64] = layer_out_ref[layer * 16 : (layer + 1) * 16, own]


def pack_shards(lat_index, *operands):
    def kernel(lat_ref, *refs):
        pack_kernel(lat_ref, *refs[:5], *refs[6:11], refs[5], refs[11])

    return pl.pallas_call(
        kernel,
        out_shape=jax.ShapeDtypeStruct((200, WIDTH), BF),
        in_specs=[pl.BlockSpec(memory_space=pltpu.SMEM)] + [pl.BlockSpec(memory_space=pl.ANY)] * 5,
        out_specs=pl.BlockSpec(memory_space=pltpu.VMEM),
        scratch_shapes=[pltpu.VMEM(a.shape, a.dtype) for a in operands]
        + [pltpu.SemaphoreType.DMA((5,))],
        compiler_params=pltpu.CompilerParams(vmem_limit_bytes=58 * MIB),
        name="pack_shards",
    )(lat_index, *operands)


def project_kernel(heads_ref, w_ref, out_ref):
    heads = jnp.concatenate([heads_ref[i] for i in range(NLAT)], axis=1)
    rows = [w_ref[y, z * 64 + 48 : z * 64 + 64] for z in range(NZ) for y in range(NY)]
    out = dot(heads, jnp.concatenate(rows, axis=0)).astype(BF)
    for z in range(NZ):
        out_ref[z] = out


def project_columns(heads, weights):
    return pl.pallas_call(
        project_kernel,
        out_shape=jax.ShapeDtypeStruct((NZ, OWN, WIDTH), BF),
        compiler_params=pltpu.CompilerParams(vmem_limit_bytes=8 * MIB),
        cost_estimate=pl.CostEstimate(
            flops=2 * OWN * D * WIDTH, bytes_accessed=MIB, transcendentals=0
        ),
        name="project_columns",
    )(heads, weights)


def dot(a, b):
    return jnp.dot(a, b, preferred_element_type=F32)


def dot_nt(a, b):
    return lax.dot_general(a, b, (((1,), (1,)), ((), ())), preferred_element_type=F32)


def split_two(x):
    high = x.astype(BF)
    return high, (x - high.astype(F32)).astype(BF)


def rotate_lanes(x, cosine, sine):
    lane = lax.broadcasted_iota(jnp.int32, x.shape, 1)
    other = jnp.where(lane % HD < HALF, pltpu.roll(x, WIDTH - HALF, 1), pltpu.roll(x, HALF, 1))
    return x * cosine + other * sine


def cross_kernel(
    w_ref, normed_ref, pick_ref, qcos_ref, qsin_ref, cos_ref, sin_ref, qpos_ref,
    out_ref, w_sc, table_sc, q_sc, s_sc, v_sc, ids_sc,
):
    for z in range(NZ):
        for y in range(NY):
            row = (z * NY + y) * 16
            for part in range(3):
                start = z * 64 + part * 16
                w_sc[row : row + 16, part * WIDTH : (part + 1) * WIDTH] = w_ref[
                    y, start : start + 16, :
                ]
    for y in range(NY):
        ids = w_ref[y, NZ * 64 :, :].astype(F32)
        for z in range(NZ):
            ids_sc[z, y * 4 : (y + 1) * 4] = ids[z * 4 : (z + 1) * 4]
    normed = normed_ref[...]
    table_sc[...] = dot(normed, w_sc[:, WIDTH:]).T.astype(BF)
    rows = dot(pick_ref[...], normed).astype(BF)
    query = dot(rows, w_sc[:, :WIDTH]) * (HD**-0.5)
    lane = lax.broadcasted_iota(jnp.int32, query.shape, 1)
    for step in range(STEPS):
        block = slice(step * OWN, (step + 1) * OWN)
        turned = rotate_lanes(query, qcos_ref[block], qsin_ref[block])
        q_sc[step, :OWN] = jnp.where(lane < HD, turned, 0.0).astype(BF)
        q_sc[step, OWN:] = jnp.where(lane < HD, 0.0, turned).astype(BF)
    token = lax.broadcasted_iota(jnp.int32, (VOCAB, 128), 0).astype(F32)

    def scores_of(step, top):
        hot = []
        ids = ids_sc[step]
        for r in range(16):
            hot.append(jnp.where(token == ids[r : r + 1, :], 1.0, 0.0).astype(BF))
        both = dot(table_sc[...], jnp.concatenate(hot, axis=1))
        v_sc[step] = both[WIDTH:].astype(BF)
        cosine, sine = cos_ref[...], sin_ref[...]
        pieces = []
        for head in range(2):
            first = both[head * HD : head * HD + HALF]
            second = both[head * HD + HALF : (head + 1) * HD]
            pieces.append(first * cosine - second * sine)
            pieces.append(second * cosine + first * sine)
        scores = dot(q_sc[step], jnp.concatenate(pieces, axis=0).astype(BF))
        kpos = step * KEYS + lax.broadcasted_iota(jnp.int32, scores.shape, 1)
        scores = jnp.where(kpos <= qpos_ref[:, :1], scores, -1e30)
        s_sc[step] = scores
        for i in range(KEYS // 128):
            top = jnp.maximum(top, scores[:, i * 128 : (i + 1) * 128])
        return top

    top = lax.fori_loop(0, STEPS, scores_of, jnp.full((2 * OWN, 128), -1e30, F32), unroll=8)
    most = jnp.max(top, axis=1, keepdims=True)

    def values_of(step, carry):
        total, acc = carry
        weight = jnp.exp(s_sc[step] - most)
        for i in range(KEYS // 128):
            total = total + weight[:, i * 128 : (i + 1) * 128]
        return total, acc + dot_nt(v_sc[step], weight.astype(BF))

    total, acc = lax.fori_loop(
        0, STEPS, values_of, (jnp.zeros((2 * OWN, 128), F32), jnp.zeros((WIDTH, 2 * OWN), F32)),
        unroll=4,
    )
    value = acc.T / jnp.sum(total, axis=1, keepdims=True)
    lane = lax.broadcasted_iota(jnp.int32, (OWN, WIDTH), 1)
    value = jnp.where(lane < HD, value[:OWN], value[OWN:]).astype(BF)
    for i in range(NLAT):
        out_ref[i] = value


def cross_attention(*operands):
    return pl.pallas_call(
        cross_kernel,
        out_shape=jax.ShapeDtypeStruct((NLAT, OWN, WIDTH), BF),
        scratch_shapes=[
            pltpu.VMEM((D, 3 * WIDTH), BF),
            pltpu.VMEM((2 * WIDTH, VOCAB), BF),
            pltpu.VMEM((STEPS, 2 * OWN, WIDTH), BF),
            pltpu.VMEM((STEPS, 2 * OWN, KEYS), F32),
            pltpu.VMEM((STEPS, WIDTH, KEYS), BF),
            pltpu.VMEM((NZ, 16, 128), F32),
        ],
        compiler_params=pltpu.CompilerParams(vmem_limit_bytes=32 * MIB),
        cost_estimate=pl.CostEstimate(
            flops=MIB, bytes_accessed=MIB, transcendentals=0
        ),
        name="cross_attention",
    )(*operands)


def out_weights(ref):
    columns = []
    for i in range(NLAT):
        rows = [ref[i, y, z] for z in range(NZ) for y in range(NY)]
        columns.append(jnp.concatenate(rows, axis=0))
    return jnp.concatenate(columns, axis=1)


def dense_kernel(first, *refs):
    lat_ref, parts_ref, state_ref, matrix_ref, gain_ref, qkv_ref, cos_ref, sin_ref = refs[:8]
    state_out, q_out, kv_out = refs[8:11]
    parts = jnp.concatenate([parts_ref[i % NC, i // NC] for i in range(NLAT)], axis=1)
    if first:
        token = lax.broadcasted_iota(jnp.int32, (VOCAB, BLOCK), 0)
        hot = jnp.where(token == state_ref[...], 1.0, 0.0).T.astype(BF)
        state = dot(hot, matrix_ref[...]) + parts.astype(F32)
        state_out[...] = state
    else:
        state = state_ref[...] + dot(parts, out_weights(matrix_ref))
        state_sc = refs[11]
        state_sc[...] = state
        own = pl.ds(pl.multiple_of(lat_ref[0] * WIDTH, WIDTH), WIDTH)
        state_out[...] = state_sc[:, own].astype(BF)
    scale = lax.rsqrt(jnp.mean(state * state, axis=1, keepdims=True) + 1e-06)
    normed = (state * scale * gain_ref[0 if first else 1, :][None]).astype(BF)
    cosine, sine = cos_ref[...], sin_ref[...]
    weights = [
        jnp.concatenate(
            [qkv_ref[y, z, i * 16 : (i + 1) * 16] for z in range(NZ) for y in range(NY)], axis=0
        )
        for i in range(3)
    ]
    product = dot(normed, jnp.concatenate(weights, axis=1))
    q_out[...] = rotate_lanes(product[:, :WIDTH], cosine, sine).astype(BF)
    k = rotate_lanes(product[:, WIDTH : 2 * WIDTH], cosine, sine).astype(BF)
    v = product[:, 2 * WIDTH :].astype(BF)
    for y in range(NY):
        kv_out[y, :, :WIDTH] = k
        kv_out[y, :, WIDTH:] = v


def dense(first, *operands):
    smem, vmem = (pl.BlockSpec(memory_space=m) for m in (pltpu.SMEM, pltpu.VMEM))
    return pl.pallas_call(
        functools.partial(dense_kernel, first),
        out_shape=(
            jax.ShapeDtypeStruct((BLOCK, D), F32)
            if first
            else jax.ShapeDtypeStruct((BLOCK, WIDTH), BF),
            jax.ShapeDtypeStruct((BLOCK, WIDTH), BF),
            jax.ShapeDtypeStruct((NY, BLOCK, 2 * WIDTH), BF),
        ),
        in_specs=[smem] + [vmem] * 7,
        scratch_shapes=[] if first else [pltpu.VMEM((BLOCK, D), F32)],
        compiler_params=pltpu.CompilerParams(vmem_limit_bytes=24 * MIB),
        cost_estimate=pl.CostEstimate(
            flops=2 * BLOCK * D * (D + 3 * WIDTH), bytes_accessed=8 * MIB, transcendentals=BLOCK
        ),
        name="dense",
    )(*operands)


def key_positions():
    column = lax.broadcasted_iota(jnp.int32, (1, L), 1)
    return (column % BLOCK) // PART * 128 + column // BLOCK * PART + column % PART


def attend(q, k, v, qpos, kpos):
    outs = []
    seen = kpos <= qpos
    for head in range(2):
        lanes = slice(head * HD, (head + 1) * HD)
        scores = dot_nt(q[:, lanes], k[:, lanes]) * (HD**-0.5)
        scores = jnp.where(seen, scores, -1e30)
        weight = jnp.exp(scores - jnp.max(scores, axis=1, keepdims=True))
        total = jnp.sum(weight, axis=1, keepdims=True)
        outs.append(dot(weight.astype(BF), v[:, lanes]) / total)
    return jnp.concatenate(outs, axis=1).astype(BF)


def attend_kernel(final, y_ref, q_ref, kv_ref, *refs):
    out_ref = refs[-1]
    row = lax.broadcasted_iota(jnp.int32, (BLOCK, 1), 0)
    qpos = row // PART * 128 + y_ref[0] * PART + row % PART
    kv = jnp.concatenate([kv_ref[i] for i in range(NY)], axis=0)
    out = attend(q_ref[...], kv[:, :WIDTH], kv[:, WIDTH:], qpos, key_positions())
    if final:
        state = refs[0][...]
        for y in range(NY):
            for i in range(NLAT):
                out_ref[y * NLAT + i, :PART] = out[i * PART : (i + 1) * PART]
                out_ref[y * NLAT + i, PART:] = state[i * PART : (i + 1) * PART]
    else:
        for i in range(NX):
            out_ref[i] = out


def attend_latents(final, *operands):
    shape = (NY * NLAT, 2 * PART, WIDTH) if final else (NX, BLOCK, WIDTH)
    smem, vmem = (pl.BlockSpec(memory_space=m) for m in (pltpu.SMEM, pltpu.VMEM))
    return pl.pallas_call(
        functools.partial(attend_kernel, final),
        out_shape=jax.ShapeDtypeStruct(shape, BF),
        in_specs=[smem] + [vmem] * (len(operands) - 1),
        compiler_params=pltpu.CompilerParams(vmem_limit_bytes=16 * MIB),
        cost_estimate=pl.CostEstimate(
            flops=8 * BLOCK * L * HD, bytes_accessed=2 * MIB, transcendentals=2 * BLOCK * L
        ),
        name="attend_latents",
    )(*operands)


def order_kernel(ref, out_ref):
    for i in range(NLAT):
        out_ref[:, i * WIDTH : (i + 1) * WIDTH] = jnp.concatenate(
            [ref[i, y, z] for z in range(NZ) for y in range(NY)], axis=0
        )


def order_weights(out_w):
    return pl.pallas_call(
        order_kernel,
        out_shape=jax.ShapeDtypeStruct((D, D), BF),
        compiler_params=pltpu.CompilerParams(vmem_limit_bytes=8 * MIB),
        name="order_weights",
    )(out_w)


def last_kernel(both_ref, out_w_ref, out_ref):
    heads, state = (
        jnp.concatenate(
            [
                jnp.concatenate(
                    [both_ref[y * NLAT + i, half * PART : (half + 1) * PART] for i in range(NLAT)],
                    axis=1,
                )
                for y in range(NY)
            ],
            axis=0,
        )
        for half in range(2)
    )
    out_ref[...] = state.astype(F32) + dot(heads, out_w_ref[...])


def last(both, out_w):
    return pl.pallas_call(
        last_kernel,
        out_shape=jax.ShapeDtypeStruct((128, D), F32),
        compiler_params=pltpu.CompilerParams(vmem_limit_bytes=16 * MIB),
        cost_estimate=pl.CostEstimate(
            flops=2 * 128 * D * D, bytes_accessed=4 * MIB, transcendentals=0
        ),
        name="last",
    )(both, out_w)


def head_angles(positions, inverse):
    angle = positions.astype(F32)[:, None] * inverse[None, :]
    cosine, sine = jnp.cos(angle), jnp.sin(angle)
    return (
        jnp.concatenate([cosine] * 4, axis=1),
        jnp.concatenate([-sine, sine, -sine, sine], axis=1),
    )


def body(token_ids, embed_table, input_gain, cross_qkv, cross_out, layer_gain, layer_qkv, layer_out):
    z, y = lax.axis_index("z"), lax.axis_index("y")
    lat = lax.axis_index(LAT)

    lat_index = jnp.full((1,), lat, jnp.int32)
    pack = pack_shards(
        lat_index, token_ids.reshape(4, 128), cross_qkv.reshape(48, WIDTH),
        layer_qkv.reshape(96, WIDTH), cross_out, layer_out.reshape(32, D),
    )
    by_z = lax.all_gather(pack, "z", axis=0)
    by_z, inverse, embed_table, input_gain = lax.optimization_barrier(
        (by_z, inverse_frequencies(), embed_table, input_gain)
    )
    now = jnp.concatenate(
        [by_z[:, :64].reshape(NZ * 64, WIDTH), by_z[:, 192:196].reshape(NZ * 4, WIDTH)], axis=0
    )
    by_zy = gather(now, "y", NY)

    latent = jnp.arange(OWN, dtype=jnp.int32) + (z // 2) * 128 + y * PART + (z % 2) * OWN
    offset = N - L + latent[None, :] - KEYS * jnp.arange(STEPS, dtype=jnp.int32)[:, None]
    qcos, qsin = head_angles(offset.reshape(STEPS * OWN), inverse)
    row = jnp.arange(BLOCK, dtype=jnp.int32)
    lpos = row // PART * 128 + y * PART + row % PART
    lcos, lsin = head_angles(lpos, inverse)
    fine = inverse[:, None] * jnp.arange(KEYS, dtype=F32)[None, :]
    tables = (qcos, qsin, jnp.cos(fine), jnp.sin(fine))
    wide = embed_table.astype(F32)
    normed = wide * lax.rsqrt(jnp.mean(wide * wide, axis=-1, keepdims=True) + 1e-06) * input_gain
    normed = normed.astype(BF)
    by_zy, rest_z, normed, tables, lcos, lsin = lax.optimization_barrier(
        (by_zy, by_z[:, 64:192], normed, tables, lcos, lsin)
    )
    rest_zy = lax.all_gather(rest_z, "y", axis=0)
    outs = [rest_zy[:, :, 64 * i + 48 : 64 * i + 64] for i in range(LAYERS)]
    qkv = [rest_zy[:, :, 64 * i : 64 * i + 48] for i in range(LAYERS)]
    latent_ids = by_zy[2:, NZ * 68 - 4 :].reshape(L).astype(jnp.int32)
    own_ids = lax.dynamic_slice_in_dim(latent_ids, latent[0], OWN, 0)
    pick = (own_ids[:, None] == jnp.arange(VOCAB, dtype=jnp.int32)[None, :]).astype(BF)
    block_ids = lax.dynamic_slice_in_dim(latent_ids.reshape(8, NY, PART), y, 1, 1).reshape(1, BLOCK)
    qpos = jnp.broadcast_to(
        (N - L + jnp.concatenate([latent, latent]))[:, None], (2 * OWN, 128)
    )
    heads = cross_attention(by_zy, normed, pick, *tables, qpos)

    heads = lax.all_to_all(heads, LAT, split_axis=0, concat_axis=0, tiled=True)
    added = project_columns(heads, by_zy)

    added = lax.all_to_all(added, "z", split_axis=0, concat_axis=0, tiled=True)
    added, outs, qkv, block_ids = lax.optimization_barrier((added, outs, qkv, block_ids))
    out_w = [lax.all_gather(w, LAT, axis=0) for w in outs]
    added = added.reshape(BLOCK, WIDTH)
    added = gather_lat(jnp.broadcast_to(added[None], (NX, BLOCK, WIDTH)))

    state, q, kv = dense(
        True, lat_index, added, block_ids, embed_table, layer_gain, qkv[0], lcos, lsin
    )
    kv = lax.all_to_all(kv, "y", split_axis=0, concat_axis=0, tiled=True)
    y_index = jnp.full((1,), y, jnp.int32)
    heads = attend_latents(False, y_index, q, kv)
    heads, layer_w = lax.optimization_barrier((heads, out_w[0]))
    heads = gather_lat(heads)
    state, q, kv = dense(
        False, lat_index, heads, state, layer_w, layer_gain, qkv[1], lcos, lsin
    )
    kv = lax.all_to_all(kv, "y", split_axis=0, concat_axis=0, tiled=True)
    both = attend_latents(True, y_index, q, kv, state)
    both = lax.all_to_all(both, ("y", "x", "c"), split_axis=0, concat_axis=0, tiled=True)
    return last(both, order_weights(out_w[1]))


def solution(mesh):
    grid = Mesh(np.asarray(mesh.devices).reshape(NZ, NY, NX, NC), ("z", "y", "x", "c"))
    return jax.shard_map(
        body,
        mesh=grid,
        in_specs=(
            P(CTX),
            P(),
            P(),
            P(None, CTX, LAT),
            P(CTX, None),
            P(),
            P(None, None, CTX, LAT),
            P(None, CTX, None),
        ),
        out_specs=P(LAT, None),
        check_vma=False,
    )
```

```python
import functools

import jax
import jax.numpy as jnp
import numpy as np
from jax import lax
from jax.experimental import pallas as pl
from jax.experimental.pallas import tpu as pltpu
from jax.sharding import Mesh
from jax.sharding import PartitionSpec as P

D = 1024
HD = 64
HALF = 32
NZ, NY, NX, NC = 16, 4, 4, 2
NLAT = NX * NC
N = 32768
L = 1024
VOCAB = 256
WIDTH = 128
OWN = 16
LAYERS = 2
PART = 32
BLOCK = 256
KEYS = 2048
STEPS = N // KEYS
LAT = ("x", "c")
CTX = ("z", "y")
BF = jnp.bfloat16
F32 = jnp.float32
MIB = 1 << 20


def inverse_frequencies():
    return 10000.0 ** (-2.0 * jnp.arange(HALF, dtype=F32) / (2 * HALF))


def gather_lat(copies):
    by_x = lax.all_to_all(copies, "x", split_axis=0, concat_axis=0, tiled=True)
    return lax.all_gather(by_x, "c", axis=0)


def pack_kernel(lat_ref, *refs):
    ids_ref, cross_ref, layer_ref, cross_out_ref, layer_out_ref = refs[5:10]
    out_ref, sem = refs[10:]
    copies = [pltpu.make_async_copy(refs[i], refs[i + 5], sem.at[i]) for i in range(5)]
    for copy in copies:
        copy.start()
    for copy in copies:
        copy.wait()
    own = pl.ds(pl.multiple_of(lat_ref[0] * WIDTH, WIDTH), WIDTH)
    out_ref[0:48] = cross_ref[...]
    out_ref[48:64] = cross_out_ref[:, own]
    ids = ids_ref[...].astype(F32)
    out_ref[192:200] = jnp.concatenate([ids, jnp.zeros((4, WIDTH), F32)], axis=0).astype(BF)
    for layer in range(LAYERS):
        start = 64 + layer * 64
        out_ref[start : start + 48] = layer_ref[layer * 48 : (layer + 1) * 48]
        out_ref[start + 48 : start + 64] = layer_out_ref[layer * 16 : (layer + 1) * 16, own]


def pack_shards(lat_index, *operands):
    def kernel(lat_ref, *refs):
        pack_kernel(lat_ref, *refs[:5], *refs[6:11], refs[5], refs[11])

    return pl.pallas_call(
        kernel,
        out_shape=jax.ShapeDtypeStruct((200, WIDTH), BF),
        in_specs=[pl.BlockSpec(memory_space=pltpu.SMEM)] + [pl.BlockSpec(memory_space=pl.ANY)] * 5,
        out_specs=pl.BlockSpec(memory_space=pltpu.VMEM),
        scratch_shapes=[pltpu.VMEM(a.shape, a.dtype) for a in operands]
        + [pltpu.SemaphoreType.DMA((5,))],
        compiler_params=pltpu.CompilerParams(vmem_limit_bytes=58 * MIB),
        name="pack_shards",
    )(lat_index, *operands)


def split_kernel(ref, now_ref, rest_ref):
    ids = [ref[z, 192:200, :].astype(F32)[:4] for z in range(NZ)]
    ids = jnp.concatenate(ids, axis=0).astype(BF)
    for y in range(NY):
        for z in range(NZ):
            now_ref[y, z * 64 : (z + 1) * 64] = ref[z, :64]
        now_ref[y, NZ * 64 :] = ids
    for z in range(NZ):
        rest_ref[z] = ref[z, 64:192]


def split_round(by_z):
    return pl.pallas_call(
        split_kernel,
        out_shape=(
            jax.ShapeDtypeStruct((NY, NZ * 68, WIDTH), BF),
            jax.ShapeDtypeStruct((NZ, 128, WIDTH), BF),
        ),
        compiler_params=pltpu.CompilerParams(vmem_limit_bytes=8 * MIB),
        name="split_round",
    )(by_z)


def project_kernel(heads_ref, w_ref, out_ref):
    heads = jnp.concatenate([heads_ref[i] for i in range(NLAT)], axis=1)
    rows = [w_ref[y, z * 64 + 48 : z * 64 + 64] for z in range(NZ) for y in range(NY)]
    out = dot(heads, jnp.concatenate(rows, axis=0)).astype(BF)
    for z in range(NZ):
        out_ref[z] = out


def project_columns(heads, weights):
    return pl.pallas_call(
        project_kernel,
        out_shape=jax.ShapeDtypeStruct((NZ, OWN, WIDTH), BF),
        compiler_params=pltpu.CompilerParams(vmem_limit_bytes=8 * MIB),
        cost_estimate=pl.CostEstimate(
            flops=2 * OWN * D * WIDTH, bytes_accessed=MIB, transcendentals=0
        ),
        name="project_columns",
    )(heads, weights)


def dot(a, b):
    return jnp.dot(a, b, preferred_element_type=F32)


def dot_nt(a, b):
    return lax.dot_general(a, b, (((1,), (1,)), ((), ())), preferred_element_type=F32)


def split_two(x):
    high = x.astype(BF)
    return high, (x - high.astype(F32)).astype(BF)


def rotate_lanes(x, cosine, sine):
    lane = lax.broadcasted_iota(jnp.int32, x.shape, 1)
    other = jnp.where(lane % HD < HALF, pltpu.roll(x, WIDTH - HALF, 1), pltpu.roll(x, HALF, 1))
    return x * cosine + other * sine


def cross_kernel(
    w_ref, normed_ref, pick_ref, qcos_ref, qsin_ref, cos_ref, sin_ref, qpos_ref,
    out_ref, w_sc, table_sc, q_sc, s_sc, v_sc, ids_sc,
):
    for z in range(NZ):
        for y in range(NY):
            row = (z * NY + y) * 16
            for part in range(3):
                start = z * 64 + part * 16
                w_sc[row : row + 16, part * WIDTH : (part + 1) * WIDTH] = w_ref[
                    y, start : start + 16, :
                ]
    for y in range(NY):
        ids = w_ref[y, NZ * 64 :, :].astype(F32)
        for z in range(NZ):
            ids_sc[z, y * 4 : (y + 1) * 4] = ids[z * 4 : (z + 1) * 4]
    normed = normed_ref[...]
    table_sc[...] = dot(normed, w_sc[:, WIDTH:]).T.astype(BF)
    rows = dot(pick_ref[...], normed).astype(BF)
    query = dot(rows, w_sc[:, :WIDTH]) * (HD**-0.5)
    lane = lax.broadcasted_iota(jnp.int32, query.shape, 1)
    for step in range(STEPS):
        block = slice(step * OWN, (step + 1) * OWN)
        turned = rotate_lanes(query, qcos_ref[block], qsin_ref[block])
        q_sc[step, :OWN] = jnp.where(lane < HD, turned, 0.0).astype(BF)
        q_sc[step, OWN:] = jnp.where(lane < HD, 0.0, turned).astype(BF)
    token = lax.broadcasted_iota(jnp.int32, (VOCAB, 128), 0).astype(F32)

    def scores_of(step, top):
        hot = []
        ids = ids_sc[step]
        for r in range(16):
            hot.append(jnp.where(token == ids[r : r + 1, :], 1.0, 0.0).astype(BF))
        both = dot(table_sc[...], jnp.concatenate(hot, axis=1))
        v_sc[step] = both[WIDTH:].astype(BF)
        cosine, sine = cos_ref[...], sin_ref[...]
        pieces = []
        for head in range(2):
            first = both[head * HD : head * HD + HALF]
            second = both[head * HD + HALF : (head + 1) * HD]
            pieces.append(first * cosine - second * sine)
            pieces.append(second * cosine + first * sine)
        scores = dot(q_sc[step], jnp.concatenate(pieces, axis=0).astype(BF))
        kpos = step * KEYS + lax.broadcasted_iota(jnp.int32, scores.shape, 1)
        scores = jnp.where(kpos <= qpos_ref[:, :1], scores, -1e30)
        s_sc[step] = scores
        for i in range(KEYS // 128):
            top = jnp.maximum(top, scores[:, i * 128 : (i + 1) * 128])
        return top

    top = lax.fori_loop(0, STEPS, scores_of, jnp.full((2 * OWN, 128), -1e30, F32), unroll=8)
    most = jnp.max(top, axis=1, keepdims=True)

    def values_of(step, carry):
        total, acc = carry
        weight = jnp.exp(s_sc[step] - most)
        for i in range(KEYS // 128):
            total = total + weight[:, i * 128 : (i + 1) * 128]
        return total, acc + dot_nt(v_sc[step], weight.astype(BF))

    total, acc = lax.fori_loop(
        0, STEPS, values_of, (jnp.zeros((2 * OWN, 128), F32), jnp.zeros((WIDTH, 2 * OWN), F32)),
        unroll=4,
    )
    value = acc.T / jnp.sum(total, axis=1, keepdims=True)
    lane = lax.broadcasted_iota(jnp.int32, (OWN, WIDTH), 1)
    value = jnp.where(lane < HD, value[:OWN], value[OWN:]).astype(BF)
    for i in range(NLAT):
        out_ref[i] = value


def cross_attention(*operands):
    return pl.pallas_call(
        cross_kernel,
        out_shape=jax.ShapeDtypeStruct((NLAT, OWN, WIDTH), BF),
        scratch_shapes=[
            pltpu.VMEM((D, 3 * WIDTH), BF),
            pltpu.VMEM((2 * WIDTH, VOCAB), BF),
            pltpu.VMEM((STEPS, 2 * OWN, WIDTH), BF),
            pltpu.VMEM((STEPS, 2 * OWN, KEYS), F32),
            pltpu.VMEM((STEPS, WIDTH, KEYS), BF),
            pltpu.VMEM((NZ, 16, 128), F32),
        ],
        compiler_params=pltpu.CompilerParams(vmem_limit_bytes=20 * MIB),
        cost_estimate=pl.CostEstimate(
            flops=MIB, bytes_accessed=MIB, transcendentals=0
        ),
        name="cross_attention",
    )(*operands)


def out_weights(ref):
    columns = []
    for i in range(NLAT):
        rows = [ref[i, y, z] for z in range(NZ) for y in range(NY)]
        columns.append(jnp.concatenate(rows, axis=0))
    return jnp.concatenate(columns, axis=1)


def dense_kernel(first, *refs):
    lat_ref, parts_ref, state_ref, matrix_ref, gain_ref, qkv_ref, cos_ref, sin_ref = refs[:8]
    state_out, q_out, kv_out = refs[8:11]
    parts = jnp.concatenate([parts_ref[i % NC, i // NC] for i in range(NLAT)], axis=1)
    if first:
        token = lax.broadcasted_iota(jnp.int32, (VOCAB, BLOCK), 0)
        hot = jnp.where(token == state_ref[...], 1.0, 0.0).T.astype(BF)
        state = dot(hot, matrix_ref[...]) + parts.astype(F32)
        state_out[...] = state
    else:
        state = state_ref[...] + dot(parts, out_weights(matrix_ref))
        state_sc = refs[11]
        state_sc[...] = state
        own = pl.ds(pl.multiple_of(lat_ref[0] * WIDTH, WIDTH), WIDTH)
        state_out[...] = state_sc[:, own].astype(BF)
    scale = lax.rsqrt(jnp.mean(state * state, axis=1, keepdims=True) + 1e-06)
    normed = (state * scale * gain_ref[0 if first else 1, :][None]).astype(BF)
    cosine, sine = cos_ref[...], sin_ref[...]
    weights = [
        jnp.concatenate(
            [qkv_ref[y, z, i * 16 : (i + 1) * 16] for z in range(NZ) for y in range(NY)], axis=0
        )
        for i in range(3)
    ]
    product = dot(normed, jnp.concatenate(weights, axis=1))
    q_out[...] = rotate_lanes(product[:, :WIDTH], cosine, sine).astype(BF)
    k = rotate_lanes(product[:, WIDTH : 2 * WIDTH], cosine, sine).astype(BF)
    v = product[:, 2 * WIDTH :].astype(BF)
    for y in range(NY):
        kv_out[y, :, :WIDTH] = k
        kv_out[y, :, WIDTH:] = v


def dense(first, *operands):
    smem, vmem = (pl.BlockSpec(memory_space=m) for m in (pltpu.SMEM, pltpu.VMEM))
    return pl.pallas_call(
        functools.partial(dense_kernel, first),
        out_shape=(
            jax.ShapeDtypeStruct((BLOCK, D), F32)
            if first
            else jax.ShapeDtypeStruct((BLOCK, WIDTH), BF),
            jax.ShapeDtypeStruct((BLOCK, WIDTH), BF),
            jax.ShapeDtypeStruct((NY, BLOCK, 2 * WIDTH), BF),
        ),
        in_specs=[smem] + [vmem] * 7,
        scratch_shapes=[] if first else [pltpu.VMEM((BLOCK, D), F32)],
        compiler_params=pltpu.CompilerParams(vmem_limit_bytes=16 * MIB),
        cost_estimate=pl.CostEstimate(
            flops=2 * BLOCK * D * (D + 3 * WIDTH), bytes_accessed=8 * MIB, transcendentals=BLOCK
        ),
        name="dense",
    )(*operands)


def key_positions():
    column = lax.broadcasted_iota(jnp.int32, (1, L), 1)
    return (column % BLOCK) // PART * 128 + column // BLOCK * PART + column % PART


def attend(q, k, v, qpos, kpos):
    outs = []
    seen = kpos <= qpos
    for head in range(2):
        lanes = slice(head * HD, (head + 1) * HD)
        scores = dot_nt(q[:, lanes], k[:, lanes]) * (HD**-0.5)
        scores = jnp.where(seen, scores, -1e30)
        weight = jnp.exp(scores - jnp.max(scores, axis=1, keepdims=True))
        total = jnp.sum(weight, axis=1, keepdims=True)
        outs.append(dot(weight.astype(BF), v[:, lanes]) / total)
    return jnp.concatenate(outs, axis=1).astype(BF)


def attend_kernel(final, y_ref, q_ref, kv_ref, *refs):
    out_ref = refs[-1]
    row = lax.broadcasted_iota(jnp.int32, (BLOCK, 1), 0)
    qpos = row // PART * 128 + y_ref[0] * PART + row % PART
    kv = jnp.concatenate([kv_ref[i] for i in range(NY)], axis=0)
    out = attend(q_ref[...], kv[:, :WIDTH], kv[:, WIDTH:], qpos, key_positions())
    if final:
        state = refs[0][...]
        for y in range(NY):
            for i in range(NLAT):
                out_ref[y * NLAT + i, :PART] = out[i * PART : (i + 1) * PART]
                out_ref[y * NLAT + i, PART:] = state[i * PART : (i + 1) * PART]
    else:
        for i in range(NX):
            out_ref[i] = out


def attend_latents(final, *operands):
    shape = (NY * NLAT, 2 * PART, WIDTH) if final else (NX, BLOCK, WIDTH)
    smem, vmem = (pl.BlockSpec(memory_space=m) for m in (pltpu.SMEM, pltpu.VMEM))
    return pl.pallas_call(
        functools.partial(attend_kernel, final),
        out_shape=jax.ShapeDtypeStruct(shape, BF),
        in_specs=[smem] + [vmem] * (len(operands) - 1),
        compiler_params=pltpu.CompilerParams(vmem_limit_bytes=12 * MIB),
        cost_estimate=pl.CostEstimate(
            flops=8 * BLOCK * L * HD, bytes_accessed=2 * MIB, transcendentals=2 * BLOCK * L
        ),
        name="attend_latents",
    )(*operands)


def order_kernel(ref, out_ref):
    for i in range(NLAT):
        out_ref[:, i * WIDTH : (i + 1) * WIDTH] = jnp.concatenate(
            [ref[i, y, z] for z in range(NZ) for y in range(NY)], axis=0
        )


def order_weights(out_w):
    return pl.pallas_call(
        order_kernel,
        out_shape=jax.ShapeDtypeStruct((D, D), BF),
        compiler_params=pltpu.CompilerParams(vmem_limit_bytes=8 * MIB),
        name="order_weights",
    )(out_w)


def last_kernel(both_ref, out_w_ref, out_ref):
    heads, state = (
        jnp.concatenate(
            [
                jnp.concatenate(
                    [both_ref[y * NLAT + i, half * PART : (half + 1) * PART] for i in range(NLAT)],
                    axis=1,
                )
                for y in range(NY)
            ],
            axis=0,
        )
        for half in range(2)
    )
    out_ref[...] = state.astype(F32) + dot(heads, out_w_ref[...])


def last(both, out_w):
    return pl.pallas_call(
        last_kernel,
        out_shape=jax.ShapeDtypeStruct((128, D), F32),
        compiler_params=pltpu.CompilerParams(vmem_limit_bytes=16 * MIB),
        cost_estimate=pl.CostEstimate(
            flops=2 * 128 * D * D, bytes_accessed=4 * MIB, transcendentals=0
        ),
        name="last",
    )(both, out_w)


def head_angles(positions, inverse):
    angle = positions.astype(F32)[:, None] * inverse[None, :]
    cosine, sine = jnp.cos(angle), jnp.sin(angle)
    return (
        jnp.concatenate([cosine] * 4, axis=1),
        jnp.concatenate([-sine, sine, -sine, sine], axis=1),
    )


def body(token_ids, embed_table, input_gain, cross_qkv, cross_out, layer_gain, layer_qkv, layer_out):
    z, y = lax.axis_index("z"), lax.axis_index("y")
    lat = lax.axis_index(LAT)

    lat_index = jnp.full((1,), lat, jnp.int32)
    pack = pack_shards(
        lat_index, token_ids.reshape(4, 128), cross_qkv.reshape(48, WIDTH),
        layer_qkv.reshape(96, WIDTH), cross_out, layer_out.reshape(32, D),
    )
    by_z = lax.all_gather(pack, "z", axis=0)
    by_z, inverse, embed_table, input_gain = lax.optimization_barrier(
        (by_z, inverse_frequencies(), embed_table, input_gain)
    )
    now, rest_z = split_round(by_z)
    by_zy = lax.all_to_all(now, "y", split_axis=0, concat_axis=0, tiled=True)

    latent = jnp.arange(OWN, dtype=jnp.int32) + (z // 2) * 128 + y * PART + (z % 2) * OWN
    offset = N - L + latent[None, :] - KEYS * jnp.arange(STEPS, dtype=jnp.int32)[:, None]
    qcos, qsin = head_angles(offset.reshape(STEPS * OWN), inverse)
    row = jnp.arange(BLOCK, dtype=jnp.int32)
    lpos = row // PART * 128 + y * PART + row % PART
    lcos, lsin = head_angles(lpos, inverse)
    fine = inverse[:, None] * jnp.arange(KEYS, dtype=F32)[None, :]
    tables = (qcos, qsin, jnp.cos(fine), jnp.sin(fine))
    wide = embed_table.astype(F32)
    normed = wide * lax.rsqrt(jnp.mean(wide * wide, axis=-1, keepdims=True) + 1e-06) * input_gain
    normed = normed.astype(BF)
    by_zy, rest_z, normed, tables, lcos, lsin = lax.optimization_barrier(
        (by_zy, rest_z, normed, tables, lcos, lsin)
    )
    rest_zy = lax.all_gather(rest_z, "y", axis=0)
    outs = [rest_zy[:, :, 64 * i + 48 : 64 * i + 64] for i in range(LAYERS)]
    qkv = [rest_zy[:, :, 64 * i : 64 * i + 48] for i in range(LAYERS)]
    latent_ids = by_zy[2:, NZ * 68 - 4 :].reshape(L).astype(jnp.int32)
    own_ids = lax.dynamic_slice_in_dim(latent_ids, latent[0], OWN, 0)
    pick = (own_ids[:, None] == jnp.arange(VOCAB, dtype=jnp.int32)[None, :]).astype(BF)
    block_ids = lax.dynamic_slice_in_dim(latent_ids.reshape(8, NY, PART), y, 1, 1).reshape(1, BLOCK)
    qpos = jnp.broadcast_to(
        (N - L + jnp.concatenate([latent, latent]))[:, None], (2 * OWN, 128)
    )
    heads = cross_attention(by_zy, normed, pick, *tables, qpos)

    heads = lax.all_to_all(heads, LAT, split_axis=0, concat_axis=0, tiled=True)
    added = project_columns(heads, by_zy)

    added = lax.all_to_all(added, "z", split_axis=0, concat_axis=0, tiled=True)
    added, outs, qkv, block_ids = lax.optimization_barrier((added, outs, qkv, block_ids))
    out_w = [lax.all_gather(w, LAT, axis=0) for w in outs]
    added = added.reshape(BLOCK, WIDTH)
    added = gather_lat(jnp.broadcast_to(added[None], (NX, BLOCK, WIDTH)))

    state, q, kv = dense(
        True, lat_index, added, block_ids, embed_table, layer_gain, qkv[0], lcos, lsin
    )
    kv = lax.all_to_all(kv, "y", split_axis=0, concat_axis=0, tiled=True)
    y_index = jnp.full((1,), y, jnp.int32)
    heads = attend_latents(False, y_index, q, kv)
    heads, layer_w = lax.optimization_barrier((heads, out_w[0]))
    heads = gather_lat(heads)
    state, q, kv = dense(
        False, lat_index, heads, state, layer_w, layer_gain, qkv[1], lcos, lsin
    )
    kv = lax.all_to_all(kv, "y", split_axis=0, concat_axis=0, tiled=True)
    both = attend_latents(True, y_index, q, kv, state)
    both = lax.all_to_all(both, ("y", "x", "c"), split_axis=0, concat_axis=0, tiled=True)
    return last(both, order_weights(out_w[1]))


def solution(mesh):
    grid = Mesh(np.asarray(mesh.devices).reshape(NZ, NY, NX, NC), ("z", "y", "x", "c"))
    return jax.shard_map(
        body,
        mesh=grid,
        in_specs=(
            P(CTX),
            P(),
            P(),
            P(None, CTX, LAT),
            P(CTX, None),
            P(),
            P(None, None, CTX, LAT),
            P(None, CTX, None),
        ),
        out_specs=P(LAT, None),
        check_vma=False,
    )
```

```python
import functools

import jax
import jax.numpy as jnp
import numpy as np
from jax import lax
from jax.experimental import pallas as pl
from jax.experimental.pallas import tpu as pltpu
from jax.sharding import Mesh
from jax.sharding import PartitionSpec as P

D = 1024
HD = 64
HALF = 32
NZ, NY, NX, NC = 16, 4, 4, 2
NLAT = NX * NC
N = 32768
L = 1024
VOCAB = 256
WIDTH = 128
OWN = 16
LAYERS = 2
PART = 32
BLOCK = 256
KEYS = 2048
STEPS = N // KEYS
LAT = ("x", "c")
CTX = ("z", "y")
BF = jnp.bfloat16
F32 = jnp.float32
MIB = 1 << 20


def inverse_frequencies():
    return 10000.0 ** (-2.0 * jnp.arange(HALF, dtype=F32) / (2 * HALF))


def gather_lat(copies):
    by_x = lax.all_to_all(copies, "x", split_axis=0, concat_axis=0, tiled=True)
    return lax.all_gather(by_x, "c", axis=0)


def pack_kernel(lat_ref, *refs):
    ids_ref, cross_ref, layer_ref, cross_out_ref, layer_out_ref = refs[5:10]
    out_ref, sem = refs[10:]
    copies = [pltpu.make_async_copy(refs[i], refs[i + 5], sem.at[i]) for i in range(5)]
    for copy in copies:
        copy.start()
    for copy in copies:
        copy.wait()
    own = pl.ds(pl.multiple_of(lat_ref[0] * WIDTH, WIDTH), WIDTH)
    out_ref[0:48] = cross_ref[...]
    out_ref[48:64] = cross_out_ref[:, own]
    ids = ids_ref[...].astype(F32)
    out_ref[192:200] = jnp.concatenate([ids, jnp.zeros((4, WIDTH), F32)], axis=0).astype(BF)
    for layer in range(LAYERS):
        start = 64 + layer * 64
        out_ref[start : start + 48] = layer_ref[layer * 48 : (layer + 1) * 48]
        out_ref[start + 48 : start + 64] = layer_out_ref[layer * 16 : (layer + 1) * 16, own]


def pack_shards(lat_index, *operands):
    def kernel(lat_ref, *refs):
        pack_kernel(lat_ref, *refs[:5], *refs[6:11], refs[5], refs[11])

    return pl.pallas_call(
        kernel,
        out_shape=jax.ShapeDtypeStruct((200, WIDTH), BF),
        in_specs=[pl.BlockSpec(memory_space=pltpu.SMEM)] + [pl.BlockSpec(memory_space=pl.ANY)] * 5,
        out_specs=pl.BlockSpec(memory_space=pltpu.VMEM),
        scratch_shapes=[pltpu.VMEM(a.shape, a.dtype) for a in operands]
        + [pltpu.SemaphoreType.DMA((5,))],
        compiler_params=pltpu.CompilerParams(vmem_limit_bytes=58 * MIB),
        name="pack_shards",
    )(lat_index, *operands)


def split_kernel(ref, now_ref, rest_ref):
    ids = [ref[z, 192:200, :].astype(F32)[:4] for z in range(NZ)]
    ids = jnp.concatenate(ids, axis=0).astype(BF)
    for y in range(NY):
        for z in range(NZ):
            now_ref[y, z * 64 : (z + 1) * 64] = ref[z, :64]
        now_ref[y, NZ * 64 :] = ids
    for z in range(NZ):
        rest_ref[z] = ref[z, 64:192]


def split_round(by_z):
    return pl.pallas_call(
        split_kernel,
        out_shape=(
            jax.ShapeDtypeStruct((NY, NZ * 68, WIDTH), BF),
            jax.ShapeDtypeStruct((NZ, 128, WIDTH), BF),
        ),
        compiler_params=pltpu.CompilerParams(vmem_limit_bytes=8 * MIB),
        name="split_round",
    )(by_z)


def project_kernel(heads_ref, w_ref, out_ref):
    heads = jnp.concatenate([heads_ref[i] for i in range(NLAT)], axis=1)
    rows = [w_ref[y, z * 64 + 48 : z * 64 + 64] for z in range(NZ) for y in range(NY)]
    out = dot(heads, jnp.concatenate(rows, axis=0)).astype(BF)
    for z in range(NZ):
        out_ref[z] = out


def project_columns(heads, weights):
    return pl.pallas_call(
        project_kernel,
        out_shape=jax.ShapeDtypeStruct((NZ, OWN, WIDTH), BF),
        compiler_params=pltpu.CompilerParams(vmem_limit_bytes=8 * MIB),
        cost_estimate=pl.CostEstimate(
            flops=2 * OWN * D * WIDTH, bytes_accessed=MIB, transcendentals=0
        ),
        name="project_columns",
    )(heads, weights)


def dot(a, b):
    return jnp.dot(a, b, preferred_element_type=F32)


def dot_nt(a, b):
    return lax.dot_general(a, b, (((1,), (1,)), ((), ())), preferred_element_type=F32)


def split_two(x):
    high = x.astype(BF)
    return high, (x - high.astype(F32)).astype(BF)


def rotate_lanes(x, cosine, sine):
    lane = lax.broadcasted_iota(jnp.int32, x.shape, 1)
    other = jnp.where(lane % HD < HALF, pltpu.roll(x, WIDTH - HALF, 1), pltpu.roll(x, HALF, 1))
    return x * cosine + other * sine


def cross_kernel(
    w_ref, normed_ref, pick_ref, qcos_ref, qsin_ref, cos_ref, sin_ref, qpos_ref,
    out_ref, w_sc, table_sc, q_sc, s_sc, v_sc, ids_sc,
):
    for z in range(NZ):
        for y in range(NY):
            row = (z * NY + y) * 16
            for part in range(3):
                start = z * 64 + part * 16
                w_sc[row : row + 16, part * WIDTH : (part + 1) * WIDTH] = w_ref[
                    y, start : start + 16, :
                ]
    for y in range(NY):
        ids = w_ref[y, NZ * 64 :, :].astype(F32)
        for z in range(NZ):
            ids_sc[z, y * 4 : (y + 1) * 4] = ids[z * 4 : (z + 1) * 4]
    normed = normed_ref[...]
    table_sc[...] = dot(normed, w_sc[:, WIDTH:]).T.astype(BF)
    rows = dot(pick_ref[...], normed).astype(BF)
    query = dot(rows, w_sc[:, :WIDTH]) * (HD**-0.5)
    lane = lax.broadcasted_iota(jnp.int32, query.shape, 1)
    for step in range(STEPS):
        block = slice(step * OWN, (step + 1) * OWN)
        turned = rotate_lanes(query, qcos_ref[block], qsin_ref[block])
        q_sc[step, :OWN] = jnp.where(lane < HD, turned, 0.0).astype(BF)
        q_sc[step, OWN:] = jnp.where(lane < HD, 0.0, turned).astype(BF)
    token = lax.broadcasted_iota(jnp.int32, (VOCAB, 128), 0).astype(F32)

    def scores_of(step, top):
        hot = []
        ids = ids_sc[step]
        for r in range(16):
            hot.append(jnp.where(token == ids[r : r + 1, :], 1.0, 0.0).astype(BF))
        both = dot(table_sc[...], jnp.concatenate(hot, axis=1))
        v_sc[step] = both[WIDTH:].astype(BF)
        cosine, sine = cos_ref[...], sin_ref[...]
        pieces = []
        for head in range(2):
            first = both[head * HD : head * HD + HALF]
            second = both[head * HD + HALF : (head + 1) * HD]
            pieces.append(first * cosine - second * sine)
            pieces.append(second * cosine + first * sine)
        scores = dot(q_sc[step], jnp.concatenate(pieces, axis=0).astype(BF))
        kpos = step * KEYS + lax.broadcasted_iota(jnp.int32, scores.shape, 1)
        scores = jnp.where(kpos <= qpos_ref[:, :1], scores, -1e30)
        s_sc[step] = scores
        for i in range(KEYS // 128):
            top = jnp.maximum(top, scores[:, i * 128 : (i + 1) * 128])
        return top

    top = lax.fori_loop(0, STEPS, scores_of, jnp.full((2 * OWN, 128), -1e30, F32), unroll=8)
    most = jnp.max(top, axis=1, keepdims=True)

    def values_of(step, carry):
        total, acc = carry
        weight = jnp.exp(s_sc[step] - most)
        for i in range(KEYS // 128):
            total = total + weight[:, i * 128 : (i + 1) * 128]
        return total, acc + dot_nt(v_sc[step], weight.astype(BF))

    total, acc = lax.fori_loop(
        0, STEPS, values_of, (jnp.zeros((2 * OWN, 128), F32), jnp.zeros((WIDTH, 2 * OWN), F32)),
        unroll=4,
    )
    value = acc.T / jnp.sum(total, axis=1, keepdims=True)
    lane = lax.broadcasted_iota(jnp.int32, (OWN, WIDTH), 1)
    value = jnp.where(lane < HD, value[:OWN], value[OWN:]).astype(BF)
    for i in range(NLAT):
        out_ref[i] = value


def cross_attention(*operands):
    return pl.pallas_call(
        cross_kernel,
        out_shape=jax.ShapeDtypeStruct((NLAT, OWN, WIDTH), BF),
        scratch_shapes=[
            pltpu.VMEM((D, 3 * WIDTH), BF),
            pltpu.VMEM((2 * WIDTH, VOCAB), BF),
            pltpu.VMEM((STEPS, 2 * OWN, WIDTH), BF),
            pltpu.VMEM((STEPS, 2 * OWN, KEYS), F32),
            pltpu.VMEM((STEPS, WIDTH, KEYS), BF),
            pltpu.VMEM((NZ, 16, 128), F32),
        ],
        compiler_params=pltpu.CompilerParams(vmem_limit_bytes=20 * MIB),
        cost_estimate=pl.CostEstimate(
            flops=MIB, bytes_accessed=MIB, transcendentals=0
        ),
        name="cross_attention",
    )(*operands)


def out_weights(ref):
    columns = []
    for i in range(NLAT):
        rows = [ref[i, y, z] for z in range(NZ) for y in range(NY)]
        columns.append(jnp.concatenate(rows, axis=0))
    return jnp.concatenate(columns, axis=1)


def dense_kernel(first, *refs):
    lat_ref, parts_ref, state_ref, matrix_ref, gain_ref, qkv_ref, cos_ref, sin_ref = refs[:8]
    state_out, q_out, kv_out = refs[8:11]
    parts = jnp.concatenate([parts_ref[i % NC, i // NC] for i in range(NLAT)], axis=1)
    if first:
        token = lax.broadcasted_iota(jnp.int32, (VOCAB, BLOCK), 0)
        hot = jnp.where(token == state_ref[...], 1.0, 0.0).T.astype(BF)
        state = dot(hot, matrix_ref[...]) + parts.astype(F32)
        state_out[...] = state
    else:
        state = state_ref[...] + dot(parts, out_weights(matrix_ref))
        state_sc = refs[11]
        state_sc[...] = state
        own = pl.ds(pl.multiple_of(lat_ref[0] * WIDTH, WIDTH), WIDTH)
        state_out[...] = state_sc[:, own].astype(BF)
    scale = lax.rsqrt(jnp.mean(state * state, axis=1, keepdims=True) + 1e-06)
    normed = (state * scale * gain_ref[0 if first else 1, :][None]).astype(BF)
    cosine, sine = cos_ref[...], sin_ref[...]
    weights = [
        jnp.concatenate(
            [qkv_ref[y, z, i * 16 : (i + 1) * 16] for z in range(NZ) for y in range(NY)], axis=0
        )
        for i in range(3)
    ]
    product = dot(normed, jnp.concatenate(weights, axis=1))
    q_out[...] = rotate_lanes(product[:, :WIDTH], cosine, sine).astype(BF)
    k = rotate_lanes(product[:, WIDTH : 2 * WIDTH], cosine, sine).astype(BF)
    v = product[:, 2 * WIDTH :].astype(BF)
    for y in range(NY):
        kv_out[y, :, :WIDTH] = k
        kv_out[y, :, WIDTH:] = v


def dense(first, *operands):
    smem, vmem = (pl.BlockSpec(memory_space=m) for m in (pltpu.SMEM, pltpu.VMEM))
    return pl.pallas_call(
        functools.partial(dense_kernel, first),
        out_shape=(
            jax.ShapeDtypeStruct((BLOCK, D), F32)
            if first
            else jax.ShapeDtypeStruct((BLOCK, WIDTH), BF),
            jax.ShapeDtypeStruct((BLOCK, WIDTH), BF),
            jax.ShapeDtypeStruct((NY, BLOCK, 2 * WIDTH), BF),
        ),
        in_specs=[smem] + [vmem] * 7,
        scratch_shapes=[] if first else [pltpu.VMEM((BLOCK, D), F32)],
        compiler_params=pltpu.CompilerParams(vmem_limit_bytes=16 * MIB),
        cost_estimate=pl.CostEstimate(
            flops=2 * BLOCK * D * (D + 3 * WIDTH), bytes_accessed=8 * MIB, transcendentals=BLOCK
        ),
        name="dense",
    )(*operands)


def key_positions():
    column = lax.broadcasted_iota(jnp.int32, (1, L), 1)
    return (column % BLOCK) // PART * 128 + column // BLOCK * PART + column % PART


def attend(q, k, v, qpos, kpos):
    outs = []
    seen = kpos <= qpos
    for head in range(2):
        lanes = slice(head * HD, (head + 1) * HD)
        scores = dot_nt(q[:, lanes], k[:, lanes]) * (HD**-0.5)
        scores = jnp.where(seen, scores, -1e30)
        weight = jnp.exp(scores - jnp.max(scores, axis=1, keepdims=True))
        total = jnp.sum(weight, axis=1, keepdims=True)
        outs.append(dot(weight.astype(BF), v[:, lanes]) / total)
    return jnp.concatenate(outs, axis=1).astype(BF)


def attend_kernel(final, y_ref, q_ref, kv_ref, *refs):
    if final:
        state_ref, out_ref = refs
    else:
        w_ref, out_ref, fetched_ref, sem = refs
        copies = [
            pltpu.make_async_copy(w_ref.at[i], fetched_ref.at[i], sem.at[i]) for i in range(NLAT)
        ]
        for copy in copies:
            copy.start()
    row = lax.broadcasted_iota(jnp.int32, (BLOCK, 1), 0)
    qpos = row // PART * 128 + y_ref[0] * PART + row % PART
    kv = jnp.concatenate([kv_ref[i] for i in range(NY)], axis=0)
    out = attend(q_ref[...], kv[:, :WIDTH], kv[:, WIDTH:], qpos, key_positions())
    if final:
        state = state_ref[...]
        for y in range(NY):
            for i in range(NLAT):
                out_ref[y * NLAT + i, :PART] = out[i * PART : (i + 1) * PART]
                out_ref[y * NLAT + i, PART:] = state[i * PART : (i + 1) * PART]
    else:
        for i in range(NX):
            out_ref[i] = out
        for copy in copies:
            copy.wait()


def attend_latents(final, *operands):
    smem, vmem, whole = (pl.BlockSpec(memory_space=m) for m in (pltpu.SMEM, pltpu.VMEM, pl.ANY))
    if final:
        out_shape = jax.ShapeDtypeStruct((NY * NLAT, 2 * PART, WIDTH), BF)
    else:
        out_shape = (
            jax.ShapeDtypeStruct((NX, BLOCK, WIDTH), BF),
            jax.ShapeDtypeStruct(operands[-1].shape, BF),
        )
    return pl.pallas_call(
        functools.partial(attend_kernel, final),
        out_shape=out_shape,
        in_specs=[smem, vmem, vmem, vmem if final else whole],
        out_specs=vmem if final else (vmem, vmem),
        scratch_shapes=[] if final else [pltpu.SemaphoreType.DMA((NLAT,))],
        compiler_params=pltpu.CompilerParams(vmem_limit_bytes=(12 if final else 50) * MIB),
        cost_estimate=pl.CostEstimate(
            flops=8 * BLOCK * L * HD, bytes_accessed=2 * MIB, transcendentals=2 * BLOCK * L
        ),
        name="attend_latents",
    )(*operands)


def order_kernel(ref, out_ref):
    for i in range(NLAT):
        out_ref[:, i * WIDTH : (i + 1) * WIDTH] = jnp.concatenate(
            [ref[i, y, z] for z in range(NZ) for y in range(NY)], axis=0
        )


def order_weights(out_w):
    return pl.pallas_call(
        order_kernel,
        out_shape=jax.ShapeDtypeStruct((D, D), BF),
        compiler_params=pltpu.CompilerParams(vmem_limit_bytes=8 * MIB),
        name="order_weights",
    )(out_w)


def last_kernel(both_ref, out_w_ref, out_ref):
    heads, state = (
        jnp.concatenate(
            [
                jnp.concatenate(
                    [both_ref[y * NLAT + i, half * PART : (half + 1) * PART] for i in range(NLAT)],
                    axis=1,
                )
                for y in range(NY)
            ],
            axis=0,
        )
        for half in range(2)
    )
    out_ref[...] = state.astype(F32) + dot(heads, out_w_ref[...])


def last(both, out_w):
    return pl.pallas_call(
        last_kernel,
        out_shape=jax.ShapeDtypeStruct((128, D), F32),
        compiler_params=pltpu.CompilerParams(vmem_limit_bytes=16 * MIB),
        cost_estimate=pl.CostEstimate(
            flops=2 * 128 * D * D, bytes_accessed=4 * MIB, transcendentals=0
        ),
        name="last",
    )(both, out_w)


def head_angles(positions, inverse):
    angle = positions.astype(F32)[:, None] * inverse[None, :]
    cosine, sine = jnp.cos(angle), jnp.sin(angle)
    return (
        jnp.concatenate([cosine] * 4, axis=1),
        jnp.concatenate([-sine, sine, -sine, sine], axis=1),
    )


def body(token_ids, embed_table, input_gain, cross_qkv, cross_out, layer_gain, layer_qkv, layer_out):
    z, y = lax.axis_index("z"), lax.axis_index("y")
    lat = lax.axis_index(LAT)

    lat_index = jnp.full((1,), lat, jnp.int32)
    pack = pack_shards(
        lat_index, token_ids.reshape(4, 128), cross_qkv.reshape(48, WIDTH),
        layer_qkv.reshape(96, WIDTH), cross_out, layer_out.reshape(32, D),
    )
    by_z = lax.all_gather(pack, "z", axis=0)
    by_z, inverse, embed_table, input_gain = lax.optimization_barrier(
        (by_z, inverse_frequencies(), embed_table, input_gain)
    )
    now, rest_z = split_round(by_z)
    by_zy = lax.all_to_all(now, "y", split_axis=0, concat_axis=0, tiled=True)

    latent = jnp.arange(OWN, dtype=jnp.int32) + (z // 2) * 128 + y * PART + (z % 2) * OWN
    offset = N - L + latent[None, :] - KEYS * jnp.arange(STEPS, dtype=jnp.int32)[:, None]
    qcos, qsin = head_angles(offset.reshape(STEPS * OWN), inverse)
    row = jnp.arange(BLOCK, dtype=jnp.int32)
    lpos = row // PART * 128 + y * PART + row % PART
    lcos, lsin = head_angles(lpos, inverse)
    fine = inverse[:, None] * jnp.arange(KEYS, dtype=F32)[None, :]
    tables = (qcos, qsin, jnp.cos(fine), jnp.sin(fine))
    wide = embed_table.astype(F32)
    normed = wide * lax.rsqrt(jnp.mean(wide * wide, axis=-1, keepdims=True) + 1e-06) * input_gain
    normed = normed.astype(BF)
    by_zy, rest_z, normed, tables, lcos, lsin = lax.optimization_barrier(
        (by_zy, rest_z, normed, tables, lcos, lsin)
    )
    rest_zy = lax.all_gather(rest_z, "y", axis=0)
    outs = [rest_zy[:, :, 64 * i + 48 : 64 * i + 64] for i in range(LAYERS)]
    qkv = [rest_zy[:, :, 64 * i : 64 * i + 48] for i in range(LAYERS)]
    latent_ids = by_zy[2:, NZ * 68 - 4 :].reshape(L).astype(jnp.int32)
    own_ids = lax.dynamic_slice_in_dim(latent_ids, latent[0], OWN, 0)
    pick = (own_ids[:, None] == jnp.arange(VOCAB, dtype=jnp.int32)[None, :]).astype(BF)
    block_ids = lax.dynamic_slice_in_dim(latent_ids.reshape(8, NY, PART), y, 1, 1).reshape(1, BLOCK)
    qpos = jnp.broadcast_to(
        (N - L + jnp.concatenate([latent, latent]))[:, None], (2 * OWN, 128)
    )
    heads = cross_attention(by_zy, normed, pick, *tables, qpos)

    heads = lax.all_to_all(heads, LAT, split_axis=0, concat_axis=0, tiled=True)
    added = project_columns(heads, by_zy)

    added = lax.all_to_all(added, "z", split_axis=0, concat_axis=0, tiled=True)
    added, outs, qkv, block_ids = lax.optimization_barrier((added, outs, qkv, block_ids))
    out_w = [lax.all_gather(w, LAT, axis=0) for w in outs]
    added = added.reshape(BLOCK, WIDTH)
    added = gather_lat(jnp.broadcast_to(added[None], (NX, BLOCK, WIDTH)))

    state, q, kv = dense(
        True, lat_index, added, block_ids, embed_table, layer_gain, qkv[0], lcos, lsin
    )
    kv = lax.all_to_all(kv, "y", split_axis=0, concat_axis=0, tiled=True)
    y_index = jnp.full((1,), y, jnp.int32)
    heads, layer_w = attend_latents(False, y_index, q, kv, out_w[0])
    heads = gather_lat(heads)
    state, q, kv = dense(
        False, lat_index, heads, state, layer_w, layer_gain, qkv[1], lcos, lsin
    )
    kv = lax.all_to_all(kv, "y", split_axis=0, concat_axis=0, tiled=True)
    both = attend_latents(True, y_index, q, kv, state)
    both = lax.all_to_all(both, ("y", "x", "c"), split_axis=0, concat_axis=0, tiled=True)
    return last(both, order_weights(out_w[1]))


def solution(mesh):
    grid = Mesh(np.asarray(mesh.devices).reshape(NZ, NY, NX, NC), ("z", "y", "x", "c"))
    return jax.shard_map(
        body,
        mesh=grid,
        in_specs=(
            P(CTX),
            P(),
            P(),
            P(None, CTX, LAT),
            P(CTX, None),
            P(),
            P(None, None, CTX, LAT),
            P(None, CTX, None),
        ),
        out_specs=P(LAT, None),
        check_vma=False,
    )
```

```python
import functools

import jax
import jax.numpy as jnp
import numpy as np
from jax import lax
from jax.experimental import pallas as pl
from jax.experimental.pallas import tpu as pltpu
from jax.sharding import Mesh
from jax.sharding import PartitionSpec as P

D = 1024
HD = 64
HALF = 32
NZ, NY, NX, NC = 16, 4, 4, 2
NLAT = NX * NC
N = 32768
L = 1024
VOCAB = 256
WIDTH = 128
OWN = 16
LAYERS = 2
PART = 32
BLOCK = 256
KEYS = 2048
STEPS = N // KEYS
LAT = ("x", "c")
CTX = ("z", "y")
BF = jnp.bfloat16
F32 = jnp.float32
MIB = 1 << 20


def inverse_frequencies():
    return 10000.0 ** (-2.0 * jnp.arange(HALF, dtype=F32) / (2 * HALF))


def gather_lat(copies):
    by_x = lax.all_to_all(copies, "x", split_axis=0, concat_axis=0, tiled=True)
    return lax.all_gather(by_x, "c", axis=0)


def pack_kernel(lat_ref, *refs):
    ids_ref, cross_ref, layer_ref, cross_out_ref, layer_out_ref = refs[5:10]
    out_ref, sem = refs[10:]
    copies = [pltpu.make_async_copy(refs[i], refs[i + 5], sem.at[i]) for i in range(5)]
    for copy in copies:
        copy.start()
    for copy in copies:
        copy.wait()
    own = pl.ds(pl.multiple_of(lat_ref[0] * WIDTH, WIDTH), WIDTH)
    out_ref[0:48] = cross_ref[...]
    out_ref[48:64] = cross_out_ref[:, own]
    ids = ids_ref[...].astype(F32)
    out_ref[192:200] = jnp.concatenate([ids, jnp.zeros((4, WIDTH), F32)], axis=0).astype(BF)
    for layer in range(LAYERS):
        start = 64 + layer * 64
        out_ref[start : start + 48] = layer_ref[layer * 48 : (layer + 1) * 48]
        out_ref[start + 48 : start + 64] = layer_out_ref[layer * 16 : (layer + 1) * 16, own]


def pack_shards(lat_index, *operands):
    def kernel(lat_ref, *refs):
        pack_kernel(lat_ref, *refs[:5], *refs[6:11], refs[5], refs[11])

    return pl.pallas_call(
        kernel,
        out_shape=jax.ShapeDtypeStruct((200, WIDTH), BF),
        in_specs=[pl.BlockSpec(memory_space=pltpu.SMEM)] + [pl.BlockSpec(memory_space=pl.ANY)] * 5,
        out_specs=pl.BlockSpec(memory_space=pltpu.VMEM),
        scratch_shapes=[pltpu.VMEM(a.shape, a.dtype) for a in operands]
        + [pltpu.SemaphoreType.DMA((5,))],
        compiler_params=pltpu.CompilerParams(vmem_limit_bytes=58 * MIB),
        name="pack_shards",
    )(lat_index, *operands)


def split_kernel(ref, now_ref):
    ids = [ref[z, 192:200, :].astype(F32)[:4] for z in range(NZ)]
    ids = jnp.concatenate(ids, axis=0).astype(BF)
    for y in range(NY):
        for z in range(NZ):
            now_ref[y, z * 64 : (z + 1) * 64] = ref[z, :64]
        now_ref[y, NZ * 64 :] = ids


def split_round(by_z):
    return pl.pallas_call(
        split_kernel,
        out_shape=jax.ShapeDtypeStruct((NY, NZ * 68, WIDTH), BF),
        compiler_params=pltpu.CompilerParams(vmem_limit_bytes=8 * MIB),
        name="split_round",
    )(by_z)


def project_kernel(heads_ref, w_ref, out_ref):
    heads = jnp.concatenate([heads_ref[i] for i in range(NLAT)], axis=1)
    rows = [w_ref[y, z * 64 + 48 : z * 64 + 64] for z in range(NZ) for y in range(NY)]
    out = dot(heads, jnp.concatenate(rows, axis=0)).astype(BF)
    for z in range(NZ):
        out_ref[z] = out


def project_columns(heads, weights):
    return pl.pallas_call(
        project_kernel,
        out_shape=jax.ShapeDtypeStruct((NZ, OWN, WIDTH), BF),
        compiler_params=pltpu.CompilerParams(vmem_limit_bytes=8 * MIB),
        cost_estimate=pl.CostEstimate(
            flops=2 * OWN * D * WIDTH, bytes_accessed=MIB, transcendentals=0
        ),
        name="project_columns",
    )(heads, weights)


def dot(a, b):
    return jnp.dot(a, b, preferred_element_type=F32)


def dot_nt(a, b):
    return lax.dot_general(a, b, (((1,), (1,)), ((), ())), preferred_element_type=F32)


def split_two(x):
    high = x.astype(BF)
    return high, (x - high.astype(F32)).astype(BF)


def rotate_lanes(x, cosine, sine):
    lane = lax.broadcasted_iota(jnp.int32, x.shape, 1)
    other = jnp.where(lane % HD < HALF, pltpu.roll(x, WIDTH - HALF, 1), pltpu.roll(x, HALF, 1))
    return x * cosine + other * sine


def cross_kernel(
    w_ref, normed_ref, pick_ref, qcos_ref, qsin_ref, cos_ref, sin_ref, qpos_ref,
    out_ref, w_sc, table_sc, q_sc, s_sc, v_sc, ids_sc,
):
    for z in range(NZ):
        for y in range(NY):
            row = (z * NY + y) * 16
            for part in range(3):
                start = z * 64 + part * 16
                w_sc[row : row + 16, part * WIDTH : (part + 1) * WIDTH] = w_ref[
                    y, start : start + 16, :
                ]
    for y in range(NY):
        ids = w_ref[y, NZ * 64 :, :].astype(F32)
        for z in range(NZ):
            ids_sc[z, y * 4 : (y + 1) * 4] = ids[z * 4 : (z + 1) * 4]
    normed = normed_ref[...]
    table_sc[...] = dot(normed, w_sc[:, WIDTH:]).T.astype(BF)
    rows = dot(pick_ref[...], normed).astype(BF)
    query = dot(rows, w_sc[:, :WIDTH]) * (HD**-0.5)
    lane = lax.broadcasted_iota(jnp.int32, query.shape, 1)
    for step in range(STEPS):
        block = slice(step * OWN, (step + 1) * OWN)
        turned = rotate_lanes(query, qcos_ref[block], qsin_ref[block])
        q_sc[step, :OWN] = jnp.where(lane < HD, turned, 0.0).astype(BF)
        q_sc[step, OWN:] = jnp.where(lane < HD, 0.0, turned).astype(BF)
    token = lax.broadcasted_iota(jnp.int32, (VOCAB, 128), 0).astype(F32).astype(BF)

    def scores_of(step, top):
        hot = []
        ids = ids_sc[step]
        for r in range(16):
            row = jnp.broadcast_to(ids[r : r + 1, :], (VOCAB, 128)).astype(BF)
            hot.append(jnp.where(token == row, jnp.ones((), BF), jnp.zeros((), BF)))
        both = dot(table_sc[...], jnp.concatenate(hot, axis=1))
        v_sc[step] = both[WIDTH:].astype(BF)
        cosine, sine = cos_ref[...], sin_ref[...]
        pieces = []
        for head in range(2):
            first = both[head * HD : head * HD + HALF]
            second = both[head * HD + HALF : (head + 1) * HD]
            pieces.append(first * cosine - second * sine)
            pieces.append(second * cosine + first * sine)
        scores = dot(q_sc[step], jnp.concatenate(pieces, axis=0).astype(BF))
        kpos = step * KEYS + lax.broadcasted_iota(jnp.int32, scores.shape, 1)
        scores = jnp.where(kpos <= qpos_ref[:, :1], scores, -1e30)
        s_sc[step] = scores
        for i in range(KEYS // 128):
            top = jnp.maximum(top, scores[:, i * 128 : (i + 1) * 128])
        return top

    top = lax.fori_loop(0, STEPS, scores_of, jnp.full((2 * OWN, 128), -1e30, F32), unroll=8)
    most = jnp.max(top, axis=1, keepdims=True)

    def values_of(step, carry):
        total, acc = carry
        weight = jnp.exp(s_sc[step] - most)
        for i in range(KEYS // 128):
            total = total + weight[:, i * 128 : (i + 1) * 128]
        return total, acc + dot_nt(v_sc[step], weight.astype(BF))

    total, acc = lax.fori_loop(
        0, STEPS, values_of, (jnp.zeros((2 * OWN, 128), F32), jnp.zeros((WIDTH, 2 * OWN), F32)),
        unroll=4,
    )
    value = acc.T / jnp.sum(total, axis=1, keepdims=True)
    lane = lax.broadcasted_iota(jnp.int32, (OWN, WIDTH), 1)
    value = jnp.where(lane < HD, value[:OWN], value[OWN:]).astype(BF)
    for i in range(NLAT):
        out_ref[i] = value


def cross_attention(*operands):
    return pl.pallas_call(
        cross_kernel,
        out_shape=jax.ShapeDtypeStruct((NLAT, OWN, WIDTH), BF),
        scratch_shapes=[
            pltpu.VMEM((D, 3 * WIDTH), BF),
            pltpu.VMEM((2 * WIDTH, VOCAB), BF),
            pltpu.VMEM((STEPS, 2 * OWN, WIDTH), BF),
            pltpu.VMEM((STEPS, 2 * OWN, KEYS), F32),
            pltpu.VMEM((STEPS, WIDTH, KEYS), BF),
            pltpu.VMEM((NZ, 16, 128), F32),
        ],
        compiler_params=pltpu.CompilerParams(vmem_limit_bytes=20 * MIB),
        cost_estimate=pl.CostEstimate(
            flops=MIB, bytes_accessed=MIB, transcendentals=0
        ),
        name="cross_attention",
    )(*operands)


def out_weights(ref):
    columns = []
    for i in range(NLAT):
        rows = [ref[i, y, z] for z in range(NZ) for y in range(NY)]
        columns.append(jnp.concatenate(rows, axis=0))
    return jnp.concatenate(columns, axis=1)


def dense_kernel(first, *refs):
    lat_ref, parts_ref, state_ref, matrix_ref, gain_ref, qkv_ref, cos_ref, sin_ref = refs[:8]
    state_out, q_out, kv_out = refs[8:11]
    parts = jnp.concatenate([parts_ref[i % NC, i // NC] for i in range(NLAT)], axis=1)
    if first:
        token = lax.broadcasted_iota(jnp.int32, (VOCAB, BLOCK), 0)
        hot = jnp.where(token == state_ref[...], 1.0, 0.0).T.astype(BF)
        state = dot(hot, matrix_ref[...]) + parts.astype(F32)
        state_out[...] = state
    else:
        state = state_ref[...] + dot(parts, out_weights(matrix_ref))
        state_sc = refs[11]
        state_sc[...] = state
        own = pl.ds(pl.multiple_of(lat_ref[0] * WIDTH, WIDTH), WIDTH)
        state_out[...] = state_sc[:, own].astype(BF)
    scale = lax.rsqrt(jnp.mean(state * state, axis=1, keepdims=True) + 1e-06)
    normed = (state * scale * gain_ref[0 if first else 1, :][None]).astype(BF)
    cosine, sine = cos_ref[...], sin_ref[...]
    weights = [
        jnp.concatenate(
            [qkv_ref[y, z, i * 16 : (i + 1) * 16] for z in range(NZ) for y in range(NY)], axis=0
        )
        for i in range(3)
    ]
    product = dot(normed, jnp.concatenate(weights, axis=1))
    q_out[...] = rotate_lanes(product[:, :WIDTH], cosine, sine).astype(BF)
    k = rotate_lanes(product[:, WIDTH : 2 * WIDTH], cosine, sine).astype(BF)
    v = product[:, 2 * WIDTH :].astype(BF)
    for y in range(NY):
        kv_out[y, :, :WIDTH] = k
        kv_out[y, :, WIDTH:] = v


def dense(first, *operands):
    smem, vmem = (pl.BlockSpec(memory_space=m) for m in (pltpu.SMEM, pltpu.VMEM))
    return pl.pallas_call(
        functools.partial(dense_kernel, first),
        out_shape=(
            jax.ShapeDtypeStruct((BLOCK, D), F32)
            if first
            else jax.ShapeDtypeStruct((BLOCK, WIDTH), BF),
            jax.ShapeDtypeStruct((BLOCK, WIDTH), BF),
            jax.ShapeDtypeStruct((NY, BLOCK, 2 * WIDTH), BF),
        ),
        in_specs=[smem] + [vmem] * 7,
        scratch_shapes=[] if first else [pltpu.VMEM((BLOCK, D), F32)],
        compiler_params=pltpu.CompilerParams(vmem_limit_bytes=16 * MIB),
        cost_estimate=pl.CostEstimate(
            flops=2 * BLOCK * D * (D + 3 * WIDTH), bytes_accessed=8 * MIB, transcendentals=BLOCK
        ),
        name="dense",
    )(*operands)


def key_positions():
    column = lax.broadcasted_iota(jnp.int32, (1, L), 1)
    return (column % BLOCK) // PART * 128 + column // BLOCK * PART + column % PART


def attend(q, k, v, qpos, kpos):
    outs = []
    seen = kpos <= qpos
    for head in range(2):
        lanes = slice(head * HD, (head + 1) * HD)
        scores = dot_nt(q[:, lanes], k[:, lanes]) * (HD**-0.5)
        scores = jnp.where(seen, scores, -1e30)
        weight = jnp.exp(scores - jnp.max(scores, axis=1, keepdims=True))
        total = jnp.sum(weight, axis=1, keepdims=True)
        outs.append(dot(weight.astype(BF), v[:, lanes]) / total)
    return jnp.concatenate(outs, axis=1).astype(BF)


def attend_kernel(final, y_ref, q_ref, kv_ref, *refs):
    out_ref = refs[-1]
    row = lax.broadcasted_iota(jnp.int32, (BLOCK, 1), 0)
    qpos = row // PART * 128 + y_ref[0] * PART + row % PART
    kv = jnp.concatenate([kv_ref[i] for i in range(NY)], axis=0)
    out = attend(q_ref[...], kv[:, :WIDTH], kv[:, WIDTH:], qpos, key_positions())
    if final:
        state = refs[0][...]
        for y in range(NY):
            for i in range(NLAT):
                out_ref[y * NLAT + i, :PART] = out[i * PART : (i + 1) * PART]
                out_ref[y * NLAT + i, PART:] = state[i * PART : (i + 1) * PART]
    else:
        for i in range(NX):
            out_ref[i] = out


def attend_latents(final, *operands):
    shape = (NY * NLAT, 2 * PART, WIDTH) if final else (NX, BLOCK, WIDTH)
    smem, vmem = (pl.BlockSpec(memory_space=m) for m in (pltpu.SMEM, pltpu.VMEM))
    return pl.pallas_call(
        functools.partial(attend_kernel, final),
        out_shape=jax.ShapeDtypeStruct(shape, BF),
        in_specs=[smem] + [vmem] * (len(operands) - 1),
        compiler_params=pltpu.CompilerParams(vmem_limit_bytes=12 * MIB),
        cost_estimate=pl.CostEstimate(
            flops=8 * BLOCK * L * HD, bytes_accessed=2 * MIB, transcendentals=2 * BLOCK * L
        ),
        name="attend_latents",
    )(*operands)


def order_kernel(ref, out_ref):
    for i in range(NLAT):
        out_ref[:, i * WIDTH : (i + 1) * WIDTH] = jnp.concatenate(
            [ref[i, y, z] for z in range(NZ) for y in range(NY)], axis=0
        )


def order_weights(out_w):
    return pl.pallas_call(
        order_kernel,
        out_shape=jax.ShapeDtypeStruct((D, D), BF),
        compiler_params=pltpu.CompilerParams(vmem_limit_bytes=8 * MIB),
        name="order_weights",
    )(out_w)


def last_kernel(both_ref, out_w_ref, out_ref):
    heads, state = (
        jnp.concatenate(
            [
                jnp.concatenate(
                    [both_ref[y * NLAT + i, half * PART : (half + 1) * PART] for i in range(NLAT)],
                    axis=1,
                )
                for y in range(NY)
            ],
            axis=0,
        )
        for half in range(2)
    )
    out_ref[...] = state.astype(F32) + dot(heads, out_w_ref[...])


def last(both, out_w):
    return pl.pallas_call(
        last_kernel,
        out_shape=jax.ShapeDtypeStruct((128, D), F32),
        compiler_params=pltpu.CompilerParams(vmem_limit_bytes=16 * MIB),
        cost_estimate=pl.CostEstimate(
            flops=2 * 128 * D * D, bytes_accessed=4 * MIB, transcendentals=0
        ),
        name="last",
    )(both, out_w)


def head_angles(positions, inverse):
    angle = positions.astype(F32)[:, None] * inverse[None, :]
    cosine, sine = jnp.cos(angle), jnp.sin(angle)
    return (
        jnp.concatenate([cosine] * 4, axis=1),
        jnp.concatenate([-sine, sine, -sine, sine], axis=1),
    )


def body(token_ids, embed_table, input_gain, cross_qkv, cross_out, layer_gain, layer_qkv, layer_out):
    z, y = lax.axis_index("z"), lax.axis_index("y")
    lat = lax.axis_index(LAT)

    lat_index = jnp.full((1,), lat, jnp.int32)
    pack = pack_shards(
        lat_index, token_ids.reshape(4, 128), cross_qkv.reshape(48, WIDTH),
        layer_qkv.reshape(96, WIDTH), cross_out, layer_out.reshape(32, D),
    )
    by_z = lax.all_gather(pack, "z", axis=0)
    by_z, inverse, embed_table, input_gain = lax.optimization_barrier(
        (by_z, inverse_frequencies(), embed_table, input_gain)
    )
    now = split_round(by_z)
    by_zy = lax.all_to_all(now, "y", split_axis=0, concat_axis=0, tiled=True)

    latent = jnp.arange(OWN, dtype=jnp.int32) + (z // 2) * 128 + y * PART + (z % 2) * OWN
    offset = N - L + latent[None, :] - KEYS * jnp.arange(STEPS, dtype=jnp.int32)[:, None]
    qcos, qsin = head_angles(offset.reshape(STEPS * OWN), inverse)
    row = jnp.arange(BLOCK, dtype=jnp.int32)
    lpos = row // PART * 128 + y * PART + row % PART
    lcos, lsin = head_angles(lpos, inverse)
    fine = inverse[:, None] * jnp.arange(KEYS, dtype=F32)[None, :]
    tables = (qcos, qsin, jnp.cos(fine), jnp.sin(fine))
    wide = embed_table.astype(F32)
    normed = wide * lax.rsqrt(jnp.mean(wide * wide, axis=-1, keepdims=True) + 1e-06) * input_gain
    normed = normed.astype(BF)
    by_zy, rest_z, normed, tables, lcos, lsin = lax.optimization_barrier(
        (by_zy, by_z[:, 64:192], normed, tables, lcos, lsin)
    )
    rest_zy = lax.all_gather(rest_z, "y", axis=0)
    outs = [rest_zy[:, :, 64 * i + 48 : 64 * i + 64] for i in range(LAYERS)]
    qkv = [rest_zy[:, :, 64 * i : 64 * i + 48] for i in range(LAYERS)]
    latent_ids = by_zy[2:, NZ * 68 - 4 :].reshape(L).astype(jnp.int32)
    own_ids = lax.dynamic_slice_in_dim(latent_ids, latent[0], OWN, 0)
    pick = (own_ids[:, None] == jnp.arange(VOCAB, dtype=jnp.int32)[None, :]).astype(BF)
    block_ids = lax.dynamic_slice_in_dim(latent_ids.reshape(8, NY, PART), y, 1, 1).reshape(1, BLOCK)
    qpos = jnp.broadcast_to(
        (N - L + jnp.concatenate([latent, latent]))[:, None], (2 * OWN, 128)
    )
    heads = cross_attention(by_zy, normed, pick, *tables, qpos)

    heads = lax.all_to_all(heads, LAT, split_axis=0, concat_axis=0, tiled=True)
    added = project_columns(heads, by_zy)

    added = lax.all_to_all(added, "z", split_axis=0, concat_axis=0, tiled=True)
    added, outs, qkv, block_ids = lax.optimization_barrier((added, outs, qkv, block_ids))
    out_w = [lax.all_gather(w, LAT, axis=0) for w in outs]
    added = added.reshape(BLOCK, WIDTH)
    added = gather_lat(jnp.broadcast_to(added[None], (NX, BLOCK, WIDTH)))

    state, q, kv = dense(
        True, lat_index, added, block_ids, embed_table, layer_gain, qkv[0], lcos, lsin
    )
    kv = lax.all_to_all(kv, "y", split_axis=0, concat_axis=0, tiled=True)
    y_index = jnp.full((1,), y, jnp.int32)
    heads = attend_latents(False, y_index, q, kv)
    heads = gather_lat(heads)
    state, q, kv = dense(
        False, lat_index, heads, state, out_w[0], layer_gain, qkv[1], lcos, lsin
    )
    kv = lax.all_to_all(kv, "y", split_axis=0, concat_axis=0, tiled=True)
    both = attend_latents(True, y_index, q, kv, state)
    both = lax.all_to_all(both, ("y", "x", "c"), split_axis=0, concat_axis=0, tiled=True)
    return last(both, order_weights(out_w[1]))


def solution(mesh):
    grid = Mesh(np.asarray(mesh.devices).reshape(NZ, NY, NX, NC), ("z", "y", "x", "c"))
    return jax.shard_map(
        body,
        mesh=grid,
        in_specs=(
            P(CTX),
            P(),
            P(),
            P(None, CTX, LAT),
            P(CTX, None),
            P(),
            P(None, None, CTX, LAT),
            P(None, CTX, None),
        ),
        out_specs=P(LAT, None),
        check_vma=False,
    )
```

```python
import functools

import jax
import jax.numpy as jnp
import numpy as np
from jax import lax
from jax.experimental import pallas as pl
from jax.experimental.pallas import tpu as pltpu
from jax.sharding import Mesh
from jax.sharding import PartitionSpec as P

D = 1024
HD = 64
HALF = 32
NZ, NY, NX, NC = 16, 4, 4, 2
NLAT = NX * NC
N = 32768
L = 1024
VOCAB = 256
WIDTH = 128
OWN = 16
LAYERS = 2
PART = 32
BLOCK = 256
KEYS = 2048
STEPS = N // KEYS
LAT = ("x", "c")
CTX = ("z", "y")
BF = jnp.bfloat16
F32 = jnp.float32
MIB = 1 << 20


def inverse_frequencies():
    return 10000.0 ** (-2.0 * jnp.arange(HALF, dtype=F32) / (2 * HALF))


def gather_lat(copies):
    by_x = lax.all_to_all(copies, "x", split_axis=0, concat_axis=0, tiled=True)
    return lax.all_gather(by_x, "c", axis=0)


def pack_kernel(lat_ref, *refs):
    ids_ref, cross_ref, layer_ref, cross_out_ref, layer_out_ref = refs[5:10]
    out_ref, sem = refs[10:]
    copies = [pltpu.make_async_copy(refs[i], refs[i + 5], sem.at[i]) for i in range(5)]
    for copy in copies:
        copy.start()
    for copy in copies:
        copy.wait()
    own = pl.ds(pl.multiple_of(lat_ref[0] * WIDTH, WIDTH), WIDTH)
    out_ref[0:48] = cross_ref[...]
    out_ref[48:64] = cross_out_ref[:, own]
    ids = ids_ref[...].astype(F32)
    out_ref[192:200] = jnp.concatenate([ids, jnp.zeros((4, WIDTH), F32)], axis=0).astype(BF)
    for layer in range(LAYERS):
        start = 64 + layer * 64
        out_ref[start : start + 48] = layer_ref[layer * 48 : (layer + 1) * 48]
        out_ref[start + 48 : start + 64] = layer_out_ref[layer * 16 : (layer + 1) * 16, own]


def pack_shards(lat_index, *operands):
    def kernel(lat_ref, *refs):
        pack_kernel(lat_ref, *refs[:5], *refs[6:11], refs[5], refs[11])

    return pl.pallas_call(
        kernel,
        out_shape=jax.ShapeDtypeStruct((200, WIDTH), BF),
        in_specs=[pl.BlockSpec(memory_space=pltpu.SMEM)] + [pl.BlockSpec(memory_space=pl.ANY)] * 5,
        out_specs=pl.BlockSpec(memory_space=pltpu.VMEM),
        scratch_shapes=[pltpu.VMEM(a.shape, a.dtype) for a in operands]
        + [pltpu.SemaphoreType.DMA((5,))],
        compiler_params=pltpu.CompilerParams(vmem_limit_bytes=58 * MIB),
        name="pack_shards",
    )(lat_index, *operands)


def split_kernel(ref, now_ref):
    ids = [ref[z, 192:200, :].astype(F32)[:4] for z in range(NZ)]
    ids = jnp.concatenate(ids, axis=0).astype(BF)
    for y in range(NY):
        for z in range(NZ):
            now_ref[y, z * 64 : (z + 1) * 64] = ref[z, :64]
        now_ref[y, NZ * 64 :] = ids


def split_round(by_z):
    return pl.pallas_call(
        split_kernel,
        out_shape=jax.ShapeDtypeStruct((NY, NZ * 68, WIDTH), BF),
        compiler_params=pltpu.CompilerParams(vmem_limit_bytes=8 * MIB),
        name="split_round",
    )(by_z)


def project_kernel(heads_ref, w_ref, out_ref):
    heads = jnp.concatenate([heads_ref[i] for i in range(NLAT)], axis=1)
    rows = [w_ref[y, z * 64 + 48 : z * 64 + 64] for z in range(NZ) for y in range(NY)]
    out = dot(heads, jnp.concatenate(rows, axis=0)).astype(BF)
    for z in range(NZ):
        out_ref[z] = out


def project_columns(heads, weights):
    return pl.pallas_call(
        project_kernel,
        out_shape=jax.ShapeDtypeStruct((NZ, OWN, WIDTH), BF),
        compiler_params=pltpu.CompilerParams(vmem_limit_bytes=8 * MIB),
        cost_estimate=pl.CostEstimate(
            flops=2 * OWN * D * WIDTH, bytes_accessed=MIB, transcendentals=0
        ),
        name="project_columns",
    )(heads, weights)


def dot(a, b):
    return jnp.dot(a, b, preferred_element_type=F32)


def dot_nt(a, b):
    return lax.dot_general(a, b, (((1,), (1,)), ((), ())), preferred_element_type=F32)


def split_two(x):
    high = x.astype(BF)
    return high, (x - high.astype(F32)).astype(BF)


def rotate_lanes(x, cosine, sine):
    lane = lax.broadcasted_iota(jnp.int32, x.shape, 1)
    other = jnp.where(lane % HD < HALF, pltpu.roll(x, WIDTH - HALF, 1), pltpu.roll(x, HALF, 1))
    return x * cosine + other * sine


def cross_kernel(
    place_ref, w_ref, normed_ref, qcos_ref, qsin_ref, cos_ref, sin_ref,
    out_ref, latent_ref, w_sc, table_sc, q_sc, s_sc, v_sc, ids_sc,
):
    for z in range(NZ):
        for y in range(NY):
            row = (z * NY + y) * 16
            for part in range(3):
                start = z * 64 + part * 16
                w_sc[row : row + 16, part * WIDTH : (part + 1) * WIDTH] = w_ref[
                    y, start : start + 16, :
                ]
    for y in range(NY):
        ids = w_ref[y, NZ * 64 :, :].astype(F32)
        for z in range(NZ):
            ids_sc[z, y * 4 : (y + 1) * 4] = ids[z * 4 : (z + 1) * 4]
    latents = jnp.concatenate([ids_sc[NZ - 1, 8:12], ids_sc[NZ - 1, 12:16]], axis=0)
    latent_ref[...] = latents
    turned = pltpu.roll(latents, place_ref[2], 1)
    here = lax.broadcasted_iota(jnp.int32, turned.shape, 0) == place_ref[1]
    own = jnp.sum(jnp.where(here, turned, 0.0), axis=0, keepdims=True)
    token = lax.broadcasted_iota(jnp.int32, (VOCAB, 128), 0).astype(F32)
    pick = jnp.where(token == own, 1.0, 0.0).T[:OWN].astype(BF)
    normed = normed_ref[...]
    table_sc[...] = dot(normed, w_sc[:, WIDTH:]).T.astype(BF)
    rows = dot(pick, normed).astype(BF)
    query = dot(rows, w_sc[:, :WIDTH]) * (HD**-0.5)
    lane = lax.broadcasted_iota(jnp.int32, query.shape, 1)
    for step in range(STEPS):
        block = slice(step * OWN, (step + 1) * OWN)
        turned = rotate_lanes(query, qcos_ref[block], qsin_ref[block])
        q_sc[step, :OWN] = jnp.where(lane < HD, turned, 0.0).astype(BF)
        q_sc[step, OWN:] = jnp.where(lane < HD, 0.0, turned).astype(BF)
    token = token.astype(BF)
    qpos = lax.broadcasted_iota(jnp.int32, (2 * OWN, 1), 0) % OWN + (N - L) + place_ref[0]

    def scores_of(step, top):
        hot = []
        ids = ids_sc[step]
        for r in range(16):
            row = jnp.broadcast_to(ids[r : r + 1, :], (VOCAB, 128)).astype(BF)
            hot.append(jnp.where(token == row, jnp.ones((), BF), jnp.zeros((), BF)))
        both = dot(table_sc[...], jnp.concatenate(hot, axis=1))
        v_sc[step] = both[WIDTH:].astype(BF)
        cosine, sine = cos_ref[...], sin_ref[...]
        pieces = []
        for head in range(2):
            first = both[head * HD : head * HD + HALF]
            second = both[head * HD + HALF : (head + 1) * HD]
            pieces.append(first * cosine - second * sine)
            pieces.append(second * cosine + first * sine)
        scores = dot(q_sc[step], jnp.concatenate(pieces, axis=0).astype(BF))
        kpos = step * KEYS + lax.broadcasted_iota(jnp.int32, scores.shape, 1)
        scores = jnp.where(kpos <= qpos, scores, -1e30)
        s_sc[step] = scores
        for i in range(KEYS // 128):
            top = jnp.maximum(top, scores[:, i * 128 : (i + 1) * 128])
        return top

    top = lax.fori_loop(0, STEPS, scores_of, jnp.full((2 * OWN, 128), -1e30, F32), unroll=8)
    most = jnp.max(top, axis=1, keepdims=True)

    def values_of(step, carry):
        total, acc = carry
        weight = jnp.exp(s_sc[step] - most)
        for i in range(KEYS // 128):
            total = total + weight[:, i * 128 : (i + 1) * 128]
        return total, acc + dot_nt(v_sc[step], weight.astype(BF))

    total, acc = lax.fori_loop(
        0, STEPS, values_of, (jnp.zeros((2 * OWN, 128), F32), jnp.zeros((WIDTH, 2 * OWN), F32)),
        unroll=8,
    )
    value = acc.T / jnp.sum(total, axis=1, keepdims=True)
    lane = lax.broadcasted_iota(jnp.int32, (OWN, WIDTH), 1)
    value = jnp.where(lane < HD, value[:OWN], value[OWN:]).astype(BF)
    for i in range(NLAT):
        out_ref[i] = value


def cross_attention(*operands):
    return pl.pallas_call(
        cross_kernel,
        out_shape=(
            jax.ShapeDtypeStruct((NLAT, OWN, WIDTH), BF),
            jax.ShapeDtypeStruct((8, 128), F32),
        ),
        in_specs=[pl.BlockSpec(memory_space=pltpu.SMEM)]
        + [pl.BlockSpec(memory_space=pltpu.VMEM)] * (len(operands) - 1),
        scratch_shapes=[
            pltpu.VMEM((D, 3 * WIDTH), BF),
            pltpu.VMEM((2 * WIDTH, VOCAB), BF),
            pltpu.VMEM((STEPS, 2 * OWN, WIDTH), BF),
            pltpu.VMEM((STEPS, 2 * OWN, KEYS), F32),
            pltpu.VMEM((STEPS, WIDTH, KEYS), BF),
            pltpu.VMEM((NZ, 16, 128), F32),
        ],
        compiler_params=pltpu.CompilerParams(vmem_limit_bytes=20 * MIB),
        cost_estimate=pl.CostEstimate(
            flops=MIB, bytes_accessed=MIB, transcendentals=0
        ),
        name="cross_attention",
    )(*operands)


def out_weights(ref):
    columns = []
    for i in range(NLAT):
        rows = [ref[i, y, z] for z in range(NZ) for y in range(NY)]
        columns.append(jnp.concatenate(rows, axis=0))
    return jnp.concatenate(columns, axis=1)


def dense_kernel(first, *refs):
    lat_ref, parts_ref, state_ref, matrix_ref, gain_ref, qkv_ref, cos_ref, sin_ref = refs[:8]
    state_out, q_out, kv_out = refs[8:11]
    parts = jnp.concatenate([parts_ref[i % NC, i // NC] for i in range(NLAT)], axis=1)
    if first:
        ids = pltpu.roll(state_ref[...], lat_ref[1], 1)
        ids = jnp.concatenate([ids[i : i + 1, :PART] for i in range(NLAT)], axis=1)
        token = lax.broadcasted_iota(jnp.int32, (VOCAB, BLOCK), 0).astype(F32)
        hot = jnp.where(token == ids, 1.0, 0.0).T.astype(BF)
        state = dot(hot, matrix_ref[...]) + parts.astype(F32)
        state_out[...] = state
    else:
        state = state_ref[...] + dot(parts, out_weights(matrix_ref))
        state_sc = refs[11]
        state_sc[...] = state
        own = pl.ds(pl.multiple_of(lat_ref[0] * WIDTH, WIDTH), WIDTH)
        state_out[...] = state_sc[:, own].astype(BF)
    scale = lax.rsqrt(jnp.mean(state * state, axis=1, keepdims=True) + 1e-06)
    normed = (state * scale * gain_ref[0 if first else 1, :][None]).astype(BF)
    cosine, sine = cos_ref[...], sin_ref[...]
    weights = [
        jnp.concatenate(
            [qkv_ref[y, z, i * 16 : (i + 1) * 16] for z in range(NZ) for y in range(NY)], axis=0
        )
        for i in range(3)
    ]
    product = dot(normed, jnp.concatenate(weights, axis=1))
    q_out[...] = rotate_lanes(product[:, :WIDTH], cosine, sine).astype(BF)
    k = rotate_lanes(product[:, WIDTH : 2 * WIDTH], cosine, sine).astype(BF)
    v = product[:, 2 * WIDTH :].astype(BF)
    for y in range(NY):
        kv_out[y, :, :WIDTH] = k
        kv_out[y, :, WIDTH:] = v


def dense(first, *operands):
    smem, vmem = (pl.BlockSpec(memory_space=m) for m in (pltpu.SMEM, pltpu.VMEM))
    return pl.pallas_call(
        functools.partial(dense_kernel, first),
        out_shape=(
            jax.ShapeDtypeStruct((BLOCK, D), F32)
            if first
            else jax.ShapeDtypeStruct((BLOCK, WIDTH), BF),
            jax.ShapeDtypeStruct((BLOCK, WIDTH), BF),
            jax.ShapeDtypeStruct((NY, BLOCK, 2 * WIDTH), BF),
        ),
        in_specs=[smem] + [vmem] * 7,
        scratch_shapes=[] if first else [pltpu.VMEM((BLOCK, D), F32)],
        compiler_params=pltpu.CompilerParams(vmem_limit_bytes=16 * MIB),
        cost_estimate=pl.CostEstimate(
            flops=2 * BLOCK * D * (D + 3 * WIDTH), bytes_accessed=8 * MIB, transcendentals=BLOCK
        ),
        name="dense",
    )(*operands)


def key_positions():
    column = lax.broadcasted_iota(jnp.int32, (1, L), 1)
    return (column % BLOCK) // PART * 128 + column // BLOCK * PART + column % PART


def attend(q, k, v, qpos, kpos):
    outs = []
    seen = kpos <= qpos
    for head in range(2):
        lanes = slice(head * HD, (head + 1) * HD)
        scores = dot_nt(q[:, lanes], k[:, lanes]) * (HD**-0.5)
        scores = jnp.where(seen, scores, -1e30)
        weight = jnp.exp(scores - jnp.max(scores, axis=1, keepdims=True))
        total = jnp.sum(weight, axis=1, keepdims=True)
        outs.append(dot(weight.astype(BF), v[:, lanes]) / total)
    return jnp.concatenate(outs, axis=1).astype(BF)


def attend_kernel(final, y_ref, q_ref, kv_ref, *refs):
    out_ref = refs[-1]
    row = lax.broadcasted_iota(jnp.int32, (BLOCK, 1), 0)
    qpos = row // PART * 128 + y_ref[0] * PART + row % PART
    kv = jnp.concatenate([kv_ref[i] for i in range(NY)], axis=0)
    out = attend(q_ref[...], kv[:, :WIDTH], kv[:, WIDTH:], qpos, key_positions())
    if final:
        state = refs[0][...]
        for y in range(NY):
            for i in range(NLAT):
                out_ref[y * NLAT + i, :PART] = out[i * PART : (i + 1) * PART]
                out_ref[y * NLAT + i, PART:] = state[i * PART : (i + 1) * PART]
    else:
        for i in range(NX):
            out_ref[i] = out


def attend_latents(final, *operands):
    shape = (NY * NLAT, 2 * PART, WIDTH) if final else (NX, BLOCK, WIDTH)
    smem, vmem = (pl.BlockSpec(memory_space=m) for m in (pltpu.SMEM, pltpu.VMEM))
    return pl.pallas_call(
        functools.partial(attend_kernel, final),
        out_shape=jax.ShapeDtypeStruct(shape, BF),
        in_specs=[smem] + [vmem] * (len(operands) - 1),
        compiler_params=pltpu.CompilerParams(vmem_limit_bytes=12 * MIB),
        cost_estimate=pl.CostEstimate(
            flops=8 * BLOCK * L * HD, bytes_accessed=2 * MIB, transcendentals=2 * BLOCK * L
        ),
        name="attend_latents",
    )(*operands)


def order_kernel(ref, out_ref):
    for i in range(NLAT):
        out_ref[:, i * WIDTH : (i + 1) * WIDTH] = jnp.concatenate(
            [ref[i, y, z] for z in range(NZ) for y in range(NY)], axis=0
        )


def order_weights(out_w):
    return pl.pallas_call(
        order_kernel,
        out_shape=jax.ShapeDtypeStruct((D, D), BF),
        compiler_params=pltpu.CompilerParams(vmem_limit_bytes=8 * MIB),
        name="order_weights",
    )(out_w)


def last_kernel(both_ref, out_w_ref, out_ref):
    heads, state = (
        jnp.concatenate(
            [
                jnp.concatenate(
                    [both_ref[y * NLAT + i, half * PART : (half + 1) * PART] for i in range(NLAT)],
                    axis=1,
                )
                for y in range(NY)
            ],
            axis=0,
        )
        for half in range(2)
    )
    out_ref[...] = state.astype(F32) + dot(heads, out_w_ref[...])


def last(both, out_w):
    return pl.pallas_call(
        last_kernel,
        out_shape=jax.ShapeDtypeStruct((128, D), F32),
        compiler_params=pltpu.CompilerParams(vmem_limit_bytes=16 * MIB),
        cost_estimate=pl.CostEstimate(
            flops=2 * 128 * D * D, bytes_accessed=4 * MIB, transcendentals=0
        ),
        name="last",
    )(both, out_w)


def head_angles(positions, inverse):
    angle = positions.astype(F32)[:, None] * inverse[None, :]
    cosine, sine = jnp.cos(angle), jnp.sin(angle)
    return (
        jnp.concatenate([cosine] * 4, axis=1),
        jnp.concatenate([-sine, sine, -sine, sine], axis=1),
    )


def body(token_ids, embed_table, input_gain, cross_qkv, cross_out, layer_gain, layer_qkv, layer_out):
    z, y = lax.axis_index("z"), lax.axis_index("y")
    lat = lax.axis_index(LAT)

    lat_index = jnp.stack([lat, (128 - y * PART) % 128])
    pack = pack_shards(
        lat_index, token_ids.reshape(4, 128), cross_qkv.reshape(48, WIDTH),
        layer_qkv.reshape(96, WIDTH), cross_out, layer_out.reshape(32, D),
    )
    by_z = lax.all_gather(pack, "z", axis=0)
    by_z, inverse, embed_table, input_gain = lax.optimization_barrier(
        (by_z, inverse_frequencies(), embed_table, input_gain)
    )
    now = split_round(by_z)
    by_zy = lax.all_to_all(now, "y", split_axis=0, concat_axis=0, tiled=True)

    latent = jnp.arange(OWN, dtype=jnp.int32) + (z // 2) * 128 + y * PART + (z % 2) * OWN
    offset = N - L + latent[None, :] - KEYS * jnp.arange(STEPS, dtype=jnp.int32)[:, None]
    qcos, qsin = head_angles(offset.reshape(STEPS * OWN), inverse)
    row = jnp.arange(BLOCK, dtype=jnp.int32)
    lpos = row // PART * 128 + y * PART + row % PART
    lcos, lsin = head_angles(lpos, inverse)
    fine = inverse[:, None] * jnp.arange(KEYS, dtype=F32)[None, :]
    tables = (qcos, qsin, jnp.cos(fine), jnp.sin(fine))
    wide = embed_table.astype(F32)
    normed = wide * lax.rsqrt(jnp.mean(wide * wide, axis=-1, keepdims=True) + 1e-06) * input_gain
    normed = normed.astype(BF)
    by_zy, rest_z, normed, tables, lcos, lsin = lax.optimization_barrier(
        (by_zy, by_z[:, 64:192], normed, tables, lcos, lsin)
    )
    rest_zy = lax.all_gather(rest_z, "y", axis=0)
    outs = [rest_zy[:, :, 64 * i + 48 : 64 * i + 64] for i in range(LAYERS)]
    qkv = [rest_zy[:, :, 64 * i : 64 * i + 48] for i in range(LAYERS)]
    place = jnp.stack([latent[0], z // 2, (128 - latent[0] % 128) % 128])
    heads, latent_ids = cross_attention(place, by_zy, normed, *tables)

    heads = lax.all_to_all(heads, LAT, split_axis=0, concat_axis=0, tiled=True)
    added = project_columns(heads, by_zy)

    added = lax.all_to_all(added, "z", split_axis=0, concat_axis=0, tiled=True)
    added, outs, qkv = lax.optimization_barrier((added, outs, qkv))
    out_w = [lax.all_gather(w, LAT, axis=0) for w in outs]
    added = added.reshape(BLOCK, WIDTH)
    added = gather_lat(jnp.broadcast_to(added[None], (NX, BLOCK, WIDTH)))

    state, q, kv = dense(
        True, lat_index, added, latent_ids, embed_table, layer_gain, qkv[0], lcos, lsin
    )
    kv = lax.all_to_all(kv, "y", split_axis=0, concat_axis=0, tiled=True)
    y_index = jnp.full((1,), y, jnp.int32)
    heads = attend_latents(False, y_index, q, kv)
    heads = gather_lat(heads)
    state, q, kv = dense(
        False, lat_index, heads, state, out_w[0], layer_gain, qkv[1], lcos, lsin
    )
    kv = lax.all_to_all(kv, "y", split_axis=0, concat_axis=0, tiled=True)
    both = attend_latents(True, y_index, q, kv, state)
    both = lax.all_to_all(both, ("y", "x", "c"), split_axis=0, concat_axis=0, tiled=True)
    return last(both, order_weights(out_w[1]))


def solution(mesh):
    grid = Mesh(np.asarray(mesh.devices).reshape(NZ, NY, NX, NC), ("z", "y", "x", "c"))
    return jax.shard_map(
        body,
        mesh=grid,
        in_specs=(
            P(CTX),
            P(),
            P(),
            P(None, CTX, LAT),
            P(CTX, None),
            P(),
            P(None, None, CTX, LAT),
            P(None, CTX, None),
        ),
        out_specs=P(LAT, None),
        check_vma=False,
    )
```

```python
import functools

import jax
import jax.numpy as jnp
import numpy as np
from jax import lax
from jax.experimental import pallas as pl
from jax.experimental.pallas import tpu as pltpu
from jax.sharding import Mesh
from jax.sharding import PartitionSpec as P

D = 1024
HD = 64
HALF = 32
NZ, NY, NX, NC = 16, 4, 4, 2
NLAT = NX * NC
N = 32768
L = 1024
VOCAB = 256
WIDTH = 128
OWN = 16
LAYERS = 2
PART = 32
BLOCK = 256
KEYS = 2048
STEPS = N // KEYS
LAT = ("x", "c")
CTX = ("z", "y")
BF = jnp.bfloat16
F32 = jnp.float32
MIB = 1 << 20


def inverse_frequencies():
    return 10000.0 ** (-2.0 * jnp.arange(HALF, dtype=F32) / (2 * HALF))


def gather_lat(copies):
    by_x = lax.all_to_all(copies, "x", split_axis=0, concat_axis=0, tiled=True)
    return lax.all_gather(by_x, "c", axis=0)


def pack_kernel(lat_ref, *refs):
    ids_ref, cross_ref, layer_ref, cross_out_ref, layer_out_ref = refs[5:10]
    out_ref, sem = refs[10:]
    copies = [pltpu.make_async_copy(refs[i], refs[i + 5], sem.at[i]) for i in range(5)]
    for copy in copies:
        copy.start()
    for copy in copies:
        copy.wait()
    own = pl.ds(pl.multiple_of(lat_ref[0] * WIDTH, WIDTH), WIDTH)
    out_ref[0:48] = cross_ref[...]
    out_ref[48:64] = cross_out_ref[:, own]
    ids = ids_ref[...].astype(F32)
    out_ref[192:200] = jnp.concatenate([ids, jnp.zeros((4, WIDTH), F32)], axis=0).astype(BF)
    for layer in range(LAYERS):
        start = 64 + layer * 64
        out_ref[start : start + 48] = layer_ref[layer * 48 : (layer + 1) * 48]
        out_ref[start + 48 : start + 64] = layer_out_ref[layer * 16 : (layer + 1) * 16, own]


def pack_shards(lat_index, *operands):
    def kernel(lat_ref, *refs):
        pack_kernel(lat_ref, *refs[:5], *refs[6:11], refs[5], refs[11])

    return pl.pallas_call(
        kernel,
        out_shape=jax.ShapeDtypeStruct((200, WIDTH), BF),
        in_specs=[pl.BlockSpec(memory_space=pltpu.SMEM)] + [pl.BlockSpec(memory_space=pl.ANY)] * 5,
        out_specs=pl.BlockSpec(memory_space=pltpu.VMEM),
        scratch_shapes=[pltpu.VMEM(a.shape, a.dtype) for a in operands]
        + [pltpu.SemaphoreType.DMA((5,))],
        compiler_params=pltpu.CompilerParams(vmem_limit_bytes=58 * MIB),
        name="pack_shards",
    )(lat_index, *operands)


def split_kernel(ref, now_ref):
    ids = [ref[z, 192:200, :].astype(F32)[:4] for z in range(NZ)]
    ids = jnp.concatenate(ids, axis=0).astype(BF)
    for y in range(NY):
        for z in range(NZ):
            now_ref[y, z * 64 : (z + 1) * 64] = ref[z, :64]
        now_ref[y, NZ * 64 :] = ids


def split_round(by_z):
    return pl.pallas_call(
        split_kernel,
        out_shape=jax.ShapeDtypeStruct((NY, NZ * 68, WIDTH), BF),
        compiler_params=pltpu.CompilerParams(vmem_limit_bytes=8 * MIB),
        name="split_round",
    )(by_z)


def project_kernel(heads_ref, w_ref, out_ref):
    heads = jnp.concatenate([heads_ref[i] for i in range(NLAT)], axis=1)
    rows = [w_ref[y, z * 64 + 48 : z * 64 + 64] for z in range(NZ) for y in range(NY)]
    out = dot(heads, jnp.concatenate(rows, axis=0)).astype(BF)
    for z in range(NZ):
        out_ref[z] = out


def project_columns(heads, weights):
    return pl.pallas_call(
        project_kernel,
        out_shape=jax.ShapeDtypeStruct((NZ, OWN, WIDTH), BF),
        compiler_params=pltpu.CompilerParams(vmem_limit_bytes=8 * MIB),
        cost_estimate=pl.CostEstimate(
            flops=2 * OWN * D * WIDTH, bytes_accessed=MIB, transcendentals=0
        ),
        name="project_columns",
    )(heads, weights)


def dot(a, b):
    return jnp.dot(a, b, preferred_element_type=F32)


def dot_nt(a, b):
    return lax.dot_general(a, b, (((1,), (1,)), ((), ())), preferred_element_type=F32)


def split_two(x):
    high = x.astype(BF)
    return high, (x - high.astype(F32)).astype(BF)


def rotate_lanes(x, cosine, sine):
    lane = lax.broadcasted_iota(jnp.int32, x.shape, 1)
    other = jnp.where(lane % HD < HALF, pltpu.roll(x, WIDTH - HALF, 1), pltpu.roll(x, HALF, 1))
    return x * cosine + other * sine


def cross_kernel(
    first_ref, row_ref, turn_ref, w_ref, normed_ref, qcos_ref, qsin_ref, cos_ref, sin_ref,
    out_ref, latent_ref, w_sc, table_sc, q_sc, s_sc, v_sc, ids_sc,
):
    for z in range(NZ):
        for y in range(NY):
            row = (z * NY + y) * 16
            for part in range(3):
                start = z * 64 + part * 16
                w_sc[row : row + 16, part * WIDTH : (part + 1) * WIDTH] = w_ref[
                    y, start : start + 16, :
                ]
    for y in range(NY):
        ids = w_ref[y, NZ * 64 :, :].astype(F32)
        for z in range(NZ):
            ids_sc[z, y * 4 : (y + 1) * 4] = ids[z * 4 : (z + 1) * 4]
    latents = jnp.concatenate([ids_sc[NZ - 1, 8:12], ids_sc[NZ - 1, 12:16]], axis=0)
    latent_ref[...] = latents
    turned = pltpu.roll(latents, turn_ref[0], 1)
    here = lax.broadcasted_iota(jnp.int32, turned.shape, 0) == row_ref[0]
    own = jnp.sum(jnp.where(here, turned, 0.0), axis=0, keepdims=True)
    token = lax.broadcasted_iota(jnp.int32, (VOCAB, 128), 0).astype(F32)
    pick = jnp.where(token == own, 1.0, 0.0).T[:OWN].astype(BF)
    normed = normed_ref[...]
    table_sc[...] = dot(normed, w_sc[:, WIDTH:]).T.astype(BF)
    rows = dot(pick, normed).astype(BF)
    query = dot(rows, w_sc[:, :WIDTH]) * (HD**-0.5)
    lane = lax.broadcasted_iota(jnp.int32, query.shape, 1)
    for step in range(STEPS):
        block = slice(step * OWN, (step + 1) * OWN)
        turned = rotate_lanes(query, qcos_ref[block], qsin_ref[block])
        q_sc[step, :OWN] = jnp.where(lane < HD, turned, 0.0).astype(BF)
        q_sc[step, OWN:] = jnp.where(lane < HD, 0.0, turned).astype(BF)
    token = token.astype(BF)
    qpos = lax.broadcasted_iota(jnp.int32, (2 * OWN, 1), 0) % OWN + (N - L) + first_ref[0]

    def scores_of(step, top):
        hot = []
        ids = ids_sc[step]
        for r in range(16):
            row = jnp.broadcast_to(ids[r : r + 1, :], (VOCAB, 128)).astype(BF)
            hot.append(jnp.where(token == row, jnp.ones((), BF), jnp.zeros((), BF)))
        both = dot(table_sc[...], jnp.concatenate(hot, axis=1))
        v_sc[step] = both[WIDTH:].astype(BF)
        cosine, sine = cos_ref[...], sin_ref[...]
        pieces = []
        for head in range(2):
            first = both[head * HD : head * HD + HALF]
            second = both[head * HD + HALF : (head + 1) * HD]
            pieces.append(first * cosine - second * sine)
            pieces.append(second * cosine + first * sine)
        scores = dot(q_sc[step], jnp.concatenate(pieces, axis=0).astype(BF))
        kpos = step * KEYS + lax.broadcasted_iota(jnp.int32, scores.shape, 1)
        scores = jnp.where(kpos <= qpos, scores, -1e30)
        s_sc[step] = scores
        for i in range(KEYS // 128):
            top = jnp.maximum(top, scores[:, i * 128 : (i + 1) * 128])
        return top

    top = lax.fori_loop(0, STEPS, scores_of, jnp.full((2 * OWN, 128), -1e30, F32), unroll=8)
    most = jnp.max(top, axis=1, keepdims=True)

    def values_of(step, carry):
        total, acc = carry
        weight = jnp.exp(s_sc[step] - most)
        for i in range(KEYS // 128):
            total = total + weight[:, i * 128 : (i + 1) * 128]
        return total, acc + dot_nt(v_sc[step], weight.astype(BF))

    total, acc = lax.fori_loop(
        0, STEPS, values_of, (jnp.zeros((2 * OWN, 128), F32), jnp.zeros((WIDTH, 2 * OWN), F32)),
        unroll=8,
    )
    value = acc.T / jnp.sum(total, axis=1, keepdims=True)
    lane = lax.broadcasted_iota(jnp.int32, (OWN, WIDTH), 1)
    value = jnp.where(lane < HD, value[:OWN], value[OWN:]).astype(BF)
    for i in range(NLAT):
        out_ref[i] = value


def cross_attention(*operands):
    return pl.pallas_call(
        cross_kernel,
        out_shape=(
            jax.ShapeDtypeStruct((NLAT, OWN, WIDTH), BF),
            jax.ShapeDtypeStruct((8, 128), F32),
        ),
        in_specs=[pl.BlockSpec(memory_space=pltpu.SMEM)] * 3
        + [pl.BlockSpec(memory_space=pltpu.VMEM)] * (len(operands) - 3),
        scratch_shapes=[
            pltpu.VMEM((D, 3 * WIDTH), BF),
            pltpu.VMEM((2 * WIDTH, VOCAB), BF),
            pltpu.VMEM((STEPS, 2 * OWN, WIDTH), BF),
            pltpu.VMEM((STEPS, 2 * OWN, KEYS), F32),
            pltpu.VMEM((STEPS, WIDTH, KEYS), BF),
            pltpu.VMEM((NZ, 16, 128), F32),
        ],
        compiler_params=pltpu.CompilerParams(vmem_limit_bytes=20 * MIB),
        cost_estimate=pl.CostEstimate(
            flops=MIB, bytes_accessed=MIB, transcendentals=0
        ),
        name="cross_attention",
    )(*operands)


def out_weights(ref):
    columns = []
    for i in range(NLAT):
        rows = [ref[i, y, z] for z in range(NZ) for y in range(NY)]
        columns.append(jnp.concatenate(rows, axis=0))
    return jnp.concatenate(columns, axis=1)


def dense_kernel(first, *refs):
    lat_ref, turn_ref, parts_ref, state_ref, matrix_ref, gain_ref, qkv_ref, cos_ref, sin_ref = refs[:9]
    state_out, q_out, kv_out = refs[9:12]
    parts = jnp.concatenate([parts_ref[i % NC, i // NC] for i in range(NLAT)], axis=1)
    if first:
        ids = pltpu.roll(state_ref[...], turn_ref[0], 1)
        ids = jnp.concatenate([ids[i : i + 1, :PART] for i in range(NLAT)], axis=1)
        token = lax.broadcasted_iota(jnp.int32, (VOCAB, BLOCK), 0).astype(F32)
        hot = jnp.where(token == ids, 1.0, 0.0).T.astype(BF)
        state = dot(hot, matrix_ref[...]) + parts.astype(F32)
        state_out[...] = state
    else:
        state = state_ref[...] + dot(parts, out_weights(matrix_ref))
        state_sc = refs[12]
        state_sc[...] = state
        own = pl.ds(pl.multiple_of(lat_ref[0] * WIDTH, WIDTH), WIDTH)
        state_out[...] = state_sc[:, own].astype(BF)
    scale = lax.rsqrt(jnp.mean(state * state, axis=1, keepdims=True) + 1e-06)
    normed = (state * scale * gain_ref[0 if first else 1, :][None]).astype(BF)
    cosine, sine = cos_ref[...], sin_ref[...]
    weights = [
        jnp.concatenate(
            [qkv_ref[y, z, i * 16 : (i + 1) * 16] for z in range(NZ) for y in range(NY)], axis=0
        )
        for i in range(3)
    ]
    product = dot(normed, jnp.concatenate(weights, axis=1))
    q_out[...] = rotate_lanes(product[:, :WIDTH], cosine, sine).astype(BF)
    k = rotate_lanes(product[:, WIDTH : 2 * WIDTH], cosine, sine).astype(BF)
    v = product[:, 2 * WIDTH :].astype(BF)
    for y in range(NY):
        kv_out[y, :, :WIDTH] = k
        kv_out[y, :, WIDTH:] = v


def dense(first, *operands):
    smem, vmem = (pl.BlockSpec(memory_space=m) for m in (pltpu.SMEM, pltpu.VMEM))
    return pl.pallas_call(
        functools.partial(dense_kernel, first),
        out_shape=(
            jax.ShapeDtypeStruct((BLOCK, D), F32)
            if first
            else jax.ShapeDtypeStruct((BLOCK, WIDTH), BF),
            jax.ShapeDtypeStruct((BLOCK, WIDTH), BF),
            jax.ShapeDtypeStruct((NY, BLOCK, 2 * WIDTH), BF),
        ),
        in_specs=[smem] * 2 + [vmem] * 7,
        scratch_shapes=[] if first else [pltpu.VMEM((BLOCK, D), F32)],
        compiler_params=pltpu.CompilerParams(vmem_limit_bytes=16 * MIB),
        cost_estimate=pl.CostEstimate(
            flops=2 * BLOCK * D * (D + 3 * WIDTH), bytes_accessed=8 * MIB, transcendentals=BLOCK
        ),
        name="dense",
    )(*operands)


def key_positions():
    column = lax.broadcasted_iota(jnp.int32, (1, L), 1)
    return (column % BLOCK) // PART * 128 + column // BLOCK * PART + column % PART


def attend(q, k, v, qpos, kpos):
    outs = []
    seen = kpos <= qpos
    for head in range(2):
        lanes = slice(head * HD, (head + 1) * HD)
        scores = dot_nt(q[:, lanes], k[:, lanes]) * (HD**-0.5)
        scores = jnp.where(seen, scores, -1e30)
        weight = jnp.exp(scores - jnp.max(scores, axis=1, keepdims=True))
        total = jnp.sum(weight, axis=1, keepdims=True)
        outs.append(dot(weight.astype(BF), v[:, lanes]) / total)
    return jnp.concatenate(outs, axis=1).astype(BF)


def attend_kernel(final, y_ref, q_ref, kv_ref, *refs):
    out_ref = refs[-1]
    row = lax.broadcasted_iota(jnp.int32, (BLOCK, 1), 0)
    qpos = row // PART * 128 + y_ref[0] * PART + row % PART
    kv = jnp.concatenate([kv_ref[i] for i in range(NY)], axis=0)
    out = attend(q_ref[...], kv[:, :WIDTH], kv[:, WIDTH:], qpos, key_positions())
    if final:
        state = refs[0][...]
        for y in range(NY):
            for i in range(NLAT):
                out_ref[y * NLAT + i, :PART] = out[i * PART : (i + 1) * PART]
                out_ref[y * NLAT + i, PART:] = state[i * PART : (i + 1) * PART]
    else:
        for i in range(NX):
            out_ref[i] = out


def attend_latents(final, *operands):
    shape = (NY * NLAT, 2 * PART, WIDTH) if final else (NX, BLOCK, WIDTH)
    smem, vmem = (pl.BlockSpec(memory_space=m) for m in (pltpu.SMEM, pltpu.VMEM))
    return pl.pallas_call(
        functools.partial(attend_kernel, final),
        out_shape=jax.ShapeDtypeStruct(shape, BF),
        in_specs=[smem] + [vmem] * (len(operands) - 1),
        compiler_params=pltpu.CompilerParams(vmem_limit_bytes=12 * MIB),
        cost_estimate=pl.CostEstimate(
            flops=8 * BLOCK * L * HD, bytes_accessed=2 * MIB, transcendentals=2 * BLOCK * L
        ),
        name="attend_latents",
    )(*operands)


def order_kernel(ref, out_ref):
    for i in range(NLAT):
        out_ref[:, i * WIDTH : (i + 1) * WIDTH] = jnp.concatenate(
            [ref[i, y, z] for z in range(NZ) for y in range(NY)], axis=0
        )


def order_weights(out_w):
    return pl.pallas_call(
        order_kernel,
        out_shape=jax.ShapeDtypeStruct((D, D), BF),
        compiler_params=pltpu.CompilerParams(vmem_limit_bytes=8 * MIB),
        name="order_weights",
    )(out_w)


def last_kernel(both_ref, out_w_ref, out_ref):
    heads, state = (
        jnp.concatenate(
            [
                jnp.concatenate(
                    [both_ref[y * NLAT + i, half * PART : (half + 1) * PART] for i in range(NLAT)],
                    axis=1,
                )
                for y in range(NY)
            ],
            axis=0,
        )
        for half in range(2)
    )
    out_ref[...] = state.astype(F32) + dot(heads, out_w_ref[...])


def last(both, out_w):
    return pl.pallas_call(
        last_kernel,
        out_shape=jax.ShapeDtypeStruct((128, D), F32),
        compiler_params=pltpu.CompilerParams(vmem_limit_bytes=16 * MIB),
        cost_estimate=pl.CostEstimate(
            flops=2 * 128 * D * D, bytes_accessed=4 * MIB, transcendentals=0
        ),
        name="last",
    )(both, out_w)


def head_angles(positions, inverse):
    angle = positions.astype(F32)[:, None] * inverse[None, :]
    cosine, sine = jnp.cos(angle), jnp.sin(angle)
    return (
        jnp.concatenate([cosine] * 4, axis=1),
        jnp.concatenate([-sine, sine, -sine, sine], axis=1),
    )


def body(token_ids, embed_table, input_gain, cross_qkv, cross_out, layer_gain, layer_qkv, layer_out):
    z, y = lax.axis_index("z"), lax.axis_index("y")
    lat = lax.axis_index(LAT)

    lat_index = jnp.full((1,), lat, jnp.int32)
    turn = (128 - y * PART) % 128
    pack = pack_shards(
        lat_index, token_ids.reshape(4, 128), cross_qkv.reshape(48, WIDTH),
        layer_qkv.reshape(96, WIDTH), cross_out, layer_out.reshape(32, D),
    )
    by_z = lax.all_gather(pack, "z", axis=0)
    by_z, inverse, embed_table, input_gain = lax.optimization_barrier(
        (by_z, inverse_frequencies(), embed_table, input_gain)
    )
    now = split_round(by_z)
    by_zy = lax.all_to_all(now, "y", split_axis=0, concat_axis=0, tiled=True)

    latent = jnp.arange(OWN, dtype=jnp.int32) + (z // 2) * 128 + y * PART + (z % 2) * OWN
    offset = N - L + latent[None, :] - KEYS * jnp.arange(STEPS, dtype=jnp.int32)[:, None]
    qcos, qsin = head_angles(offset.reshape(STEPS * OWN), inverse)
    row = jnp.arange(BLOCK, dtype=jnp.int32)
    lpos = row // PART * 128 + y * PART + row % PART
    lcos, lsin = head_angles(lpos, inverse)
    fine = inverse[:, None] * jnp.arange(KEYS, dtype=F32)[None, :]
    tables = (qcos, qsin, jnp.cos(fine), jnp.sin(fine))
    wide = embed_table.astype(F32)
    normed = wide * lax.rsqrt(jnp.mean(wide * wide, axis=-1, keepdims=True) + 1e-06) * input_gain
    normed = normed.astype(BF)
    by_zy, rest_z, normed, tables, lcos, lsin = lax.optimization_barrier(
        (by_zy, by_z[:, 64:192], normed, tables, lcos, lsin)
    )
    rest_zy = lax.all_gather(rest_z, "y", axis=0)
    outs = [rest_zy[:, :, 64 * i + 48 : 64 * i + 64] for i in range(LAYERS)]
    qkv = [rest_zy[:, :, 64 * i : 64 * i + 48] for i in range(LAYERS)]
    first = (z // 2) * 128 + y * PART + (z % 2) * OWN
    place = [jnp.full((1,), i, jnp.int32) for i in (first, z // 2, (128 - first % 128) % 128)]
    heads, latent_ids = cross_attention(*place, by_zy, normed, *tables)

    heads = lax.all_to_all(heads, LAT, split_axis=0, concat_axis=0, tiled=True)
    added = project_columns(heads, by_zy)

    added = lax.all_to_all(added, "z", split_axis=0, concat_axis=0, tiled=True)
    added, outs, qkv, turn = lax.optimization_barrier((added, outs, qkv, turn))
    turn = jnp.full((1,), turn, jnp.int32)
    out_w = [lax.all_gather(w, LAT, axis=0) for w in outs]
    added = added.reshape(BLOCK, WIDTH)
    added = gather_lat(jnp.broadcast_to(added[None], (NX, BLOCK, WIDTH)))

    state, q, kv = dense(
        True, lat_index, turn, added, latent_ids, embed_table, layer_gain, qkv[0], lcos, lsin
    )
    kv = lax.all_to_all(kv, "y", split_axis=0, concat_axis=0, tiled=True)
    y_index = jnp.full((1,), y, jnp.int32)
    heads = attend_latents(False, y_index, q, kv)
    heads = gather_lat(heads)
    state, q, kv = dense(
        False, lat_index, turn, heads, state, out_w[0], layer_gain, qkv[1], lcos, lsin
    )
    kv = lax.all_to_all(kv, "y", split_axis=0, concat_axis=0, tiled=True)
    both = attend_latents(True, y_index, q, kv, state)
    both = lax.all_to_all(both, ("y", "x", "c"), split_axis=0, concat_axis=0, tiled=True)
    return last(both, order_weights(out_w[1]))


def solution(mesh):
    grid = Mesh(np.asarray(mesh.devices).reshape(NZ, NY, NX, NC), ("z", "y", "x", "c"))
    return jax.shard_map(
        body,
        mesh=grid,
        in_specs=(
            P(CTX),
            P(),
            P(),
            P(None, CTX, LAT),
            P(CTX, None),
            P(),
            P(None, None, CTX, LAT),
            P(None, CTX, None),
        ),
        out_specs=P(LAT, None),
        check_vma=False,
    )
```

```python
import functools

import jax
import jax.numpy as jnp
import numpy as np
from jax import lax
from jax.experimental import pallas as pl
from jax.experimental.pallas import tpu as pltpu
from jax.sharding import Mesh
from jax.sharding import PartitionSpec as P

D = 1024
HD = 64
HALF = 32
NZ, NY, NX, NC = 16, 4, 4, 2
NLAT = NX * NC
N = 32768
L = 1024
VOCAB = 256
WIDTH = 128
OWN = 16
LAYERS = 2
PART = 32
BLOCK = 256
KEYS = 2048
STEPS = N // KEYS
LAT = ("x", "c")
CTX = ("z", "y")
BF = jnp.bfloat16
F32 = jnp.float32
MIB = 1 << 20


def inverse_frequencies():
    return 10000.0 ** (-2.0 * jnp.arange(HALF, dtype=F32) / (2 * HALF))


def gather_lat(copies):
    by_x = lax.all_to_all(copies, "x", split_axis=0, concat_axis=0, tiled=True)
    return lax.all_gather(by_x, "c", axis=0)


def pack_kernel(lat_ref, *refs):
    ids_ref, cross_ref, layer_ref, cross_out_ref, layer_out_ref = refs[5:10]
    out_ref, sem = refs[10:]
    copies = [pltpu.make_async_copy(refs[i], refs[i + 5], sem.at[i]) for i in range(5)]
    for copy in copies:
        copy.start()
    for copy in copies:
        copy.wait()
    own = pl.ds(pl.multiple_of(lat_ref[0] * WIDTH, WIDTH), WIDTH)
    out_ref[0:48] = cross_ref[...]
    out_ref[48:64] = cross_out_ref[:, own]
    ids = ids_ref[...].astype(F32)
    out_ref[192:200] = jnp.concatenate([ids, jnp.zeros((4, WIDTH), F32)], axis=0).astype(BF)
    for layer in range(LAYERS):
        start = 64 + layer * 64
        out_ref[start : start + 48] = layer_ref[layer * 48 : (layer + 1) * 48]
        out_ref[start + 48 : start + 64] = layer_out_ref[layer * 16 : (layer + 1) * 16, own]


def pack_shards(lat_index, *operands):
    def kernel(lat_ref, *refs):
        pack_kernel(lat_ref, *refs[:5], *refs[6:11], refs[5], refs[11])

    return pl.pallas_call(
        kernel,
        out_shape=jax.ShapeDtypeStruct((200, WIDTH), BF),
        in_specs=[pl.BlockSpec(memory_space=pltpu.SMEM)] + [pl.BlockSpec(memory_space=pl.ANY)] * 5,
        out_specs=pl.BlockSpec(memory_space=pltpu.VMEM),
        scratch_shapes=[pltpu.VMEM(a.shape, a.dtype) for a in operands]
        + [pltpu.SemaphoreType.DMA((5,))],
        compiler_params=pltpu.CompilerParams(vmem_limit_bytes=58 * MIB),
        name="pack_shards",
    )(lat_index, *operands)


def split_kernel(ref, now_ref):
    ids = [ref[z, 192:200, :].astype(F32)[:4] for z in range(NZ)]
    ids = jnp.concatenate(ids, axis=0).astype(BF)
    for y in range(NY):
        for z in range(NZ):
            now_ref[y, z * 64 : (z + 1) * 64] = ref[z, :64]
        now_ref[y, NZ * 64 :] = ids


def split_round(by_z):
    return pl.pallas_call(
        split_kernel,
        out_shape=jax.ShapeDtypeStruct((NY, NZ * 68, WIDTH), BF),
        compiler_params=pltpu.CompilerParams(vmem_limit_bytes=8 * MIB),
        name="split_round",
    )(by_z)


def project_kernel(heads_ref, w_ref, out_ref):
    heads = jnp.concatenate([heads_ref[i] for i in range(NLAT)], axis=1)
    rows = [w_ref[y, z * 64 + 48 : z * 64 + 64] for z in range(NZ) for y in range(NY)]
    out = dot(heads, jnp.concatenate(rows, axis=0)).astype(BF)
    for z in range(NZ):
        out_ref[z] = out


def project_columns(heads, weights):
    return pl.pallas_call(
        project_kernel,
        out_shape=jax.ShapeDtypeStruct((NZ, OWN, WIDTH), BF),
        compiler_params=pltpu.CompilerParams(vmem_limit_bytes=8 * MIB),
        cost_estimate=pl.CostEstimate(
            flops=2 * OWN * D * WIDTH, bytes_accessed=MIB, transcendentals=0
        ),
        name="project_columns",
    )(heads, weights)


def dot(a, b):
    return jnp.dot(a, b, preferred_element_type=F32)


def dot_nt(a, b):
    return lax.dot_general(a, b, (((1,), (1,)), ((), ())), preferred_element_type=F32)


def split_two(x):
    high = x.astype(BF)
    return high, (x - high.astype(F32)).astype(BF)


def rotate_lanes(x, cosine, sine):
    lane = lax.broadcasted_iota(jnp.int32, x.shape, 1)
    other = jnp.where(lane % HD < HALF, pltpu.roll(x, WIDTH - HALF, 1), pltpu.roll(x, HALF, 1))
    return x * cosine + other * sine


def cross_kernel(
    first_ref, row_ref, turn_ref, w_ref, normed_ref, qcos_ref, qsin_ref, cos_ref, sin_ref,
    out_ref, latent_ref, w_sc, table_sc, q_sc, s_sc, v_sc, ids_sc,
):
    for z in range(NZ):
        for y in range(NY):
            row = (z * NY + y) * 16
            for part in range(3):
                start = z * 64 + part * 16
                w_sc[row : row + 16, part * WIDTH : (part + 1) * WIDTH] = w_ref[
                    y, start : start + 16, :
                ]
    for y in range(NY):
        ids = w_ref[y, NZ * 64 :, :].astype(F32)
        for z in range(NZ):
            ids_sc[z, y * 4 : (y + 1) * 4] = ids[z * 4 : (z + 1) * 4]
    latents = jnp.concatenate([ids_sc[NZ - 1, 8:12], ids_sc[NZ - 1, 12:16]], axis=0)
    latent_ref[...] = latents
    turned = pltpu.roll(latents, turn_ref[0], 1)
    here = lax.broadcasted_iota(jnp.int32, turned.shape, 0) == row_ref[0]
    own = jnp.sum(jnp.where(here, turned, 0.0), axis=0, keepdims=True)
    token = lax.broadcasted_iota(jnp.int32, (VOCAB, 128), 0).astype(F32)
    pick = jnp.where(token == own, 1.0, 0.0).T[:OWN].astype(BF)
    normed = normed_ref[...]
    table_sc[...] = dot(normed, w_sc[:, WIDTH:]).T.astype(BF)
    rows = dot(pick, normed).astype(BF)
    query = dot(rows, w_sc[:, :WIDTH]) * (HD**-0.5)
    lane = lax.broadcasted_iota(jnp.int32, query.shape, 1)
    for step in range(STEPS):
        block = slice(step * OWN, (step + 1) * OWN)
        turned = rotate_lanes(query, qcos_ref[block], qsin_ref[block])
        q_sc[step, :OWN] = jnp.where(lane < HD, turned, 0.0).astype(BF)
        q_sc[step, OWN:] = jnp.where(lane < HD, 0.0, turned).astype(BF)
    token = token.astype(BF)
    qpos = lax.broadcasted_iota(jnp.int32, (2 * OWN, 1), 0) % OWN + (N - L) + first_ref[0]

    def scores_of(step, top):
        hot = []
        ids = ids_sc[step]
        for r in range(16):
            row = jnp.broadcast_to(ids[r : r + 1, :], (VOCAB, 128)).astype(BF)
            hot.append(jnp.where(token == row, jnp.ones((), BF), jnp.zeros((), BF)))
        both = dot(table_sc[...], jnp.concatenate(hot, axis=1))
        v_sc[step] = both[WIDTH:].astype(BF)
        cosine, sine = cos_ref[...], sin_ref[...]
        pieces = []
        for head in range(2):
            first = both[head * HD : head * HD + HALF]
            second = both[head * HD + HALF : (head + 1) * HD]
            pieces.append(first * cosine - second * sine)
            pieces.append(second * cosine + first * sine)
        scores = dot(q_sc[step], jnp.concatenate(pieces, axis=0).astype(BF))
        kpos = step * KEYS + lax.broadcasted_iota(jnp.int32, scores.shape, 1)
        scores = jnp.where(kpos <= qpos, scores, -1e30)
        s_sc[step] = scores
        for i in range(KEYS // 128):
            top = jnp.maximum(top, scores[:, i * 128 : (i + 1) * 128])
        return top

    top = lax.fori_loop(0, STEPS, scores_of, jnp.full((2 * OWN, 128), -1e30, F32), unroll=8)
    most = jnp.max(top, axis=1, keepdims=True)

    def values_of(step, carry):
        total, acc = carry
        weight = jnp.exp(s_sc[step] - most)
        for i in range(KEYS // 128):
            total = total + weight[:, i * 128 : (i + 1) * 128]
        return total, acc + dot_nt(v_sc[step], weight.astype(BF))

    total, acc = lax.fori_loop(
        0, STEPS, values_of, (jnp.zeros((2 * OWN, 128), F32), jnp.zeros((WIDTH, 2 * OWN), F32)),
        unroll=8,
    )
    value = acc.T / jnp.sum(total, axis=1, keepdims=True)
    lane = lax.broadcasted_iota(jnp.int32, (OWN, WIDTH), 1)
    value = jnp.where(lane < HD, value[:OWN], value[OWN:]).astype(BF)
    for i in range(NLAT):
        out_ref[i] = value


def cross_attention(*operands):
    return pl.pallas_call(
        cross_kernel,
        out_shape=(
            jax.ShapeDtypeStruct((NLAT, OWN, WIDTH), BF),
            jax.ShapeDtypeStruct((8, 128), F32),
        ),
        in_specs=[pl.BlockSpec(memory_space=pltpu.SMEM)] * 3
        + [pl.BlockSpec(memory_space=pltpu.VMEM)] * (len(operands) - 3),
        scratch_shapes=[
            pltpu.VMEM((D, 3 * WIDTH), BF),
            pltpu.VMEM((2 * WIDTH, VOCAB), BF),
            pltpu.VMEM((STEPS, 2 * OWN, WIDTH), BF),
            pltpu.VMEM((STEPS, 2 * OWN, KEYS), F32),
            pltpu.VMEM((STEPS, WIDTH, KEYS), BF),
            pltpu.VMEM((NZ, 16, 128), F32),
        ],
        compiler_params=pltpu.CompilerParams(vmem_limit_bytes=20 * MIB),
        cost_estimate=pl.CostEstimate(
            flops=MIB, bytes_accessed=MIB, transcendentals=0
        ),
        name="cross_attention",
    )(*operands)


def out_weights(ref):
    columns = []
    for i in range(NLAT):
        rows = [ref[i, y, z] for z in range(NZ) for y in range(NY)]
        columns.append(jnp.concatenate(rows, axis=0))
    return jnp.concatenate(columns, axis=1)


def dense_kernel(first, *refs):
    lat_ref, turn_ref, parts_ref, state_ref, matrix_ref, gain_ref, qkv_ref, cos_ref, sin_ref = refs[:9]
    state_out, q_out, kv_out = refs[9:12]
    parts = jnp.concatenate([parts_ref[i % NC, i // NC] for i in range(NLAT)], axis=1)
    if first:
        ids = pltpu.roll(state_ref[...], turn_ref[0], 1)
        ids = jnp.concatenate([ids[i : i + 1, :PART] for i in range(NLAT)], axis=1)
        token = lax.broadcasted_iota(jnp.int32, (VOCAB, BLOCK), 0).astype(F32)
        hot = jnp.where(token == ids, 1.0, 0.0).T.astype(BF)
        state = dot(hot, matrix_ref[...]) + parts.astype(F32)
        state_out[...] = state
    else:
        state = state_ref[...] + dot(parts, out_weights(matrix_ref))
        state_sc = refs[12]
        state_sc[...] = state
        own = pl.ds(pl.multiple_of(lat_ref[0] * WIDTH, WIDTH), WIDTH)
        state_out[...] = state_sc[:, own].astype(BF)
    scale = lax.rsqrt(jnp.mean(state * state, axis=1, keepdims=True) + 1e-06)
    normed = (state * scale * gain_ref[0 if first else 1, :][None]).astype(BF)
    cosine, sine = cos_ref[...], sin_ref[...]
    weights = [
        jnp.concatenate(
            [qkv_ref[y, z, i * 16 : (i + 1) * 16] for z in range(NZ) for y in range(NY)], axis=0
        )
        for i in range(3)
    ]
    product = dot(normed, jnp.concatenate(weights, axis=1))
    q_out[...] = rotate_lanes(product[:, :WIDTH], cosine, sine).astype(BF)
    k = rotate_lanes(product[:, WIDTH : 2 * WIDTH], cosine, sine).astype(BF)
    v = product[:, 2 * WIDTH :].astype(BF)
    for y in range(NY):
        kv_out[y, :, :WIDTH] = k
        kv_out[y, :, WIDTH:] = v


def dense(first, *operands):
    smem, vmem = (pl.BlockSpec(memory_space=m) for m in (pltpu.SMEM, pltpu.VMEM))
    return pl.pallas_call(
        functools.partial(dense_kernel, first),
        out_shape=(
            jax.ShapeDtypeStruct((BLOCK, D), F32)
            if first
            else jax.ShapeDtypeStruct((BLOCK, WIDTH), BF),
            jax.ShapeDtypeStruct((BLOCK, WIDTH), BF),
            jax.ShapeDtypeStruct((NY, BLOCK, 2 * WIDTH), BF),
        ),
        in_specs=[smem] * 2 + [vmem] * 7,
        scratch_shapes=[] if first else [pltpu.VMEM((BLOCK, D), F32)],
        compiler_params=pltpu.CompilerParams(vmem_limit_bytes=16 * MIB),
        cost_estimate=pl.CostEstimate(
            flops=2 * BLOCK * D * (D + 3 * WIDTH), bytes_accessed=8 * MIB, transcendentals=BLOCK
        ),
        name="dense",
    )(*operands)


def key_positions():
    column = lax.broadcasted_iota(jnp.int32, (1, L), 1)
    return (column % BLOCK) // PART * 128 + column // BLOCK * PART + column % PART


def attend(q, k, v, qpos, kpos):
    outs = []
    seen = kpos <= qpos
    for head in range(2):
        lanes = slice(head * HD, (head + 1) * HD)
        scores = dot_nt(q[:, lanes], k[:, lanes]) * (HD**-0.5)
        scores = jnp.where(seen, scores, -1e30)
        weight = jnp.exp(scores - jnp.max(scores, axis=1, keepdims=True))
        total = jnp.sum(weight, axis=1, keepdims=True)
        outs.append(dot(weight.astype(BF), v[:, lanes]) / total)
    return jnp.concatenate(outs, axis=1).astype(BF)


def attend_kernel(final, y_ref, q_ref, kv_ref, *refs):
    out_ref = refs[-1]
    row = lax.broadcasted_iota(jnp.int32, (BLOCK, 1), 0)
    qpos = row // PART * 128 + y_ref[0] * PART + row % PART
    kv = jnp.concatenate([kv_ref[i] for i in range(NY)], axis=0)
    out = attend(q_ref[...], kv[:, :WIDTH], kv[:, WIDTH:], qpos, key_positions())
    if final:
        state = refs[0][...]
        for y in range(NY):
            for i in range(NLAT):
                out_ref[y * NLAT + i, :PART] = out[i * PART : (i + 1) * PART]
                out_ref[y * NLAT + i, PART:] = state[i * PART : (i + 1) * PART]
    else:
        for i in range(NX):
            out_ref[i] = out


def attend_latents(final, *operands):
    shape = (NY * NLAT, 2 * PART, WIDTH) if final else (NX, BLOCK, WIDTH)
    smem, vmem = (pl.BlockSpec(memory_space=m) for m in (pltpu.SMEM, pltpu.VMEM))
    return pl.pallas_call(
        functools.partial(attend_kernel, final),
        out_shape=jax.ShapeDtypeStruct(shape, BF),
        in_specs=[smem] + [vmem] * (len(operands) - 1),
        compiler_params=pltpu.CompilerParams(vmem_limit_bytes=12 * MIB),
        cost_estimate=pl.CostEstimate(
            flops=8 * BLOCK * L * HD, bytes_accessed=2 * MIB, transcendentals=2 * BLOCK * L
        ),
        name="attend_latents",
    )(*operands)


def order_kernel(ref, out_ref):
    for i in range(NLAT):
        out_ref[:, i * WIDTH : (i + 1) * WIDTH] = jnp.concatenate(
            [ref[i, y, z] for z in range(NZ) for y in range(NY)], axis=0
        )


def order_weights(out_w):
    return pl.pallas_call(
        order_kernel,
        out_shape=jax.ShapeDtypeStruct((D, D), BF),
        compiler_params=pltpu.CompilerParams(vmem_limit_bytes=8 * MIB),
        name="order_weights",
    )(out_w)


def last_kernel(both_ref, out_w_ref, out_ref):
    heads, state = (
        jnp.concatenate(
            [
                jnp.concatenate(
                    [both_ref[y * NLAT + i, half * PART : (half + 1) * PART] for i in range(NLAT)],
                    axis=1,
                )
                for y in range(NY)
            ],
            axis=0,
        )
        for half in range(2)
    )
    out_ref[...] = state.astype(F32) + dot(heads, out_w_ref[...])


def last(both, out_w):
    return pl.pallas_call(
        last_kernel,
        out_shape=jax.ShapeDtypeStruct((128, D), F32),
        compiler_params=pltpu.CompilerParams(vmem_limit_bytes=16 * MIB),
        cost_estimate=pl.CostEstimate(
            flops=2 * 128 * D * D, bytes_accessed=4 * MIB, transcendentals=0
        ),
        name="last",
    )(both, out_w)


def head_angles(positions, inverse):
    angle = positions.astype(F32)[:, None] * inverse[None, :]
    cosine, sine = jnp.cos(angle), jnp.sin(angle)
    return (
        jnp.concatenate([cosine] * 4, axis=1),
        jnp.concatenate([-sine, sine, -sine, sine], axis=1),
    )


def body(token_ids, embed_table, input_gain, cross_qkv, cross_out, layer_gain, layer_qkv, layer_out):
    z, y = lax.axis_index("z"), lax.axis_index("y")
    lat = lax.axis_index(LAT)

    lat_index = jnp.full((1,), lat, jnp.int32)
    turn = (128 - y * PART) % 128
    pack = pack_shards(
        lat_index, token_ids.reshape(4, 128), cross_qkv.reshape(48, WIDTH),
        layer_qkv.reshape(96, WIDTH), cross_out, layer_out.reshape(32, D),
    )
    by_z = lax.all_gather(pack, "z", axis=0)
    by_z, inverse, embed_table, input_gain = lax.optimization_barrier(
        (by_z, inverse_frequencies(), embed_table, input_gain)
    )
    now = split_round(by_z)
    by_zy = lax.all_to_all(now, "y", split_axis=0, concat_axis=0, tiled=True)

    latent = jnp.arange(OWN, dtype=jnp.int32) + (z // 2) * 128 + y * PART + (z % 2) * OWN
    offset = N - L + latent[None, :] - KEYS * jnp.arange(STEPS, dtype=jnp.int32)[:, None]
    qcos, qsin = head_angles(offset.reshape(STEPS * OWN), inverse)
    row = jnp.arange(BLOCK, dtype=jnp.int32)
    lpos = row // PART * 128 + y * PART + row % PART
    lcos, lsin = head_angles(lpos, inverse)
    fine = inverse[:, None] * jnp.arange(KEYS, dtype=F32)[None, :]
    tables = (qcos, qsin, jnp.cos(fine), jnp.sin(fine))
    wide = embed_table.astype(F32)
    normed = wide * lax.rsqrt(jnp.mean(wide * wide, axis=-1, keepdims=True) + 1e-06) * input_gain
    normed = normed.astype(BF)
    by_zy, rest_z, normed, tables, lcos, lsin, turn, y = lax.optimization_barrier(
        (by_zy, by_z[:, 64:192], normed, tables, lcos, lsin, turn, y)
    )
    turn = jnp.full((1,), turn, jnp.int32)
    y_index = jnp.full((1,), y, jnp.int32)
    rest_zy = lax.all_gather(rest_z, "y", axis=0)
    outs = [rest_zy[:, :, 64 * i + 48 : 64 * i + 64] for i in range(LAYERS)]
    qkv = [rest_zy[:, :, 64 * i : 64 * i + 48] for i in range(LAYERS)]
    first = (z // 2) * 128 + y * PART + (z % 2) * OWN
    place = [jnp.full((1,), i, jnp.int32) for i in (first, z // 2, (128 - first % 128) % 128)]
    heads, latent_ids = cross_attention(*place, by_zy, normed, *tables)

    heads = lax.all_to_all(heads, LAT, split_axis=0, concat_axis=0, tiled=True)
    added = project_columns(heads, by_zy)

    added = lax.all_to_all(added, "z", split_axis=0, concat_axis=0, tiled=True)
    added, outs, qkv = lax.optimization_barrier((added, outs, qkv))
    out_w = [lax.all_gather(w, LAT, axis=0) for w in outs]
    added = added.reshape(BLOCK, WIDTH)
    added = gather_lat(jnp.broadcast_to(added[None], (NX, BLOCK, WIDTH)))

    state, q, kv = dense(
        True, lat_index, turn, added, latent_ids, embed_table, layer_gain, qkv[0], lcos, lsin
    )
    kv = lax.all_to_all(kv, "y", split_axis=0, concat_axis=0, tiled=True)
    heads = attend_latents(False, y_index, q, kv)
    heads = gather_lat(heads)
    state, q, kv = dense(
        False, lat_index, turn, heads, state, out_w[0], layer_gain, qkv[1], lcos, lsin
    )
    kv = lax.all_to_all(kv, "y", split_axis=0, concat_axis=0, tiled=True)
    both = attend_latents(True, y_index, q, kv, state)
    both = lax.all_to_all(both, ("y", "x", "c"), split_axis=0, concat_axis=0, tiled=True)
    return last(both, order_weights(out_w[1]))


def solution(mesh):
    grid = Mesh(np.asarray(mesh.devices).reshape(NZ, NY, NX, NC), ("z", "y", "x", "c"))
    return jax.shard_map(
        body,
        mesh=grid,
        in_specs=(
            P(CTX),
            P(),
            P(),
            P(None, CTX, LAT),
            P(CTX, None),
            P(),
            P(None, None, CTX, LAT),
            P(None, CTX, None),
        ),
        out_specs=P(LAT, None),
        check_vma=False,
    )
```

```python
import functools

import jax
import jax.numpy as jnp
import numpy as np
from jax import lax
from jax.experimental import pallas as pl
from jax.experimental.pallas import tpu as pltpu
from jax.sharding import Mesh
from jax.sharding import PartitionSpec as P

D = 1024
HD = 64
HALF = 32
NZ, NY, NX, NC = 16, 4, 4, 2
NLAT = NX * NC
N = 32768
L = 1024
VOCAB = 256
WIDTH = 128
OWN = 16
LAYERS = 2
PART = 32
BLOCK = 256
KEYS = 2048
STEPS = N // KEYS
LAT = ("x", "c")
CTX = ("z", "y")
BF = jnp.bfloat16
F32 = jnp.float32
MIB = 1 << 20


def inverse_frequencies():
    return 10000.0 ** (-2.0 * jnp.arange(HALF, dtype=F32) / (2 * HALF))


def gather_lat(copies):
    by_x = lax.all_to_all(copies, "x", split_axis=0, concat_axis=0, tiled=True)
    return lax.all_gather(by_x, "c", axis=0)


def pack_kernel(lat_ref, *refs):
    ids_ref, cross_ref, layer_ref, cross_out_ref, layer_out_ref = refs[5:10]
    out_ref, sem = refs[10:]
    copies = [pltpu.make_async_copy(refs[i], refs[i + 5], sem.at[i]) for i in range(5)]
    for copy in copies:
        copy.start()
    for copy in copies:
        copy.wait()
    own = pl.ds(pl.multiple_of(lat_ref[0] * WIDTH, WIDTH), WIDTH)
    out_ref[0:48] = cross_ref[...]
    out_ref[48:64] = cross_out_ref[:, own]
    ids = ids_ref[...].astype(F32)
    out_ref[192:200] = jnp.concatenate([ids, jnp.zeros((4, WIDTH), F32)], axis=0).astype(BF)
    for layer in range(LAYERS):
        start = 64 + layer * 64
        out_ref[start : start + 48] = layer_ref[layer * 48 : (layer + 1) * 48]
        out_ref[start + 48 : start + 64] = layer_out_ref[layer * 16 : (layer + 1) * 16, own]


def pack_shards(lat_index, *operands):
    def kernel(lat_ref, *refs):
        pack_kernel(lat_ref, *refs[:5], *refs[6:11], refs[5], refs[11])

    return pl.pallas_call(
        kernel,
        out_shape=jax.ShapeDtypeStruct((200, WIDTH), BF),
        in_specs=[pl.BlockSpec(memory_space=pltpu.SMEM)] + [pl.BlockSpec(memory_space=pl.ANY)] * 5,
        out_specs=pl.BlockSpec(memory_space=pltpu.VMEM),
        scratch_shapes=[pltpu.VMEM(a.shape, a.dtype) for a in operands]
        + [pltpu.SemaphoreType.DMA((5,))],
        compiler_params=pltpu.CompilerParams(vmem_limit_bytes=58 * MIB),
        name="pack_shards",
    )(lat_index, *operands)


def split_kernel(ref, now_ref):
    ids = [ref[z, 192:200, :].astype(F32)[:4] for z in range(NZ)]
    ids = jnp.concatenate(ids, axis=0).astype(BF)
    for y in range(NY):
        for z in range(NZ):
            now_ref[y, z * 64 : (z + 1) * 64] = ref[z, :64]
        now_ref[y, NZ * 64 :] = ids


def split_round(by_z):
    return pl.pallas_call(
        split_kernel,
        out_shape=jax.ShapeDtypeStruct((NY, NZ * 68, WIDTH), BF),
        compiler_params=pltpu.CompilerParams(vmem_limit_bytes=8 * MIB),
        name="split_round",
    )(by_z)


def project_kernel(heads_ref, w_ref, out_ref):
    heads = jnp.concatenate([heads_ref[i] for i in range(NLAT)], axis=1)
    rows = [w_ref[y, z * 64 + 48 : z * 64 + 64] for z in range(NZ) for y in range(NY)]
    out = dot(heads, jnp.concatenate(rows, axis=0)).astype(BF)
    for z in range(NZ):
        out_ref[z] = out


def project_columns(heads, weights):
    return pl.pallas_call(
        project_kernel,
        out_shape=jax.ShapeDtypeStruct((NZ, OWN, WIDTH), BF),
        compiler_params=pltpu.CompilerParams(vmem_limit_bytes=8 * MIB),
        cost_estimate=pl.CostEstimate(
            flops=2 * OWN * D * WIDTH, bytes_accessed=MIB, transcendentals=0
        ),
        name="project_columns",
    )(heads, weights)


def dot(a, b):
    return jnp.dot(a, b, preferred_element_type=F32)


def dot_nt(a, b):
    return lax.dot_general(a, b, (((1,), (1,)), ((), ())), preferred_element_type=F32)


def split_two(x):
    high = x.astype(BF)
    return high, (x - high.astype(F32)).astype(BF)


def rotate_lanes(x, cosine, sine):
    lane = lax.broadcasted_iota(jnp.int32, x.shape, 1)
    other = jnp.where(lane % HD < HALF, pltpu.roll(x, WIDTH - HALF, 1), pltpu.roll(x, HALF, 1))
    return x * cosine + other * sine


def cross_kernel(
    first_ref, row_ref, turn_ref, w_ref, normed_ref, qcos_ref, qsin_ref, cos_ref, sin_ref,
    out_ref, latent_ref, w_sc, table_sc, q_sc, s_sc, v_sc, ids_sc,
):
    for z in range(NZ):
        for y in range(NY):
            row = (z * NY + y) * 16
            for part in range(3):
                start = z * 64 + part * 16
                w_sc[row : row + 16, part * WIDTH : (part + 1) * WIDTH] = w_ref[
                    y, start : start + 16, :
                ]
    for y in range(NY):
        ids = w_ref[y, NZ * 64 :, :].astype(F32)
        for z in range(NZ):
            ids_sc[z, y * 4 : (y + 1) * 4] = ids[z * 4 : (z + 1) * 4]
    latents = jnp.concatenate([ids_sc[NZ - 1, 8:12], ids_sc[NZ - 1, 12:16]], axis=0)
    latent_ref[...] = latents
    turned = pltpu.roll(latents, turn_ref[0], 1)
    here = lax.broadcasted_iota(jnp.int32, turned.shape, 0) == row_ref[0]
    own = jnp.sum(jnp.where(here, turned, 0.0), axis=0, keepdims=True)
    token = lax.broadcasted_iota(jnp.int32, (VOCAB, 128), 0).astype(F32)
    pick = jnp.where(token == own, 1.0, 0.0).T[:OWN].astype(BF)
    normed = normed_ref[...]
    table_sc[...] = dot(normed, w_sc[:, WIDTH:]).T.astype(BF)
    rows = dot(pick, normed).astype(BF)
    query = dot(rows, w_sc[:, :WIDTH]) * (HD**-0.5)
    lane = lax.broadcasted_iota(jnp.int32, query.shape, 1)
    for step in range(STEPS):
        block = slice(step * OWN, (step + 1) * OWN)
        turned = rotate_lanes(query, qcos_ref[block], qsin_ref[block])
        q_sc[step, :OWN] = jnp.where(lane < HD, turned, 0.0).astype(BF)
        q_sc[step, OWN:] = jnp.where(lane < HD, 0.0, turned).astype(BF)
    token = token.astype(BF)
    qpos = lax.broadcasted_iota(jnp.int32, (2 * OWN, 1), 0) % OWN + (N - L) + first_ref[0]

    def scores_of(step, top):
        hot = []
        ids = ids_sc[step]
        for r in range(16):
            row = jnp.broadcast_to(ids[r : r + 1, :], (VOCAB, 128)).astype(BF)
            hot.append(jnp.where(token == row, jnp.ones((), BF), jnp.zeros((), BF)))
        both = dot(table_sc[...], jnp.concatenate(hot, axis=1))
        v_sc[step] = both[WIDTH:].astype(BF)
        cosine, sine = cos_ref[...], sin_ref[...]
        pieces = []
        for head in range(2):
            first = both[head * HD : head * HD + HALF]
            second = both[head * HD + HALF : (head + 1) * HD]
            pieces.append(first * cosine - second * sine)
            pieces.append(second * cosine + first * sine)
        scores = dot(q_sc[step], jnp.concatenate(pieces, axis=0).astype(BF))
        kpos = step * KEYS + lax.broadcasted_iota(jnp.int32, scores.shape, 1)
        scores = jnp.where(kpos <= qpos, scores, -1e30)
        s_sc[step] = scores
        for i in range(KEYS // 128):
            top = jnp.maximum(top, scores[:, i * 128 : (i + 1) * 128])
        return top

    top = lax.fori_loop(0, STEPS, scores_of, jnp.full((2 * OWN, 128), -1e30, F32), unroll=8)
    most = jnp.max(top, axis=1, keepdims=True)

    def values_of(step, carry):
        total, acc = carry
        weight = jnp.exp(s_sc[step] - most)
        for i in range(KEYS // 128):
            total = total + weight[:, i * 128 : (i + 1) * 128]
        return total, acc + dot_nt(v_sc[step], weight.astype(BF))

    total, acc = lax.fori_loop(
        0, STEPS, values_of, (jnp.zeros((2 * OWN, 128), F32), jnp.zeros((WIDTH, 2 * OWN), F32)),
        unroll=8,
    )
    value = acc.T / jnp.sum(total, axis=1, keepdims=True)
    lane = lax.broadcasted_iota(jnp.int32, (OWN, WIDTH), 1)
    value = jnp.where(lane < HD, value[:OWN], value[OWN:]).astype(BF)
    for i in range(NLAT):
        out_ref[i] = value


def cross_attention(*operands):
    return pl.pallas_call(
        cross_kernel,
        out_shape=(
            jax.ShapeDtypeStruct((NLAT, OWN, WIDTH), BF),
            jax.ShapeDtypeStruct((8, 128), F32),
        ),
        in_specs=[pl.BlockSpec(memory_space=pltpu.SMEM)] * 3
        + [pl.BlockSpec(memory_space=pltpu.VMEM)] * (len(operands) - 3),
        scratch_shapes=[
            pltpu.VMEM((D, 3 * WIDTH), BF),
            pltpu.VMEM((2 * WIDTH, VOCAB), BF),
            pltpu.VMEM((STEPS, 2 * OWN, WIDTH), BF),
            pltpu.VMEM((STEPS, 2 * OWN, KEYS), F32),
            pltpu.VMEM((STEPS, WIDTH, KEYS), BF),
            pltpu.VMEM((NZ, 16, 128), F32),
        ],
        compiler_params=pltpu.CompilerParams(vmem_limit_bytes=20 * MIB),
        cost_estimate=pl.CostEstimate(
            flops=MIB, bytes_accessed=MIB, transcendentals=0
        ),
        name="cross_attention",
    )(*operands)


def dense_kernel(first, *refs):
    lat_ref, turn_ref, parts_ref, state_ref, matrix_ref, gain_ref, qkv_ref, cos_ref, sin_ref = refs[:9]
    state_out, q_out, kv_out = refs[9:12]
    if not first:
        state_sc, w_sc, sem = refs[12:]
        copies = [
            pltpu.make_async_copy(matrix_ref.at[i], w_sc.at[i], sem.at[i]) for i in range(NLAT)
        ]
        for copy in copies:
            copy.start()
    parts = jnp.concatenate([parts_ref[i % NC, i // NC] for i in range(NLAT)], axis=1)
    if first:
        ids = pltpu.roll(state_ref[...], turn_ref[0], 1)
        ids = jnp.concatenate([ids[i : i + 1, :PART] for i in range(NLAT)], axis=1)
        token = lax.broadcasted_iota(jnp.int32, (VOCAB, BLOCK), 0).astype(F32)
        hot = jnp.where(token == ids, 1.0, 0.0).T.astype(BF)
        state = dot(hot, matrix_ref[...]) + parts.astype(F32)
        state_out[...] = state
    else:
        columns = []
        for i in range(0, NLAT, 2):
            copies[i].wait()
            copies[i + 1].wait()
            pair = [
                jnp.concatenate([w_sc[j, y, z] for z in range(NZ) for y in range(NY)], axis=0)
                for j in (i, i + 1)
            ]
            columns.append(dot(parts, jnp.concatenate(pair, axis=1)))
        state = state_ref[...] + jnp.concatenate(columns, axis=1)
        state_sc[...] = state
        own = pl.ds(pl.multiple_of(lat_ref[0] * WIDTH, WIDTH), WIDTH)
        state_out[...] = state_sc[:, own].astype(BF)
    scale = lax.rsqrt(jnp.mean(state * state, axis=1, keepdims=True) + 1e-06)
    normed = (state * scale * gain_ref[0 if first else 1, :][None]).astype(BF)
    cosine, sine = cos_ref[...], sin_ref[...]
    weights = [
        jnp.concatenate(
            [qkv_ref[y, z, i * 16 : (i + 1) * 16] for z in range(NZ) for y in range(NY)], axis=0
        )
        for i in range(3)
    ]
    product = dot(normed, jnp.concatenate(weights, axis=1))
    q_out[...] = rotate_lanes(product[:, :WIDTH], cosine, sine).astype(BF)
    k = rotate_lanes(product[:, WIDTH : 2 * WIDTH], cosine, sine).astype(BF)
    v = product[:, 2 * WIDTH :].astype(BF)
    for y in range(NY):
        kv_out[y, :, :WIDTH] = k
        kv_out[y, :, WIDTH:] = v


def dense(first, *operands):
    smem, vmem = (pl.BlockSpec(memory_space=m) for m in (pltpu.SMEM, pltpu.VMEM))
    return pl.pallas_call(
        functools.partial(dense_kernel, first),
        out_shape=(
            jax.ShapeDtypeStruct((BLOCK, D), F32)
            if first
            else jax.ShapeDtypeStruct((BLOCK, WIDTH), BF),
            jax.ShapeDtypeStruct((BLOCK, WIDTH), BF),
            jax.ShapeDtypeStruct((NY, BLOCK, 2 * WIDTH), BF),
        ),
        in_specs=[smem] * 2
        + [vmem] * 2
        + [vmem if first else pl.BlockSpec(memory_space=pl.ANY)]
        + [vmem] * 4,
        scratch_shapes=[]
        if first
        else [
            pltpu.VMEM((BLOCK, D), F32),
            pltpu.VMEM((NLAT, NY, NZ, 16, WIDTH), BF),
            pltpu.SemaphoreType.DMA((NLAT,)),
        ],
        compiler_params=pltpu.CompilerParams(vmem_limit_bytes=(16 if first else 50) * MIB),
        cost_estimate=pl.CostEstimate(
            flops=2 * BLOCK * D * (D + 3 * WIDTH), bytes_accessed=8 * MIB, transcendentals=BLOCK
        ),
        name="dense",
    )(*operands)


def key_positions():
    column = lax.broadcasted_iota(jnp.int32, (1, L), 1)
    return (column % BLOCK) // PART * 128 + column // BLOCK * PART + column % PART


def attend(q, k, v, qpos, kpos):
    outs = []
    seen = kpos <= qpos
    for head in range(2):
        lanes = slice(head * HD, (head + 1) * HD)
        scores = dot_nt(q[:, lanes], k[:, lanes]) * (HD**-0.5)
        scores = jnp.where(seen, scores, -1e30)
        weight = jnp.exp(scores - jnp.max(scores, axis=1, keepdims=True))
        total = jnp.sum(weight, axis=1, keepdims=True)
        outs.append(dot(weight.astype(BF), v[:, lanes]) / total)
    return jnp.concatenate(outs, axis=1).astype(BF)


def attend_kernel(final, y_ref, q_ref, kv_ref, *refs):
    out_ref = refs[-1]
    row = lax.broadcasted_iota(jnp.int32, (BLOCK, 1), 0)
    qpos = row // PART * 128 + y_ref[0] * PART + row % PART
    kv = jnp.concatenate([kv_ref[i] for i in range(NY)], axis=0)
    out = attend(q_ref[...], kv[:, :WIDTH], kv[:, WIDTH:], qpos, key_positions())
    if final:
        state = refs[0][...]
        for y in range(NY):
            for i in range(NLAT):
                out_ref[y * NLAT + i, :PART] = out[i * PART : (i + 1) * PART]
                out_ref[y * NLAT + i, PART:] = state[i * PART : (i + 1) * PART]
    else:
        for i in range(NX):
            out_ref[i] = out


def attend_latents(final, *operands):
    shape = (NY * NLAT, 2 * PART, WIDTH) if final else (NX, BLOCK, WIDTH)
    smem, vmem = (pl.BlockSpec(memory_space=m) for m in (pltpu.SMEM, pltpu.VMEM))
    return pl.pallas_call(
        functools.partial(attend_kernel, final),
        out_shape=jax.ShapeDtypeStruct(shape, BF),
        in_specs=[smem] + [vmem] * (len(operands) - 1),
        compiler_params=pltpu.CompilerParams(vmem_limit_bytes=12 * MIB),
        cost_estimate=pl.CostEstimate(
            flops=8 * BLOCK * L * HD, bytes_accessed=2 * MIB, transcendentals=2 * BLOCK * L
        ),
        name="attend_latents",
    )(*operands)


def order_kernel(ref, out_ref):
    for i in range(NLAT):
        out_ref[:, i * WIDTH : (i + 1) * WIDTH] = jnp.concatenate(
            [ref[i, y, z] for z in range(NZ) for y in range(NY)], axis=0
        )


def order_weights(out_w):
    return pl.pallas_call(
        order_kernel,
        out_shape=jax.ShapeDtypeStruct((D, D), BF),
        compiler_params=pltpu.CompilerParams(vmem_limit_bytes=8 * MIB),
        name="order_weights",
    )(out_w)


def last_kernel(both_ref, out_w_ref, out_ref):
    heads, state = (
        jnp.concatenate(
            [
                jnp.concatenate(
                    [both_ref[y * NLAT + i, half * PART : (half + 1) * PART] for i in range(NLAT)],
                    axis=1,
                )
                for y in range(NY)
            ],
            axis=0,
        )
        for half in range(2)
    )
    out_ref[...] = state.astype(F32) + dot(heads, out_w_ref[...])


def last(both, out_w):
    return pl.pallas_call(
        last_kernel,
        out_shape=jax.ShapeDtypeStruct((128, D), F32),
        compiler_params=pltpu.CompilerParams(vmem_limit_bytes=16 * MIB),
        cost_estimate=pl.CostEstimate(
            flops=2 * 128 * D * D, bytes_accessed=4 * MIB, transcendentals=0
        ),
        name="last",
    )(both, out_w)


def head_angles(positions, inverse):
    angle = positions.astype(F32)[:, None] * inverse[None, :]
    cosine, sine = jnp.cos(angle), jnp.sin(angle)
    return (
        jnp.concatenate([cosine] * 4, axis=1),
        jnp.concatenate([-sine, sine, -sine, sine], axis=1),
    )


def body(token_ids, embed_table, input_gain, cross_qkv, cross_out, layer_gain, layer_qkv, layer_out):
    z, y = lax.axis_index("z"), lax.axis_index("y")
    lat = lax.axis_index(LAT)

    lat_index = jnp.full((1,), lat, jnp.int32)
    turn = (128 - y * PART) % 128
    pack = pack_shards(
        lat_index, token_ids.reshape(4, 128), cross_qkv.reshape(48, WIDTH),
        layer_qkv.reshape(96, WIDTH), cross_out, layer_out.reshape(32, D),
    )
    by_z = lax.all_gather(pack, "z", axis=0)
    by_z, inverse, embed_table, input_gain = lax.optimization_barrier(
        (by_z, inverse_frequencies(), embed_table, input_gain)
    )
    now = split_round(by_z)
    by_zy = lax.all_to_all(now, "y", split_axis=0, concat_axis=0, tiled=True)

    latent = jnp.arange(OWN, dtype=jnp.int32) + (z // 2) * 128 + y * PART + (z % 2) * OWN
    offset = N - L + latent[None, :] - KEYS * jnp.arange(STEPS, dtype=jnp.int32)[:, None]
    qcos, qsin = head_angles(offset.reshape(STEPS * OWN), inverse)
    row = jnp.arange(BLOCK, dtype=jnp.int32)
    lpos = row // PART * 128 + y * PART + row % PART
    lcos, lsin = head_angles(lpos, inverse)
    fine = inverse[:, None] * jnp.arange(KEYS, dtype=F32)[None, :]
    tables = (qcos, qsin, jnp.cos(fine), jnp.sin(fine))
    wide = embed_table.astype(F32)
    normed = wide * lax.rsqrt(jnp.mean(wide * wide, axis=-1, keepdims=True) + 1e-06) * input_gain
    normed = normed.astype(BF)
    by_zy, rest_z, normed, tables, lcos, lsin, turn, y = lax.optimization_barrier(
        (by_zy, by_z[:, 64:192], normed, tables, lcos, lsin, turn, y)
    )
    turn = jnp.full((1,), turn, jnp.int32)
    y_index = jnp.full((1,), y, jnp.int32)
    rest_zy = lax.all_gather(rest_z, "y", axis=0)
    outs = [rest_zy[:, :, 64 * i + 48 : 64 * i + 64] for i in range(LAYERS)]
    qkv = [rest_zy[:, :, 64 * i : 64 * i + 48] for i in range(LAYERS)]
    first = (z // 2) * 128 + y * PART + (z % 2) * OWN
    place = [jnp.full((1,), i, jnp.int32) for i in (first, z // 2, (128 - first % 128) % 128)]
    heads, latent_ids = cross_attention(*place, by_zy, normed, *tables)

    heads = lax.all_to_all(heads, LAT, split_axis=0, concat_axis=0, tiled=True)
    added = project_columns(heads, by_zy)

    added = lax.all_to_all(added, "z", split_axis=0, concat_axis=0, tiled=True)
    added, outs, qkv = lax.optimization_barrier((added, outs, qkv))
    out_w = [lax.all_gather(w, LAT, axis=0) for w in outs]
    added = added.reshape(BLOCK, WIDTH)
    added = gather_lat(jnp.broadcast_to(added[None], (NX, BLOCK, WIDTH)))

    state, q, kv = dense(
        True, lat_index, turn, added, latent_ids, embed_table, layer_gain, qkv[0], lcos, lsin
    )
    kv = lax.all_to_all(kv, "y", split_axis=0, concat_axis=0, tiled=True)
    heads = attend_latents(False, y_index, q, kv)
    heads = gather_lat(heads)
    state, q, kv = dense(
        False, lat_index, turn, heads, state, out_w[0], layer_gain, qkv[1], lcos, lsin
    )
    kv = lax.all_to_all(kv, "y", split_axis=0, concat_axis=0, tiled=True)
    both = attend_latents(True, y_index, q, kv, state)
    both = lax.all_to_all(both, ("y", "x", "c"), split_axis=0, concat_axis=0, tiled=True)
    return last(both, order_weights(out_w[1]))


def solution(mesh):
    grid = Mesh(np.asarray(mesh.devices).reshape(NZ, NY, NX, NC), ("z", "y", "x", "c"))
    return jax.shard_map(
        body,
        mesh=grid,
        in_specs=(
            P(CTX),
            P(),
            P(),
            P(None, CTX, LAT),
            P(CTX, None),
            P(),
            P(None, None, CTX, LAT),
            P(None, CTX, None),
        ),
        out_specs=P(LAT, None),
        check_vma=False,
    )
```

```python
import functools

import jax
import jax.numpy as jnp
import numpy as np
from jax import lax
from jax.experimental import pallas as pl
from jax.experimental.pallas import tpu as pltpu
from jax.sharding import Mesh
from jax.sharding import PartitionSpec as P

D = 1024
HD = 64
HALF = 32
NZ, NY, NX, NC = 16, 4, 4, 2
NLAT = NX * NC
N = 32768
L = 1024
VOCAB = 256
WIDTH = 128
OWN = 16
LAYERS = 2
PART = 32
BLOCK = 256
KEYS = 2048
STEPS = N // KEYS
LAT = ("x", "c")
CTX = ("z", "y")
BF = jnp.bfloat16
F32 = jnp.float32
MIB = 1 << 20


def inverse_frequencies():
    return 10000.0 ** (-2.0 * jnp.arange(HALF, dtype=F32) / (2 * HALF))


def gather_lat(copies):
    by_x = lax.all_to_all(copies, "x", split_axis=0, concat_axis=0, tiled=True)
    return lax.all_gather(by_x, "c", axis=0)


def pack_kernel(lat_ref, *refs):
    ids_ref, cross_ref, layer_ref, cross_out_ref, layer_out_ref = refs[5:10]
    out_ref, sem = refs[10:]
    copies = [pltpu.make_async_copy(refs[i], refs[i + 5], sem.at[i]) for i in range(5)]
    for copy in copies:
        copy.start()
    for copy in copies:
        copy.wait()
    own = pl.ds(pl.multiple_of(lat_ref[0] * WIDTH, WIDTH), WIDTH)
    out_ref[0:48] = cross_ref[...]
    out_ref[48:64] = cross_out_ref[:, own]
    ids = ids_ref[...].astype(F32)
    out_ref[192:200] = jnp.concatenate([ids, jnp.zeros((4, WIDTH), F32)], axis=0).astype(BF)
    for layer in range(LAYERS):
        start = 64 + layer * 64
        out_ref[start : start + 48] = layer_ref[layer * 48 : (layer + 1) * 48]
        out_ref[start + 48 : start + 64] = layer_out_ref[layer * 16 : (layer + 1) * 16, own]


def pack_shards(lat_index, *operands):
    def kernel(lat_ref, *refs):
        pack_kernel(lat_ref, *refs[:5], *refs[6:11], refs[5], refs[11])

    return pl.pallas_call(
        kernel,
        out_shape=jax.ShapeDtypeStruct((200, WIDTH), BF),
        in_specs=[pl.BlockSpec(memory_space=pltpu.SMEM)] + [pl.BlockSpec(memory_space=pl.ANY)] * 5,
        out_specs=pl.BlockSpec(memory_space=pltpu.VMEM),
        scratch_shapes=[pltpu.VMEM(a.shape, a.dtype) for a in operands]
        + [pltpu.SemaphoreType.DMA((5,))],
        compiler_params=pltpu.CompilerParams(vmem_limit_bytes=58 * MIB),
        name="pack_shards",
    )(lat_index, *operands)


def split_kernel(ref, now_ref):
    ids = [ref[z, 192:200, :].astype(F32)[:4] for z in range(NZ)]
    ids = jnp.concatenate(ids, axis=0).astype(BF)
    for y in range(NY):
        for z in range(NZ):
            now_ref[y, z * 64 : (z + 1) * 64] = ref[z, :64]
        now_ref[y, NZ * 64 :] = ids


def split_round(by_z):
    return pl.pallas_call(
        split_kernel,
        out_shape=jax.ShapeDtypeStruct((NY, NZ * 68, WIDTH), BF),
        compiler_params=pltpu.CompilerParams(vmem_limit_bytes=8 * MIB),
        name="split_round",
    )(by_z)


def project_kernel(heads_ref, w_ref, out_ref):
    heads = jnp.concatenate([heads_ref[i] for i in range(NLAT)], axis=1)
    rows = [w_ref[y, z * 64 + 48 : z * 64 + 64] for z in range(NZ) for y in range(NY)]
    out = dot(heads, jnp.concatenate(rows, axis=0)).astype(BF)
    for z in range(NZ):
        out_ref[z] = out


def project_columns(heads, weights):
    return pl.pallas_call(
        project_kernel,
        out_shape=jax.ShapeDtypeStruct((NZ, OWN, WIDTH), BF),
        compiler_params=pltpu.CompilerParams(vmem_limit_bytes=8 * MIB),
        cost_estimate=pl.CostEstimate(
            flops=2 * OWN * D * WIDTH, bytes_accessed=MIB, transcendentals=0
        ),
        name="project_columns",
    )(heads, weights)


def dot(a, b):
    return jnp.dot(a, b, preferred_element_type=F32)


def dot_nt(a, b):
    return lax.dot_general(a, b, (((1,), (1,)), ((), ())), preferred_element_type=F32)


def split_two(x):
    high = x.astype(BF)
    return high, (x - high.astype(F32)).astype(BF)


def rotate_lanes(x, cosine, sine):
    lane = lax.broadcasted_iota(jnp.int32, x.shape, 1)
    other = jnp.where(lane % HD < HALF, pltpu.roll(x, WIDTH - HALF, 1), pltpu.roll(x, HALF, 1))
    return x * cosine + other * sine


def cross_kernel(
    first_ref, row_ref, turn_ref, w_ref, normed_ref, qcos_ref, qsin_ref, cos_ref, sin_ref,
    out_ref, latent_ref, w_sc, table_sc, q_sc, s_sc, v_sc, ids_sc,
):
    for z in range(NZ):
        for y in range(NY):
            row = (z * NY + y) * 16
            for part in range(3):
                start = z * 64 + part * 16
                w_sc[row : row + 16, part * WIDTH : (part + 1) * WIDTH] = w_ref[
                    y, start : start + 16, :
                ]
    for y in range(NY):
        ids = w_ref[y, NZ * 64 :, :].astype(F32)
        for z in range(NZ):
            ids_sc[z, y * 4 : (y + 1) * 4] = ids[z * 4 : (z + 1) * 4]
    latents = jnp.concatenate([ids_sc[NZ - 1, 8:12], ids_sc[NZ - 1, 12:16]], axis=0)
    latent_ref[...] = latents
    turned = pltpu.roll(latents, turn_ref[0], 1)
    here = lax.broadcasted_iota(jnp.int32, turned.shape, 0) == row_ref[0]
    own = jnp.sum(jnp.where(here, turned, 0.0), axis=0, keepdims=True)
    token = lax.broadcasted_iota(jnp.int32, (VOCAB, 128), 0).astype(F32)
    pick = jnp.where(token == own, 1.0, 0.0).T[:OWN].astype(BF)
    normed = normed_ref[...]
    table_sc[...] = dot(normed, w_sc[:, WIDTH:]).T.astype(BF)
    rows = dot(pick, normed).astype(BF)
    query = dot(rows, w_sc[:, :WIDTH]) * (HD**-0.5)
    lane = lax.broadcasted_iota(jnp.int32, query.shape, 1)
    for step in range(STEPS):
        block = slice(step * OWN, (step + 1) * OWN)
        turned = rotate_lanes(query, qcos_ref[block], qsin_ref[block])
        q_sc[step, :OWN] = jnp.where(lane < HD, turned, 0.0).astype(BF)
        q_sc[step, OWN:] = jnp.where(lane < HD, 0.0, turned).astype(BF)
    token = token.astype(BF)
    qpos = lax.broadcasted_iota(jnp.int32, (2 * OWN, 1), 0) % OWN + (N - L) + first_ref[0]

    def scores_of(step, top):
        hot = []
        ids = ids_sc[step]
        for r in range(16):
            row = jnp.broadcast_to(ids[r : r + 1, :], (VOCAB, 128)).astype(BF)
            hot.append(jnp.where(token == row, jnp.ones((), BF), jnp.zeros((), BF)))
        both = dot(table_sc[...], jnp.concatenate(hot, axis=1))
        v_sc[step] = both[WIDTH:].astype(BF)
        cosine, sine = cos_ref[...], sin_ref[...]
        pieces = []
        for head in range(2):
            first = both[head * HD : head * HD + HALF]
            second = both[head * HD + HALF : (head + 1) * HD]
            pieces.append(first * cosine - second * sine)
            pieces.append(second * cosine + first * sine)
        scores = dot(q_sc[step], jnp.concatenate(pieces, axis=0).astype(BF))
        kpos = step * KEYS + lax.broadcasted_iota(jnp.int32, scores.shape, 1)
        scores = jnp.where(kpos <= qpos, scores, -1e30)
        s_sc[step] = scores
        for i in range(KEYS // 128):
            top = jnp.maximum(top, scores[:, i * 128 : (i + 1) * 128])
        return top

    top = lax.fori_loop(0, STEPS, scores_of, jnp.full((2 * OWN, 128), -1e30, F32), unroll=8)
    most = jnp.max(top, axis=1, keepdims=True)

    def values_of(step, carry):
        total, acc = carry
        weight = jnp.exp(s_sc[step] - most)
        for i in range(KEYS // 128):
            total = total + weight[:, i * 128 : (i + 1) * 128]
        return total, acc + dot_nt(v_sc[step], weight.astype(BF))

    total, acc = lax.fori_loop(
        0, STEPS, values_of, (jnp.zeros((2 * OWN, 128), F32), jnp.zeros((WIDTH, 2 * OWN), F32)),
        unroll=8,
    )
    value = acc.T / jnp.sum(total, axis=1, keepdims=True)
    lane = lax.broadcasted_iota(jnp.int32, (OWN, WIDTH), 1)
    value = jnp.where(lane < HD, value[:OWN], value[OWN:]).astype(BF)
    for i in range(NLAT):
        out_ref[i] = value


def cross_attention(*operands):
    return pl.pallas_call(
        cross_kernel,
        out_shape=(
            jax.ShapeDtypeStruct((NLAT, OWN, WIDTH), BF),
            jax.ShapeDtypeStruct((8, 128), F32),
        ),
        in_specs=[pl.BlockSpec(memory_space=pltpu.SMEM)] * 3
        + [pl.BlockSpec(memory_space=pltpu.VMEM)] * (len(operands) - 3),
        scratch_shapes=[
            pltpu.VMEM((D, 3 * WIDTH), BF),
            pltpu.VMEM((2 * WIDTH, VOCAB), BF),
            pltpu.VMEM((STEPS, 2 * OWN, WIDTH), BF),
            pltpu.VMEM((STEPS, 2 * OWN, KEYS), F32),
            pltpu.VMEM((STEPS, WIDTH, KEYS), BF),
            pltpu.VMEM((NZ, 16, 128), F32),
        ],
        compiler_params=pltpu.CompilerParams(vmem_limit_bytes=20 * MIB),
        cost_estimate=pl.CostEstimate(
            flops=MIB, bytes_accessed=MIB, transcendentals=0
        ),
        name="cross_attention",
    )(*operands)


def out_weights(ref):
    columns = []
    for i in range(NLAT):
        rows = [ref[i, y, z] for z in range(NZ) for y in range(NY)]
        columns.append(jnp.concatenate(rows, axis=0))
    return jnp.concatenate(columns, axis=1)


def dense_kernel(first, *refs):
    lat_ref, turn_ref, parts_ref, state_ref, matrix_ref, gain_ref, qkv_ref, cos_ref, sin_ref = refs[:9]
    state_out, q_out, kv_out = refs[9:12]
    parts = jnp.concatenate([parts_ref[i % NC, i // NC] for i in range(NLAT)], axis=1)
    if first:
        ids = pltpu.roll(state_ref[...], turn_ref[0], 1)
        ids = jnp.concatenate([ids[i : i + 1, :PART] for i in range(NLAT)], axis=1)
        token = lax.broadcasted_iota(jnp.int32, (VOCAB, BLOCK), 0).astype(F32)
        hot = jnp.where(token == ids, 1.0, 0.0).T.astype(BF)
        state = dot(hot, matrix_ref[...]) + parts.astype(F32)
        state_out[...] = state
    else:
        state = state_ref[...] + dot(parts, out_weights(matrix_ref))
        state_sc = refs[12]
        state_sc[...] = state
        own = pl.ds(pl.multiple_of(lat_ref[0] * WIDTH, WIDTH), WIDTH)
        state_out[...] = state_sc[:, own].astype(BF)
    scale = lax.rsqrt(jnp.mean(state * state, axis=1, keepdims=True) + 1e-06)
    normed = (state * scale * gain_ref[0 if first else 1, :][None]).astype(BF)
    cosine, sine = cos_ref[...], sin_ref[...]
    weights = [
        jnp.concatenate(
            [qkv_ref[y, z, i * 16 : (i + 1) * 16] for z in range(NZ) for y in range(NY)], axis=0
        )
        for i in range(3)
    ]
    product = dot(normed, jnp.concatenate(weights, axis=1))
    q_out[...] = rotate_lanes(product[:, :WIDTH], cosine, sine).astype(BF)
    k = rotate_lanes(product[:, WIDTH : 2 * WIDTH], cosine, sine).astype(BF)
    v = product[:, 2 * WIDTH :].astype(BF)
    for y in range(NY):
        kv_out[y, :, :WIDTH] = k
        kv_out[y, :, WIDTH:] = v


def dense(first, *operands):
    smem, vmem = (pl.BlockSpec(memory_space=m) for m in (pltpu.SMEM, pltpu.VMEM))
    return pl.pallas_call(
        functools.partial(dense_kernel, first),
        out_shape=(
            jax.ShapeDtypeStruct((BLOCK, D), F32)
            if first
            else jax.ShapeDtypeStruct((BLOCK, WIDTH), BF),
            jax.ShapeDtypeStruct((BLOCK, WIDTH), BF),
            jax.ShapeDtypeStruct((NY, BLOCK, 2 * WIDTH), BF),
        ),
        in_specs=[smem] * 2 + [vmem] * 7,
        scratch_shapes=[] if first else [pltpu.VMEM((BLOCK, D), F32)],
        compiler_params=pltpu.CompilerParams(vmem_limit_bytes=16 * MIB),
        cost_estimate=pl.CostEstimate(
            flops=2 * BLOCK * D * (D + 3 * WIDTH), bytes_accessed=8 * MIB, transcendentals=BLOCK
        ),
        name="dense",
    )(*operands)


def key_positions():
    column = lax.broadcasted_iota(jnp.int32, (1, L), 1)
    return (column % BLOCK) // PART * 128 + column // BLOCK * PART + column % PART


def attend(q, k, v, qpos, kpos):
    outs = []
    seen = kpos <= qpos
    for head in range(2):
        lanes = slice(head * HD, (head + 1) * HD)
        scores = dot_nt(q[:, lanes], k[:, lanes]) * (HD**-0.5)
        scores = jnp.where(seen, scores, -1e30)
        weight = jnp.exp(scores - jnp.max(scores, axis=1, keepdims=True))
        total = jnp.sum(weight, axis=1, keepdims=True)
        outs.append(dot(weight.astype(BF), v[:, lanes]) / total)
    return jnp.concatenate(outs, axis=1).astype(BF)


def attend_kernel(final, y_ref, q_ref, kv_ref, *refs):
    out_ref = refs[-1]
    row = lax.broadcasted_iota(jnp.int32, (BLOCK, 1), 0)
    qpos = row // PART * 128 + y_ref[0] * PART + row % PART
    kv = jnp.concatenate([kv_ref[i] for i in range(NY)], axis=0)
    out = attend(q_ref[...], kv[:, :WIDTH], kv[:, WIDTH:], qpos, key_positions())
    if final:
        state = refs[0][...]
        for y in range(NY):
            for i in range(NLAT):
                out_ref[y * NLAT + i, :PART] = out[i * PART : (i + 1) * PART]
                out_ref[y * NLAT + i, PART:] = state[i * PART : (i + 1) * PART]
    else:
        for i in range(NX):
            out_ref[i] = out


def attend_latents(final, *operands):
    shape = (NY * NLAT, 2 * PART, WIDTH) if final else (NX, BLOCK, WIDTH)
    smem, vmem = (pl.BlockSpec(memory_space=m) for m in (pltpu.SMEM, pltpu.VMEM))
    return pl.pallas_call(
        functools.partial(attend_kernel, final),
        out_shape=jax.ShapeDtypeStruct(shape, BF),
        in_specs=[smem] + [vmem] * (len(operands) - 1),
        compiler_params=pltpu.CompilerParams(vmem_limit_bytes=12 * MIB),
        cost_estimate=pl.CostEstimate(
            flops=8 * BLOCK * L * HD, bytes_accessed=2 * MIB, transcendentals=2 * BLOCK * L
        ),
        name="attend_latents",
    )(*operands)


def order_kernel(ref, out_ref):
    for i in range(NLAT):
        out_ref[:, i * WIDTH : (i + 1) * WIDTH] = jnp.concatenate(
            [ref[i, y, z] for z in range(NZ) for y in range(NY)], axis=0
        )


def order_weights(out_w):
    return pl.pallas_call(
        order_kernel,
        out_shape=jax.ShapeDtypeStruct((D, D), BF),
        compiler_params=pltpu.CompilerParams(vmem_limit_bytes=8 * MIB),
        name="order_weights",
    )(out_w)


def last_kernel(both_ref, out_w_ref, out_ref):
    heads, state = (
        jnp.concatenate(
            [
                jnp.concatenate(
                    [both_ref[y * NLAT + i, half * PART : (half + 1) * PART] for i in range(NLAT)],
                    axis=1,
                )
                for y in range(NY)
            ],
            axis=0,
        )
        for half in range(2)
    )
    out_ref[...] = state.astype(F32) + dot(heads, out_w_ref[...])


def last(both, out_w):
    return pl.pallas_call(
        last_kernel,
        out_shape=jax.ShapeDtypeStruct((128, D), F32),
        compiler_params=pltpu.CompilerParams(vmem_limit_bytes=16 * MIB),
        cost_estimate=pl.CostEstimate(
            flops=2 * 128 * D * D, bytes_accessed=4 * MIB, transcendentals=0
        ),
        name="last",
    )(both, out_w)


def head_angles(positions, inverse):
    angle = positions.astype(F32)[:, None] * inverse[None, :]
    cosine, sine = jnp.cos(angle), jnp.sin(angle)
    return (
        jnp.concatenate([cosine] * 4, axis=1),
        jnp.concatenate([-sine, sine, -sine, sine], axis=1),
    )


def body(token_ids, embed_table, input_gain, cross_qkv, cross_out, layer_gain, layer_qkv, layer_out):
    z, y = lax.axis_index("z"), lax.axis_index("y")
    lat = lax.axis_index(LAT)

    lat_index = jnp.full((1,), lat, jnp.int32)
    turn = (128 - y * PART) % 128
    pack = pack_shards(
        lat_index, token_ids.reshape(4, 128), cross_qkv.reshape(48, WIDTH),
        layer_qkv.reshape(96, WIDTH), cross_out, layer_out.reshape(32, D),
    )
    by_z = lax.all_gather(pack, "z", axis=0)
    by_z, inverse, embed_table, input_gain = lax.optimization_barrier(
        (by_z, inverse_frequencies(), embed_table, input_gain)
    )
    now = split_round(by_z)
    by_zy = lax.all_to_all(now, "y", split_axis=0, concat_axis=0, tiled=True)

    latent = jnp.arange(OWN, dtype=jnp.int32) + (z // 2) * 128 + y * PART + (z % 2) * OWN
    offset = N - L + latent[None, :] - KEYS * jnp.arange(STEPS, dtype=jnp.int32)[:, None]
    qcos, qsin = head_angles(offset.reshape(STEPS * OWN), inverse)
    row = jnp.arange(BLOCK, dtype=jnp.int32)
    lpos = row // PART * 128 + y * PART + row % PART
    lcos, lsin = head_angles(lpos, inverse)
    fine = inverse[:, None] * jnp.arange(KEYS, dtype=F32)[None, :]
    tables = (qcos, qsin, jnp.cos(fine), jnp.sin(fine))
    wide = embed_table.astype(F32)
    normed = wide * lax.rsqrt(jnp.mean(wide * wide, axis=-1, keepdims=True) + 1e-06) * input_gain
    normed = normed.astype(BF)
    by_zy, rest_z, normed, tables, lcos, lsin, turn, y = lax.optimization_barrier(
        (by_zy, by_z[:, 64:192], normed, tables, lcos, lsin, turn, y)
    )
    turn = jnp.full((1,), turn, jnp.int32)
    y_index = jnp.full((1,), y, jnp.int32)
    rest_zy = lax.all_gather(rest_z, "y", axis=0)
    outs = [rest_zy[:, :, 64 * i + 48 : 64 * i + 64] for i in range(LAYERS)]
    qkv = [rest_zy[:, :, 64 * i : 64 * i + 48] for i in range(LAYERS)]
    first = (z // 2) * 128 + y * PART + (z % 2) * OWN
    place = [jnp.full((1,), i, jnp.int32) for i in (first, z // 2, (128 - first % 128) % 128)]
    heads, latent_ids = cross_attention(*place, by_zy, normed, *tables)

    heads = lax.all_to_all(heads, LAT, split_axis=0, concat_axis=0, tiled=True)
    added = project_columns(heads, by_zy)

    added = lax.all_to_all(added, "z", split_axis=0, concat_axis=0, tiled=True)
    added, outs, qkv = lax.optimization_barrier((added, outs, qkv))
    out_w = [lax.all_gather(outs[0], LAT, axis=0)]
    added = added.reshape(BLOCK, WIDTH)
    added = jnp.broadcast_to(added[None], (NX, BLOCK, WIDTH))
    added = lax.all_to_all(added, "x", split_axis=0, concat_axis=0, tiled=True)
    added, last_out = lax.optimization_barrier((added, outs[1]))
    out_w.append(lax.all_gather(last_out, LAT, axis=0))
    added = lax.all_gather(added, "c", axis=0)

    state, q, kv = dense(
        True, lat_index, turn, added, latent_ids, embed_table, layer_gain, qkv[0], lcos, lsin
    )
    kv = lax.all_to_all(kv, "y", split_axis=0, concat_axis=0, tiled=True)
    heads = attend_latents(False, y_index, q, kv)
    heads = gather_lat(heads)
    state, q, kv = dense(
        False, lat_index, turn, heads, state, out_w[0], layer_gain, qkv[1], lcos, lsin
    )
    kv = lax.all_to_all(kv, "y", split_axis=0, concat_axis=0, tiled=True)
    both = attend_latents(True, y_index, q, kv, state)
    both = lax.all_to_all(both, ("y", "x", "c"), split_axis=0, concat_axis=0, tiled=True)
    return last(both, order_weights(out_w[1]))


def solution(mesh):
    grid = Mesh(np.asarray(mesh.devices).reshape(NZ, NY, NX, NC), ("z", "y", "x", "c"))
    return jax.shard_map(
        body,
        mesh=grid,
        in_specs=(
            P(CTX),
            P(),
            P(),
            P(None, CTX, LAT),
            P(CTX, None),
            P(),
            P(None, None, CTX, LAT),
            P(None, CTX, None),
        ),
        out_specs=P(LAT, None),
        check_vma=False,
    )
```
